32 devices in a mesh: dp: 8 (over z, x), mp: 4 (over y, core).
Axes of the slice: x: 2, y: 2, z: 4, core: 2. Of those that a mesh axis runs over, the one named last changes fastest.
Arguments:
- block_input: bfloat16 [16384, 768], P(('dp', 'mp')), may hold values from -6 to 6
- cotangent: bfloat16 [16384, 768], P(('dp', 'mp')), may hold values from -5.2 to 5.2
- lengths: int32 [256], P('dp'), may hold values from 3 to 64, as said below
- attn_input: float32 [768, 3, 768], P('dp', None, 'mp')
- attn_input_first: float32 [768, 3, 768], P('dp', None, 'mp'), may hold values from -0.005859375 to 0.005859375
- attn_input_second: float32 [768, 3, 768], P('dp', None, 'mp'), may hold values from 1.4110135e-07 to 5.644054e-07
- attn_output: float32 [768, 768], P('dp', 'mp'), may hold values from -0.875 to 0.875
- attn_output_first: float32 [768, 768], P('dp', 'mp'), may hold values from -0.005859375 to 0.005859375
- attn_output_second: float32 [768, 768], P('dp', 'mp'), may hold values from 1.4110135e-07 to 5.644054e-07
- mlp_up: float32 [768, 3072], P('dp', 'mp')
- mlp_up_first: float32 [768, 3072], P('dp', 'mp'), may hold values from -0.0017089844 to 0.0017089844
- mlp_up_second: float32 [768, 3072], P('dp', 'mp'), may hold values from 1.4110136e-08 to 5.6440545e-08
- mlp_down: float32 [768, 3072], P('dp', 'mp'), may hold values from -0.109375 to 0.109375
- mlp_down_first: float32 [768, 3072], P('dp', 'mp'), may hold values from -0.005859375 to 0.005859375
- mlp_down_second: float32 [768, 3072], P('dp', 'mp'), may hold values from 1.4110135e-07 to 5.644054e-07
- norm_params: float32 [4, 768], replicated, may hold values from -1.2 to 2.1
- norm_first: float32 [4, 768], P(None, ('dp', 'mp')), may hold values from -0.005859375 to 0.005859375
- norm_second: float32 [4, 768], P(None, ('dp', 'mp')), may hold values from 1.4110135e-07 to 5.644054e-07
- bias_params: float32 [8, 768], replicated, may hold values from -4 to 4
- bias_first: float32 [8, 768], P(None, ('dp', 'mp')), may hold values from -0.005859375 to 0.005859375
- bias_second: float32 [8, 768], P(None, ('dp', 'mp')), may hold values from 1.4110135e-07 to 5.644054e-07
Outputs:
- block_output: bfloat16 [16384, 768], P(('dp', 'mp'))
- input_grad: float32 [16384, 768], P(('dp', 'mp'))
- grad_norm: float32 [], replicated
- attn_input_grad: float32 [768, 3, 768], P('dp', None, 'mp')
- attn_input_new: float32 [768, 3, 768], P('dp', None, 'mp')
- attn_input_first_new: float32 [768, 3, 768], P('dp', None, 'mp')
- attn_input_second_new: float32 [768, 3, 768], P('dp', None, 'mp')
- attn_input_copy: bfloat16 [768, 3, 768], P('dp', None, 'mp')
- attn_output_grad: float32 [768, 768], P('dp', 'mp')
- attn_output_new: float32 [768, 768], P('dp', 'mp')
- attn_output_first_new: float32 [768, 768], P('dp', 'mp')
- attn_output_second_new: float32 [768, 768], P('dp', 'mp')
- attn_output_copy: bfloat16 [768, 768], P('dp', 'mp')
- mlp_up_grad: float32 [768, 3072], P('dp', 'mp')
- mlp_up_new: float32 [768, 3072], P('dp', 'mp')
- mlp_up_first_new: float32 [768, 3072], P('dp', 'mp')
- mlp_up_second_new: float32 [768, 3072], P('dp', 'mp')
- mlp_up_copy: bfloat16 [768, 3072], P('dp', 'mp')
- mlp_down_grad: float32 [768, 3072], P('dp', 'mp')
- mlp_down_new: float32 [768, 3072], P('dp', 'mp')
- mlp_down_first_new: float32 [768, 3072], P('dp', 'mp')
- mlp_down_second_new: float32 [768, 3072], P('dp', 'mp')
- mlp_down_copy: bfloat16 [768, 3072], P('dp', 'mp')
- norm_grad: float32 [4, 768], P(None, ('dp', 'mp'))
- norm_new: float32 [4, 768], P(None, ('dp', 'mp'))
- norm_first_new: float32 [4, 768], P(None, ('dp', 'mp'))
- norm_second_new: float32 [4, 768], P(None, ('dp', 'mp'))
- bias_grad: float32 [8, 768], P(None, ('dp', 'mp'))
- bias_new: float32 [8, 768], P(None, ('dp', 'mp'))
- bias_first_new: float32 [8, 768], P(None, ('dp', 'mp'))
- bias_second_new: float32 [8, 768], P(None, ('dp', 'mp'))
The draws below stay inside these ranges and needn't reach their ends.
Inputs may be any that keep to these rules, and one draw needn't show every extreme that they name: `lengths`: mostly short; in every aligned block of 8 * 4 captions one caption has length 64.
All inputs are finite; a program needn't handle non-finite values.
Results may differ from the reference program's by a relative error of at most 0.018.
Values may be sent and summed in bfloat16 or wider, within the bound.
No kernel may reach another device: no remote copies, remote signals or barrier semaphores. Data moves between devices by JAX's collectives and lax.ppermute only.
A program may use at most 128 MiB of HBM per device.

```python
import math
import jax
import jax.numpy as jnp
from jax import lax

D = 768
HEAD = 64
FF = 3072
LENGTH = 64
CAP_DEV = 8
STEP = 10
CAPTIONS = 256
TOKENS = 16384
N_DP = 8
N_MP = 4


def draw_lengths(key, part):
    key = jax.random.fold_in(key, 11)
    keys = jax.random.split(key, 4)
    first = jax.random.randint(keys[0], (CAPTIONS,), 3, LENGTH + 1)
    second = jax.random.randint(keys[1], (CAPTIONS,), 3, LENGTH + 1)
    third = jax.random.randint(keys[2], (CAPTIONS,), 3, LENGTH + 1)
    shortest = jnp.minimum(jnp.minimum(first, second), third)
    block = CAP_DEV * N_MP
    chosen = jax.random.randint(keys[3], (CAPTIONS // block,), 0, block)
    place = jnp.arange(CAPTIONS, dtype=jnp.int32) % block
    return jnp.where(place == jnp.repeat(chosen, block), LENGTH, shortest).astype(jnp.int32)


def draw_norm_params(key, part):
    key = jax.random.fold_in(key, 12)
    keys = jax.random.split(key, 2)
    ramp = 1.0 + 0.8 * jnp.arange(D, dtype=jnp.float32) / D
    gains = ramp[None, :] * jax.random.uniform(keys[0], (2, D), jnp.float32, 0.85, 1.15)
    shifts = 0.3 * jax.random.truncated_normal(keys[1], -4.0, 4.0, (2, D), jnp.float32)
    return jnp.stack([gains[0], shifts[0], gains[1], shifts[1]])


def draw_attn_input(key, part):
    key = jax.random.fold_in(key, 13)
    ramp = 0.75 + 0.5 * jnp.arange(D, dtype=jnp.float32) / D
    base = jax.random.truncated_normal(key, -4.0, 4.0, (D, 3, D), jnp.float32)
    return base * D ** (-0.5) * ramp[None, None, :]


def draw_mlp_up(key, part):
    key = jax.random.fold_in(key, 14)
    ramp = 0.75 + 0.5 * jnp.arange(FF, dtype=jnp.float32) / FF
    base = jax.random.truncated_normal(key, -4.0, 4.0, (D, FF), jnp.float32)
    return base * D ** (-0.5) * ramp[None, :]


def draw_cotangent(key, part):
    key = jax.random.fold_in(key, 15)
    ramp = 0.7 + 0.6 * jnp.arange(D, dtype=jnp.float32) / D
    base = jax.random.truncated_normal(key, -4.0, 4.0, (TOKENS, D), jnp.float32)
    return (base * ramp[None, :]).astype(jnp.bfloat16)


def block_levels(stream_key, extent, cuts, least, top_value):
    level = 1.0
    for dim, shards_of in cuts:
        heights = jax.random.uniform(jax.random.fold_in(jax.random.fold_in(stream_key, 6), dim), (shards_of,), jnp.float32, least / len(cuts), top_value / len(cuts))
        level = level * jnp.repeat(jnp.exp(heights), extent[dim] // shards_of).reshape((-1,) + (1,) * (len(extent) - 1 - dim))
    return level


def gaussian(stream_key, shape, scale, reach, pieces=(), kind=jnp.bfloat16):
    result = jax.random.normal(stream_key, shape, jnp.float32) * scale
    if len(pieces) > 0:
        result = block_levels(stream_key, shape, pieces, -0.22, 0.18) * result
    return jnp.clip(result, min=-reach, max=reach).astype(kind)


def setup_inputs(seed: int = 0) -> dict:
    seeds = jax.random.split(jax.random.key(seed), 22)
    return {
        "block_input": gaussian(seeds[0], (TOKENS, D), 1.0, 6.0, ((0, 32),)),
        "cotangent": draw_cotangent(jax.random.fold_in(seeds[21], 71), 0),
        "lengths": draw_lengths(jax.random.fold_in(seeds[21], 71), 0),
        "attn_input": draw_attn_input(jax.random.fold_in(seeds[21], 71), 0),
        "attn_input_first": gaussian(seeds[4], (D, 3, D), ((4 * D * D + 2 * D * FF + 8 * D + FF) ** -0.5), 0.005859375, ((0, 8), (2, 4)), jnp.float32),
        "attn_input_second": jnp.clip(jnp.exp(math.log(5.644054112963204e-07) - 1.3862944 * jax.random.uniform(seeds[5], (D, 3, D), jnp.float32) ** block_levels(seeds[5], (D, 3, D), ((0, 8), (2, 4)), -0.2, 0.2)), 1.411013528240801e-07, 5.644054112963204e-07),
        "attn_output": gaussian(seeds[6], (D, D), (D // 16) ** -0.5, 0.875, ((0, 8), (1, 4)), jnp.float32),
        "attn_output_first": gaussian(seeds[7], (D, D), ((4 * D * D + 2 * D * FF + 8 * D + FF) ** -0.5), 0.005859375, ((0, 8), (1, 4)), jnp.float32),
        "attn_output_second": jnp.clip(jnp.exp(math.log(5.644054112963204e-07) - 1.3862944 * jax.random.uniform(seeds[8], (D, D), jnp.float32) ** block_levels(seeds[8], (D, D), ((0, 8), (1, 4)), -0.2, 0.2)), 1.411013528240801e-07, 5.644054112963204e-07),
        "mlp_up": draw_mlp_up(jax.random.fold_in(seeds[21], 71), 0),
        "mlp_up_first": gaussian(seeds[10], (D, FF), (0.3 * (4 * D * D + 2 * D * FF + 8 * D + FF) ** -0.5), 0.0017089844, ((0, 8), (1, 4)), jnp.float32),
        "mlp_up_second": jnp.clip(jnp.exp(math.log(5.644054468234572e-08) - 1.3862944 * jax.random.uniform(seeds[11], (D, FF), jnp.float32) ** block_levels(seeds[11], (D, FF), ((0, 8), (1, 4)), -0.2, 0.2)), 1.411013617058643e-08, 5.644054468234572e-08),
        "mlp_down": gaussian(seeds[12], (D, FF), FF ** -0.5, 0.109375, ((0, 8), (1, 4)), jnp.float32),
        "mlp_down_first": gaussian(seeds[13], (D, FF), ((4 * D * D + 2 * D * FF + 8 * D + FF) ** -0.5), 0.005859375, ((0, 8), (1, 4)), jnp.float32),
        "mlp_down_second": jnp.clip(jnp.exp(math.log(5.644054112963204e-07) - 1.3862944 * jax.random.uniform(seeds[14], (D, FF), jnp.float32) ** block_levels(seeds[14], (D, FF), ((0, 8), (1, 4)), -0.2, 0.2)), 1.411013528240801e-07, 5.644054112963204e-07),
        "norm_params": draw_norm_params(jax.random.fold_in(seeds[21], 71), 0),
        "norm_first": gaussian(seeds[16], (4, D), ((4 * D * D + 2 * D * FF + 8 * D + FF) ** -0.5), 0.005859375, ((1, 32),), jnp.float32),
        "norm_second": jnp.clip(jnp.exp(math.log(5.644054112963204e-07) - 1.3862944 * jax.random.uniform(seeds[17], (4, D), jnp.float32) ** block_levels(seeds[17], (4, D), ((1, 32),), -0.2, 0.2)), 1.411013528240801e-07, 5.644054112963204e-07),
        "bias_params": gaussian(seeds[18], (FF // D + 4, D), 0.3, 4.0, (), jnp.float32),
        "bias_first": gaussian(seeds[19], (FF // D + 4, D), ((4 * D * D + 2 * D * FF + 8 * D + FF) ** -0.5), 0.005859375, ((1, 32),), jnp.float32),
        "bias_second": jnp.clip(jnp.exp(math.log(5.644054112963204e-07) - 1.3862944 * jax.random.uniform(seeds[20], (FF // D + 4, D), jnp.float32) ** block_levels(seeds[20], (FF // D + 4, D), ((1, 32),), -0.2, 0.2)), 1.411013528240801e-07, 5.644054112963204e-07),
    }


@jax.custom_vjp
def low(v):
    return lax.optimization_barrier(v.astype(jnp.bfloat16)).astype(jnp.float32)

@jax.custom_vjp
def low_back(v):
    return v

def low_keep(v):
    return (low(v), None)

def low_pass(kept, grad):
    return (grad,)

def back_keep(v):
    return (v, None)

def back_low(kept, grad):
    return (low(grad),)
low.defvjp(low_keep, low_pass)
low_back.defvjp(back_keep, back_low)
highest = lax.Precision.HIGHEST
norm_eps = 1e-06
beta_first = 0.5
beta_second = 0.5
adam_eps = 1e-08
matrix_rate = 0.03
small_rate = 0.3
matrix_decay = 0.01
clip_limit = 1.0
masked_score = -1e+30

def layer_norm(rows, gain, shift):
    center = lax.optimization_barrier(jnp.mean(rows, axis=-1, keepdims=True))
    centered = rows - center
    spread = lax.optimization_barrier(jnp.mean(centered * centered, axis=-1, keepdims=True))
    return centered * lax.rsqrt(spread + norm_eps) * gain + shift

def forward(rows, attn_input, attn_output, mlp_up, mlp_down, norm_params, bias_params, valid):
    count, length = valid.shape
    width = rows.shape[1]
    units = bias_params.shape[0] - 4
    heads = width // HEAD
    input_low = low(attn_input)
    output_low = low(attn_output)
    up_low = low(mlp_up)
    down_low = low(mlp_down)
    normed_one = low(layer_norm(rows, norm_params[0], norm_params[1]))
    joined = jnp.dot(normed_one, input_low.reshape(width, 3 * width), precision=highest)
    query = low_back(low(joined[:, :width] + bias_params[units]))
    keys_all = low_back(low(joined[:, width:2 * width]))
    values = low_back(low(joined[:, 2 * width:] + bias_params[units + 1]))

    def split(tensor):
        return tensor.reshape(count, length, heads, HEAD)
    scores = jnp.einsum('cqhd,ckhd->chqk', split(query), split(keys_all), precision=highest) * HEAD ** (-0.5)
    scores = low_back(scores)
    scores = jnp.where(valid[:, None, None, :], scores, masked_score)
    top = lax.optimization_barrier(jnp.max(scores, axis=-1, keepdims=True))
    expo = jnp.exp(scores - top)
    probs = low(expo / lax.optimization_barrier(jnp.sum(expo, axis=-1, keepdims=True)))
    attended = jnp.einsum('chqk,ckhd->cqhd', probs, split(values), precision=highest).reshape(count * length, width)
    attended = low_back(low(attended))
    branch = low_back(jnp.dot(attended, output_low.T, precision=highest))
    middle = rows + branch + bias_params[units + 2]
    normed_two = low(layer_norm(middle, norm_params[2], norm_params[3]))
    expanded = low_back(jnp.dot(normed_two, up_low, precision=highest) + bias_params[:units].reshape(-1))
    hidden = low(jax.nn.gelu(expanded, approximate=True))
    branch_two = low_back(jnp.dot(hidden, down_low.T, precision=highest))
    return middle + branch_two + bias_params[units + 3]

def adam_step(weight, first, second, grad, rate, decay):
    first_new = beta_first * first + (1.0 - beta_first) * grad
    second_new = beta_second * second + (1.0 - beta_second) * grad * grad
    first_hat = first_new / (1.0 - beta_first ** STEP)
    second_hat = second_new / (1.0 - beta_second ** STEP)
    weight_new = weight - rate * (first_hat / (jnp.sqrt(second_hat) + adam_eps) + decay * weight)
    return (weight_new, first_new, second_new)

def reference(block_input, cotangent, lengths, attn_input, attn_input_first, attn_input_second, attn_output, attn_output_first, attn_output_second, mlp_up, mlp_up_first, mlp_up_second, mlp_down, mlp_down_first, mlp_down_second, norm_params, norm_first, norm_second, bias_params, bias_first, bias_second):
    params = (attn_input, attn_output, mlp_up, mlp_down, norm_params, bias_params)
    block = CAP_DEV * N_MP
    rows = block_input.astype(jnp.float32).reshape(N_DP, block * LENGTH, D)
    cots = cotangent.astype(jnp.float32).reshape(N_DP, block * LENGTH, D)
    lens = lengths.reshape(N_DP, block)
    positions = jnp.arange(LENGTH, dtype=jnp.int32)

    def step(total, item):
        part_rows, part_cots, part_lens = item
        valid = positions[None, :] < part_lens[:, None]

        def local(x, first_w, second_w, third_w, fourth_w, norms, biases):
            return forward(x, first_w, second_w, third_w, fourth_w, norms, biases, valid)
        output, pull = jax.vjp(local, part_rows, *params)
        grads = pull(part_cots * valid.reshape(-1, 1).astype(jnp.float32))
        total = tuple((acc + grad for acc, grad in zip(total, grads[1:])))
        return (total, (output, grads[0]))
    start = tuple((jnp.zeros_like(param) for param in params))
    total, (outputs, input_grads) = lax.scan(step, start, (rows, cots, lens))
    square_total = jnp.zeros((), jnp.float32)
    for grad in total:
        square_total = square_total + jnp.sum(grad * grad)
    grad_norm = jnp.sqrt(square_total)
    factor = jnp.minimum(1.0, clip_limit / (grad_norm + 1e-06))
    results = [outputs.reshape(TOKENS, D).astype(jnp.bfloat16), input_grads.reshape(TOKENS, D), grad_norm]
    matrices = ((attn_input, attn_input_first, attn_input_second), (attn_output, attn_output_first, attn_output_second), (mlp_up, mlp_up_first, mlp_up_second), (mlp_down, mlp_down_first, mlp_down_second))
    for index in range(4):
        weight, first, second = matrices[index]
        clipped = total[index] * factor
        new, first_new, second_new = adam_step(weight, first, second, clipped, matrix_rate, matrix_decay)
        results += [clipped, new, first_new, second_new, new.astype(jnp.bfloat16)]
    smalls = ((norm_params, norm_first, norm_second), (bias_params, bias_first, bias_second))
    for index in range(2):
        weight, first, second = smalls[index]
        clipped = total[4 + index] * factor
        new, first_new, second_new = adam_step(weight, first, second, clipped, small_rate, 0.0)
        results += [clipped, new, first_new, second_new]
    return tuple(results)
```

```python
import functools
import math

import jax
import jax.numpy as jnp
import numpy as np
from jax import lax
from jax.experimental import pallas as pl
from jax.experimental.pallas import tpu as pltpu
from jax.sharding import Mesh, PartitionSpec as P

HEAD = 64
STEP = 10

norm_eps = 1e-06
beta_first = 0.5
beta_second = 0.5
adam_eps = 1e-08
matrix_rate = 0.03
small_rate = 0.3
matrix_decay = 0.01
clip_limit = 1.0
masked_score = -1e30

f32 = jnp.float32
bf16 = jnp.bfloat16
AXES = ("z", "x", "y", "c")
VMEM_LIMIT = 56 * 1024 * 1024
PAIR = 2 * HEAD
GELU_A = math.sqrt(2.0 / math.pi)
GELU_B = 0.044715


class Plan:
    def __init__(self, dims):
        self.dims = dims
        self.z = dims[0]
        self.zbits = [1 << i for i in range(int(math.log2(self.z)))]
        places = [tuple(p) for p in np.ndindex(*dims)]

        def perm(move):
            index = {p: i for i, p in enumerate(places)}
            return [(index[p], index[move(*p)]) for p in places]

        self.to_core = perm(lambda z, x, y, c: (z, x, y, 1 - c))
        self.to_a = perm(lambda z, x, y, c: (z, x ^ (1 - c), y ^ c, c))
        self.to_b = perm(lambda z, x, y, c: (z, x ^ c, y ^ (1 - c), c))
        self.to_z = [
            perm(lambda z, x, y, c, bit=bit: (z ^ bit, x, y, c)) for bit in self.zbits
        ]
        self.slots = [
            (pc, br, ar, zr)
            for pc in range(2)
            for br in range(2)
            for ar in range(2)
            for zr in range(self.z)
        ]

    def send(self, value, perm):
        return lax.ppermute(value, AXES, perm)

    def table(self):
        me = [lax.axis_index(axis) for axis in AXES]
        pc, br, ar, zr = (jnp.asarray(v, jnp.int32) for v in zip(*self.slots))
        core = me[3] ^ pc
        x = me[1] ^ jnp.where(core == 0, ar, br)
        y = me[2] ^ jnp.where(core == 0, br, ar)
        dp = (me[0] ^ zr) * self.dims[1] + x
        mp = y * 2 + core
        return mp * (self.z * self.dims[1]) + dp

    def gather(self, shard):
        block = shard[None]
        for to_z in self.to_z:
            block = jnp.concatenate([block, self.send(block, to_z)], axis=0)
        from_a = self.send(block, self.to_a)
        from_b = self.send(block, self.to_b)
        from_ab = self.send(from_a, self.to_b)
        own = [block, from_a, from_b, from_ab]
        return own + [self.send(piece, self.to_core) for piece in own]

    def reduce(self, own, other, wire):
        z = self.z

        def up(v):
            return v.astype(f32)

        from_core = self.send(other, self.to_core)
        part = up(own[2 * z :]) + up(from_core[2 * z :])
        from_b = self.send(part.astype(wire), self.to_b)
        part = up(own[z : 2 * z]) + up(from_core[z : 2 * z]) + up(from_b[z:])
        from_a = self.send(part.astype(wire), self.to_a)
        total = up(own[:z]) + up(from_core[:z]) + up(from_b[:z]) + up(from_a)
        for bit, to_z in zip(reversed(self.zbits), reversed(self.to_z)):
            received = self.send(total[bit:].astype(wire), to_z)
            total = total[:bit] + up(received)
        return total[0]

    def all_sum(self, value):
        for perm in [self.to_core, self.to_a, self.to_b] + self.to_z:
            value = value + self.send(value, perm)
        return value


def dot(left, right):
    return lax.dot_general(left, right, (((1,), (0,)), ((), ())), preferred_element_type=f32)


def dot_cols(left, right):
    return lax.dot_general(left, right, (((1,), (1,)), ((), ())), preferred_element_type=f32)


def dot_rows(left, right):
    return lax.dot_general(left, right, (((0,), (0,)), ((), ())), preferred_element_type=f32)


def low_lanes(shape):
    return lax.broadcasted_iota(jnp.int32, shape, len(shape) - 1) < HEAD


def swap(value):
    return pltpu.roll(value, HEAD, axis=1)


def moments(rows):
    center = jnp.mean(rows, axis=1, keepdims=True)
    centered = rows - center
    spread = jnp.mean(centered * centered, axis=1, keepdims=True)
    inverse = lax.rsqrt(spread + norm_eps)
    return centered * inverse, inverse


def norm_back(grad_rows, normed, inverse, gain):
    scaled = grad_rows * gain
    return inverse * (
        scaled
        - jnp.mean(scaled, axis=1, keepdims=True)
        - normed * jnp.mean(scaled * normed, axis=1, keepdims=True)
    )


def start_loads(table, pieces, weight, sems, rows, blocks_dp):
    slot = 0
    for piece in pieces:
        for i in range(piece.shape[0]):
            block = table[slot]
            mp = lax.div(block, blocks_dp)
            row = pl.multiple_of(lax.rem(block, blocks_dp) * rows, 16)
            pltpu.make_async_copy(
                piece.at[i], weight.at[mp, pl.ds(row, rows), :], sems.at[mp]
            ).start()
            slot += 1


def wait_load(weight, sems, mp):
    pltpu.make_async_copy(weight.at[mp], weight.at[mp], sems.at[mp]).wait()


def store_blocks(place, stage, step, own, other, sem, rows, dims):
    mz, mx, my, mc = (place[i] for i in range(4))
    pc, yr = 1 - step // 2, step % 2
    target = other if pc else own
    core = mc ^ pc
    z = dims[0]
    for xr in range(2):
        ar = jnp.where(core == 0, xr, yr)
        br = jnp.where(core == 0, yr, xr)
        for zr in range(z):
            dp = (mz ^ zr) * dims[1] + (mx ^ xr)
            row = pl.multiple_of(dp * rows, 16)
            pltpu.make_async_copy(
                stage.at[pl.ds(row, rows), :], target.at[br * (2 * z) + ar * z + zr], sem
            ).start()


def step_mp(place, step):
    pc, yr = 1 - step // 2, step % 2
    return (place[2] ^ yr) * 2 + (place[3] ^ pc)


class Matrix:
    def __init__(self, plan, width, rows):
        self.plan = plan
        self.width = width
        self.rows = rows
        self.direct = rows % 16 == 0
        self.blocks_dp = plan.dims[0] * plan.dims[1]

    def weight_arg(self, pieces, table):
        if self.direct:
            return pieces, table
        stacked = jnp.concatenate(pieces, axis=0)
        order = jnp.argsort(table)
        whole = jnp.take(stacked, order, axis=0)
        whole = whole.reshape(4, self.width, whole.shape[-1])
        return [whole], jnp.arange(4, dtype=jnp.int32)

    def load(self, table, pieces, weight, sems):
        if self.direct:
            start_loads(table, pieces, weight, sems, self.rows, self.blocks_dp)
        else:
            start_loads(table, pieces, weight, sems, self.width, 1)

    def grad_shapes(self, cols):
        if self.direct:
            count = 4 * self.plan.z
            return [jax.ShapeDtypeStruct((count, self.rows, cols), bf16)] * 2
        return [jax.ShapeDtypeStruct((4, self.width, cols), bf16)]

    def store(self, place, stage, step, outs, sem):
        if self.direct:
            store_blocks(place, stage, step, outs[0], outs[1], sem, self.rows, self.plan.dims)
        else:
            pltpu.make_async_copy(stage, outs[0].at[step_mp(place, step)], sem).start()

    def grad_result(self, outs, table):
        if self.direct:
            return outs[0], outs[1]
        whole = outs[0].reshape(4 * self.blocks_dp, self.rows, outs[0].shape[-1])
        half = table.shape[0] // 2
        return jnp.take(whole, table[:half], axis=0), jnp.take(whole, table[half:], axis=0)


def any_spec():
    return pl.BlockSpec(memory_space=pl.ANY)


def vmem_spec():
    return pl.BlockSpec(memory_space=pltpu.VMEM)


def smem_spec():
    return pl.BlockSpec(memory_space=pltpu.SMEM)


def call(kernel, name, args, specs, outs, out_specs, scratch, flops):
    moved = sum(math.prod(a.shape) * a.dtype.itemsize for a in list(args) + list(outs))
    return pl.pallas_call(
        kernel,
        name=name,
        out_shape=outs,
        in_specs=specs,
        out_specs=out_specs,
        scratch_shapes=scratch,
        compiler_params=pltpu.CompilerParams(vmem_limit_bytes=VMEM_LIMIT),
        cost_estimate=pl.CostEstimate(flops=int(flops), bytes_accessed=int(moved), transcendentals=0),
    )(*args)


def attention_forward(matrix, count, width, pieces_n):
    row_block = 256 if count % 256 == 0 else count

    def kernel(*refs):
        table, lens, x_ref, norm_ref, qb_ref, vb_ref, ob_ref = refs[:7]
        pieces = refs[7 : 7 + pieces_n]
        n1_ref, q_ref, k_ref, v_ref, p_ref, a_ref, mid_ref, n2_ref = refs[7 + pieces_n : 15 + pieces_n]
        weight, tail, att, sems = refs[15 + pieces_n :]
        matrix.load(table, pieces, weight, sems)
        gain1, shift1 = norm_ref[0:1, :], norm_ref[1:2, :]
        for r in range(0, count, row_block):
            normed, _ = moments(x_ref[r : r + row_block, :].astype(f32))
            n1_ref[r : r + row_block, :] = (normed * gain1 + shift1).astype(bf16)
        for mp in range(4):
            wait_load(weight, sems, mp)

            def rows_of(i, _, mp=mp):
                at = pl.ds(pl.multiple_of(i * row_block, row_block), row_block)
                joined = dot(n1_ref[at, :], weight[mp, :, 0 : 5 * PAIR])
                q_ref[mp, at, :] = (joined[:, 0:PAIR] + qb_ref[mp : mp + 1, :]).astype(bf16)
                k_ref[mp, at, :] = joined[:, PAIR : 2 * PAIR].astype(bf16)
                v_ref[mp, at, :] = (joined[:, 2 * PAIR : 3 * PAIR] + vb_ref[mp : mp + 1, :]).astype(bf16)
                if mp % 2 == 0:
                    tail[at, :] = joined[:, 3 * PAIR :]
                else:
                    pair = 4 + mp // 2
                    low = low_lanes((row_block, PAIR))
                    even3, even4 = tail[at, 0:PAIR], tail[at, PAIR:]
                    odd3, odd4 = joined[:, 3 * PAIR : 4 * PAIR], joined[:, 4 * PAIR :]
                    query = jnp.where(low, even3, swap(odd3)) + qb_ref[pair : pair + 1, :]
                    value = jnp.where(low, even4, swap(odd4)) + vb_ref[pair : pair + 1, :]
                    q_ref[pair, at, :] = query.astype(bf16)
                    k_ref[pair, at, :] = jnp.where(low, swap(even3), odd3).astype(bf16)
                    v_ref[pair, at, :] = value.astype(bf16)
                return 0

            lax.fori_loop(0, count // row_block, rows_of, 0)

        blocks = count // PAIR
        lane = lax.broadcasted_iota(jnp.int32, (2 * PAIR, PAIR), 1)
        line = lax.broadcasted_iota(jnp.int32, (2 * PAIR, PAIR), 0)
        same = ((line // HEAD) % 2) == (lane // HEAD)
        low = low_lanes((PAIR, PAIR))
        zero = jnp.zeros((PAIR, PAIR), bf16)

        def attend(i, _):
            r = lax.div(i, 6)
            pair = lax.rem(i, 6)
            at = pl.ds(pl.multiple_of(r * PAIR, PAIR), PAIR)
            query = q_ref[pair, at, :]
            stacked = jnp.concatenate([jnp.where(low, query, zero), jnp.where(low, zero, query)], axis=0)
            scores = dot_cols(stacked, k_ref[pair, at, :]) * (HEAD ** (-0.5))
            limit = jnp.where(lane < HEAD, lens[2 * r], lens[2 * r + 1] + HEAD)
            scores = jnp.where(same & (lane < limit), scores, masked_score)
            expo = jnp.exp(scores - jnp.max(scores, axis=1, keepdims=True))
            probs = (expo / jnp.sum(expo, axis=1, keepdims=True)).astype(bf16)
            p_ref[i] = probs
            out = dot(probs, v_ref[pair, at, :])
            att[pair, at, :] = jnp.where(low, out[0:PAIR], out[PAIR:])
            return 0

        lax.fori_loop(0, 6 * blocks, attend, 0, unroll=2)
        low_all = low_lanes((count, PAIR))
        for mp in range(4):
            second = att[4 + mp // 2]
            second = swap(second) if mp % 2 == 0 else second
            a_ref[mp, :, 0:PAIR] = jnp.where(low_all, 0.0, second).astype(bf16)
            a_ref[mp, :, PAIR:] = att[mp].astype(bf16)

        gain2, shift2 = norm_ref[2:3, :], norm_ref[3:4, :]

        def finish(i, _):
            at = pl.ds(pl.multiple_of(i * row_block, row_block), row_block)
            branch = x_ref[at, :].astype(f32) + ob_ref[...]
            for mp in range(4):
                branch = branch + dot_cols(a_ref[mp, at, :], weight[mp, :, 4 * PAIR :])
            mid_ref[at, :] = branch
            normed, _ = moments(branch)
            n2_ref[at, :] = (normed * gain2 + shift2).astype(bf16)
            return 0

        lax.fori_loop(0, count // row_block, finish, 0)

    outs = [
        jax.ShapeDtypeStruct((count, width), bf16),
        jax.ShapeDtypeStruct((6, count, PAIR), bf16),
        jax.ShapeDtypeStruct((6, count, PAIR), bf16),
        jax.ShapeDtypeStruct((6, count, PAIR), bf16),
        jax.ShapeDtypeStruct((6 * (count // PAIR), 2 * PAIR, PAIR), bf16),
        jax.ShapeDtypeStruct((4, count, 2 * PAIR), bf16),
        jax.ShapeDtypeStruct((count, width), f32),
        jax.ShapeDtypeStruct((count, width), bf16),
    ]
    scratch = [
        pltpu.VMEM((4, width, 6 * PAIR), bf16),
        pltpu.VMEM((count, 2 * PAIR), f32),
        pltpu.VMEM((6, count, PAIR), f32),
        pltpu.SemaphoreType.DMA((4,)),
    ]
    return kernel, outs, scratch


def mlp_forward(matrix, count, width, pieces_n):
    row_block = 256 if count % 256 == 0 else count

    def kernel(*refs):
        table, place, n2_ref, glow_ref, ub_ref = refs[:5]
        pieces = refs[5 : 5 + pieces_n]
        h_ref, gp_ref = refs[5 + pieces_n : 7 + pieces_n]
        n_grads = 2 if matrix.direct else 1
        grads = refs[7 + pieces_n : 7 + pieces_n + n_grads]
        weight, stage, sems, out_sem = refs[7 + pieces_n + n_grads :]
        matrix.load(table, pieces, weight, sems)
        for step in range(4):
            mp = step_mp(place, step)
            wait_load(weight, sems, mp)

            def rows_of(i, _):
                at = pl.ds(pl.multiple_of(i * row_block, row_block), row_block)
                value = dot(n2_ref[at, :], weight[mp]) + ub_ref[mp]
                square = value * value
                inner = (GELU_A * value) * (1.0 + GELU_B * square)
                t = jnp.tanh(inner)
                half = 0.5 * (1.0 + t)
                h_ref[mp, at, :] = (value * half).astype(bf16)
                slope = half + (0.5 * GELU_A) * value * (1.0 - t * t) * (1.0 + (3.0 * GELU_B) * square)
                gp_ref[mp, at, :] = slope.astype(bf16)
                return 0

            lax.fori_loop(0, count // row_block, rows_of, 0)
            stage[step] = dot_rows(glow_ref[...], h_ref[mp]).astype(bf16)
            matrix.store(place, stage.at[step], step, grads, out_sem)
        pltpu.make_async_copy(stage, stage, out_sem).wait()

    outs = [
        jax.ShapeDtypeStruct((4, count, width), bf16),
        jax.ShapeDtypeStruct((4, count, width), bf16),
    ] + matrix.grad_shapes(width)
    scratch = [
        pltpu.VMEM((4, width, width), bf16),
        pltpu.VMEM((4, width, width), bf16),
        pltpu.SemaphoreType.DMA((4,)),
        pltpu.SemaphoreType.DMA,
    ]
    return kernel, outs, scratch


def mlp_backward(matrix, count, width, pieces_n):
    row_block = 256 if count % 256 == 0 else count

    def kernel(*refs):
        table, place, glow_ref, gp_ref, n2_ref = refs[:5]
        pieces = refs[5 : 5 + pieces_n]
        eg_ref, ubg_ref = refs[5 + pieces_n : 7 + pieces_n]
        n_grads = 2 if matrix.direct else 1
        grads = refs[7 + pieces_n : 7 + pieces_n + n_grads]
        weight, stage, sems, out_sem = refs[7 + pieces_n + n_grads :]
        matrix.load(table, pieces, weight, sems)
        for step in range(4):
            mp = step_mp(place, step)
            wait_load(weight, sems, mp)

            def rows_of(i, total):
                at = pl.ds(pl.multiple_of(i * row_block, row_block), row_block)
                grad = dot(glow_ref[at, :], weight[mp]) * gp_ref[mp, at, :].astype(f32)
                grad = grad.astype(bf16)
                eg_ref[mp, at, :] = grad
                return total + jnp.sum(grad.astype(f32), axis=0, keepdims=True)

            ubg_ref[mp] = lax.fori_loop(
                0, count // row_block, rows_of, jnp.zeros((1, width), f32)
            )
            stage[step] = dot_rows(n2_ref[...], eg_ref[mp]).astype(bf16)
            matrix.store(place, stage.at[step], step, grads, out_sem)
        pltpu.make_async_copy(stage, stage, out_sem).wait()

    outs = [
        jax.ShapeDtypeStruct((4, count, width), bf16),
        jax.ShapeDtypeStruct((4, 1, width), f32),
    ] + matrix.grad_shapes(width)
    scratch = [
        pltpu.VMEM((4, width, width), bf16),
        pltpu.VMEM((4, width, width), bf16),
        pltpu.SemaphoreType.DMA((4,)),
        pltpu.SemaphoreType.DMA,
    ]
    return kernel, outs, scratch


def middle_backward(matrix, count, width, pieces_n):
    row_block = 256 if count % 256 == 0 else count

    def kernel(*refs):
        table, eg_ref, mid_ref, glow_ref, norm_ref = refs[:5]
        pieces = refs[5 : 5 + pieces_n]
        mg_ref, ml_ref, sums_ref, weight, sems = refs[5 + pieces_n :]
        matrix.load(table, pieces, weight, sems)
        for mp in range(4):
            wait_load(weight, sems, mp)

        def rows_of(i, total):
            at = pl.ds(pl.multiple_of(i * row_block, row_block), row_block)
            two = dot_cols(eg_ref[0, at, :], weight[0])
            for mp in range(1, 4):
                two = two + dot_cols(eg_ref[mp, at, :], weight[mp])
            normed, inverse = moments(mid_ref[at, :])
            out_grad = glow_ref[at, :].astype(f32)
            grad = out_grad + norm_back(two, normed, inverse, norm_ref[2:3, :])
            mg_ref[at, :] = grad
            ml_ref[at, :] = grad.astype(bf16)
            lines = [two * normed, two, grad, out_grad]
            lines = [jnp.sum(line, axis=0, keepdims=True) for line in lines]
            return total + jnp.concatenate(lines, axis=0)

        sums_ref[...] = lax.fori_loop(0, count // row_block, rows_of, jnp.zeros((4, width), f32))

    outs = [
        jax.ShapeDtypeStruct((count, width), f32),
        jax.ShapeDtypeStruct((count, width), bf16),
        jax.ShapeDtypeStruct((4, width), f32),
    ]
    scratch = [pltpu.VMEM((4, width, width), bf16), pltpu.SemaphoreType.DMA((4,))]
    return kernel, outs, scratch


def block_out(matrix, count, width, pieces_n):
    row_block = 256 if count % 256 == 0 else count

    def kernel(*refs):
        table, h_ref, mid_ref, bias_ref = refs[:4]
        pieces = refs[4 : 4 + pieces_n]
        out_ref, weight, sems = refs[4 + pieces_n :]
        matrix.load(table, pieces, weight, sems)
        for mp in range(4):
            wait_load(weight, sems, mp)

        def rows_of(i, _):
            at = pl.ds(pl.multiple_of(i * row_block, row_block), row_block)
            total = mid_ref[at, :] + bias_ref[...]
            for mp in range(4):
                total = total + dot_cols(h_ref[mp, at, :], weight[mp])
            out_ref[at, :] = total.astype(bf16)
            return 0

        lax.fori_loop(0, count // row_block, rows_of, 0)

    outs = [jax.ShapeDtypeStruct((count, width), bf16)]
    scratch = [pltpu.VMEM((4, width, width), bf16), pltpu.SemaphoreType.DMA((4,))]
    return kernel, outs, scratch


def attention_backward(matrix, count, width, pieces_n):
    row_block = 256 if count % 256 == 0 else count

    def kernel(*refs):
        table, place, ml_ref, a_ref, q_ref, k_ref, v_ref, p_ref, n1_ref = refs[:9]
        pieces = refs[9 : 9 + pieces_n]
        dj_ref, qs_ref, vs_ref = refs[9 + pieces_n : 12 + pieces_n]
        n_grads = 2 if matrix.direct else 1
        grads = refs[12 + pieces_n : 12 + pieces_n + n_grads]
        weight, tail, da, dq, dk, dv, stage, sems, out_sem = refs[12 + pieces_n + n_grads :]
        matrix.load(table, pieces, weight, sems)
        for mp in range(4):
            wait_load(weight, sems, mp)

            def rows_of(i, _, mp=mp):
                at = pl.ds(pl.multiple_of(i * row_block, row_block), row_block)
                grad = dot(ml_ref[at, :], weight[mp, :, 4 * PAIR :])
                da[mp, at, :] = grad[:, PAIR:].astype(bf16)
                if mp % 2 == 0:
                    tail[at, :] = grad[:, 0:PAIR]
                else:
                    low = low_lanes((row_block, PAIR))
                    both = jnp.where(low, swap(tail[at, :]), grad[:, 0:PAIR])
                    da[4 + mp // 2, at, :] = both.astype(bf16)
                return 0

            lax.fori_loop(0, count // row_block, rows_of, 0)

        low = low_lanes((PAIR, PAIR))
        zero = jnp.zeros((PAIR, PAIR), bf16)

        def stack(value):
            return jnp.concatenate([jnp.where(low, value, zero), jnp.where(low, zero, value)], axis=0)

        def attend(i, _):
            r = lax.div(i, 6)
            pair = lax.rem(i, 6)
            at = pl.ds(pl.multiple_of(r * PAIR, PAIR), PAIR)
            grad = stack(da[pair, at, :])
            low_probs = p_ref[i]
            probs = low_probs.astype(f32)
            probs_grad = dot_cols(grad, v_ref[pair, at, :])
            shared = jnp.sum(probs * probs_grad, axis=1, keepdims=True)
            scores_grad = (probs * (probs_grad - shared)).astype(bf16)
            dv[pair, at, :] = dot_rows(low_probs, grad)
            both = dot(scores_grad, k_ref[pair, at, :])
            scale = HEAD ** (-0.5)
            dq[pair, at, :] = jnp.where(low, both[0:PAIR], both[PAIR:]) * scale
            dk[pair, at, :] = dot_rows(scores_grad, stack(q_ref[pair, at, :])) * scale
            return 0

        lax.fori_loop(0, 6 * (count // PAIR), attend, 0, unroll=2)
        for pair in range(6):
            qs_ref[pair : pair + 1, :] = jnp.sum(dq[pair].astype(bf16).astype(f32), axis=0, keepdims=True)
            vs_ref[pair : pair + 1, :] = jnp.sum(dv[pair].astype(bf16).astype(f32), axis=0, keepdims=True)
        low_all = low_lanes((count, PAIR))
        for mp in range(4):
            dj_ref[mp, :, 0:PAIR] = dq[mp].astype(bf16)
            dj_ref[mp, :, PAIR : 2 * PAIR] = dk[mp].astype(bf16)
            dj_ref[mp, :, 2 * PAIR : 3 * PAIR] = dv[mp].astype(bf16)
            query, keys, value = dq[4 + mp // 2], dk[4 + mp // 2], dv[4 + mp // 2]
            if mp % 2 == 0:
                third = jnp.where(low_all, query, swap(keys))
                fourth = jnp.where(low_all, value, 0.0)
            else:
                third = jnp.where(low_all, swap(query), keys)
                fourth = jnp.where(low_all, swap(value), 0.0)
            dj_ref[mp, :, 3 * PAIR : 4 * PAIR] = third.astype(bf16)
            dj_ref[mp, :, 4 * PAIR : 5 * PAIR] = fourth.astype(bf16)
        for step in range(4):
            mp = step_mp(place, step)
            first = dot_rows(n1_ref[...], dj_ref[mp])
            second = dot_rows(ml_ref[...], a_ref[mp])
            stage[step, :, 0 : 4 * PAIR] = first[:, 0 : 4 * PAIR].astype(bf16)
            stage[step, :, 4 * PAIR : 5 * PAIR] = (first[:, 4 * PAIR :] + second[:, 0:PAIR]).astype(bf16)
            stage[step, :, 5 * PAIR :] = second[:, PAIR:].astype(bf16)
            matrix.store(place, stage.at[step], step, grads, out_sem)
        pltpu.make_async_copy(stage, stage, out_sem).wait()

    outs = [
        jax.ShapeDtypeStruct((4, count, 5 * PAIR), bf16),
        jax.ShapeDtypeStruct((6, PAIR), f32),
        jax.ShapeDtypeStruct((6, PAIR), f32),
    ] + matrix.grad_shapes(6 * PAIR)
    scratch = [
        pltpu.VMEM((4, width, 6 * PAIR), bf16),
        pltpu.VMEM((count, PAIR), f32),
        pltpu.VMEM((6, count, PAIR), bf16),
        pltpu.VMEM((6, count, PAIR), f32),
        pltpu.VMEM((6, count, PAIR), f32),
        pltpu.VMEM((6, count, PAIR), f32),
        pltpu.VMEM((4, width, 6 * PAIR), bf16),
        pltpu.SemaphoreType.DMA((4,)),
        pltpu.SemaphoreType.DMA,
    ]
    return kernel, outs, scratch


def input_backward(matrix, count, width, pieces_n):
    row_block = 256 if count % 256 == 0 else count

    def kernel(*refs):
        table, dj_ref, x_ref, mg_ref, norm_ref = refs[:5]
        pieces = refs[5 : 5 + pieces_n]
        out_ref, sums_ref, weight, sems = refs[5 + pieces_n :]
        matrix.load(table, pieces, weight, sems)
        for mp in range(4):
            wait_load(weight, sems, mp)

        def rows_of(i, total):
            at = pl.ds(pl.multiple_of(i * row_block, row_block), row_block)
            one = dot_cols(dj_ref[0, at, :], weight[0, :, 0 : 5 * PAIR])
            for mp in range(1, 4):
                one = one + dot_cols(dj_ref[mp, at, :], weight[mp, :, 0 : 5 * PAIR])
            normed, inverse = moments(x_ref[at, :].astype(f32))
            out_ref[at, :] = mg_ref[at, :] + norm_back(one, normed, inverse, norm_ref[0:1, :])
            lines = [jnp.sum(one * normed, axis=0, keepdims=True), jnp.sum(one, axis=0, keepdims=True)]
            return total + jnp.concatenate(lines, axis=0)

        sums_ref[...] = lax.fori_loop(0, count // row_block, rows_of, jnp.zeros((2, width), f32))

    outs = [
        jax.ShapeDtypeStruct((count, width), f32),
        jax.ShapeDtypeStruct((2, width), f32),
    ]
    scratch = [pltpu.VMEM((4, width, 6 * PAIR), bf16), pltpu.SemaphoreType.DMA((4,))]
    return kernel, outs, scratch


def adam_step(weight, first, second, grad, rate, decay):
    first_new = beta_first * first + (1.0 - beta_first) * grad
    second_new = beta_second * second + (1.0 - beta_second) * grad * grad
    first_hat = first_new / (1.0 - beta_first**STEP)
    second_hat = second_new / (1.0 - beta_second**STEP)
    weight_new = weight - rate * (first_hat / (jnp.sqrt(second_hat) + adam_eps) + decay * weight)
    return (weight_new, first_new, second_new)


def pack_attention(inputs, output):
    q, k, v = inputs[:, 0], inputs[:, 1], inputs[:, 2]
    return jnp.concatenate(
        [
            q[:, :PAIR],
            k[:, :PAIR],
            v[:, :PAIR],
            q[:, PAIR:],
            k[:, PAIR:],
            v[:, PAIR:],
            output[:, PAIR:],
            output[:, :PAIR],
        ],
        axis=1,
    )


def unpack_attention(packed):
    def cut(start, size):
        return packed[:, start : start + size]

    q = jnp.concatenate([cut(0, PAIR), cut(3 * PAIR, HEAD)], axis=1)
    k = jnp.concatenate([cut(PAIR, PAIR), cut(3 * PAIR + HEAD, HEAD)], axis=1)
    v = jnp.concatenate([cut(2 * PAIR, PAIR), cut(4 * PAIR, HEAD)], axis=1)
    output = jnp.concatenate([cut(5 * PAIR, PAIR), cut(4 * PAIR + HEAD, HEAD)], axis=1)
    return jnp.stack([q, k, v], axis=1), output


def to_pairs(line):
    groups = line.reshape(4, 3 * HEAD)
    return jnp.concatenate([groups[:, :PAIR], groups[:, PAIR:].reshape(2, PAIR)], axis=0)


def from_pairs(pairs):
    groups = jnp.concatenate([pairs[:4], pairs[4:].reshape(4, HEAD)], axis=1)
    return groups.reshape(-1)


def body(
    plan,
    block_input,
    cotangent,
    lengths,
    attn_input,
    attn_input_first,
    attn_input_second,
    attn_output,
    attn_output_first,
    attn_output_second,
    mlp_up,
    mlp_up_first,
    mlp_up_second,
    mlp_down,
    mlp_down_first,
    mlp_down_second,
    norm_params,
    norm_first,
    norm_second,
    bias_params,
    bias_first,
    bias_second,
):
    width = norm_params.shape[1]
    units = bias_params.shape[0] - 4
    count = block_input.shape[0]
    shard_rows = attn_input.shape[0]
    place = jnp.stack([lax.axis_index(axis) for axis in AXES]).astype(jnp.int32)
    rank = place[2] * 2 + place[3]
    group = (place[0] * plan.dims[1] + place[1]) * 4 + rank
    captions = lengths.shape[0] // 4
    length = count // captions
    lens = lax.dynamic_slice_in_dim(lengths, rank * captions, captions, 0)
    valid = lax.broadcasted_iota(jnp.int32, (captions, length), 1) < lens[:, None]
    grad_low = jnp.where(valid.reshape(-1, 1), cotangent, jnp.zeros((), bf16))
    matrix = Matrix(plan, width, shard_rows)
    table = plan.table()

    pieces_attn = plan.gather(pack_attention(attn_input.astype(bf16), attn_output.astype(bf16)))
    pieces_up = plan.gather(mlp_up.astype(bf16))
    pieces_down = plan.gather(mlp_down.astype(bf16))
    pieces_attn, order = matrix.weight_arg(pieces_attn, table)
    pieces_up, _ = matrix.weight_arg(pieces_up, table)
    pieces_down, _ = matrix.weight_arg(pieces_down, table)
    pieces_n = len(pieces_attn)
    any_pieces = [any_spec()] * pieces_n
    grads_n = 2 if matrix.direct else 1
    any_grads = [any_spec()] * grads_n
    macs = 2.0 * count * width * width

    kernel, outs, scratch = attention_forward(matrix, count, width, pieces_n)
    n1, q, k, v, probs, a_out, middle, n2 = call(
        kernel,
        "attention_forward",
        [order, lens, block_input, norm_params, to_pairs(bias_params[units]), to_pairs(bias_params[units + 1]), bias_params[units + 2 : units + 3]]
        + pieces_attn,
        [smem_spec()] * 2 + [vmem_spec()] * 5 + any_pieces,
        outs,
        [vmem_spec()] * 8,
        scratch,
        5 * macs,
    )
    kernel, outs, scratch = mlp_forward(matrix, count, width, pieces_n)
    hidden, slope, *down_parts = call(
        kernel,
        "mlp_forward",
        [order, place, n2, grad_low, bias_params[:units].reshape(4, 1, width)] + pieces_up,
        [smem_spec()] * 2 + [vmem_spec()] * 3 + any_pieces,
        outs,
        [vmem_spec()] * 2 + any_grads,
        scratch,
        8 * macs,
    )
    kernel, outs, scratch = mlp_backward(matrix, count, width, pieces_n)
    expanded_grad, up_bias_grad, *up_parts = call(
        kernel,
        "mlp_backward",
        [order, place, grad_low, slope, n2] + pieces_down,
        [smem_spec()] * 2 + [vmem_spec()] * 3 + any_pieces,
        outs,
        [vmem_spec()] * 2 + any_grads,
        scratch,
        8 * macs,
    )
    kernel, outs, scratch = middle_backward(matrix, count, width, pieces_n)
    middle_grad, middle_low, sums_two = call(
        kernel,
        "middle_backward",
        [order, expanded_grad, middle, grad_low, norm_params] + pieces_up,
        [smem_spec()] + [vmem_spec()] * 4 + any_pieces,
        outs,
        [vmem_spec()] * 3,
        scratch,
        4 * macs,
    )
    kernel, outs, scratch = attention_backward(matrix, count, width, pieces_n)
    joined_grad, query_sums, value_sums, *attn_parts = call(
        kernel,
        "attention_backward",
        [order, place, middle_low, a_out, q, k, v, probs, n1] + pieces_attn,
        [smem_spec()] * 2 + [vmem_spec()] * 7 + any_pieces,
        outs,
        [vmem_spec()] * 3 + any_grads,
        scratch,
        7 * macs,
    )
    kernel, outs, scratch = input_backward(matrix, count, width, pieces_n)
    input_grad, sums_one = call(
        kernel,
        "input_backward",
        [order, joined_grad, block_input, middle_grad, norm_params] + pieces_attn,
        [smem_spec()] + [vmem_spec()] * 4 + any_pieces,
        outs,
        [vmem_spec()] * 2,
        scratch,
        3 * macs,
    )
    kernel, outs, scratch = block_out(matrix, count, width, pieces_n)
    (block_output,) = call(
        kernel,
        "block_out",
        [order, hidden, middle, bias_params[units + 3 : units + 4]] + pieces_down,
        [smem_spec()] + [vmem_spec()] * 3 + any_pieces,
        outs,
        [vmem_spec()],
        scratch,
        4 * macs,
    )

    down_sum = plan.reduce(*matrix.grad_result(down_parts, table), bf16)
    up_sum = plan.reduce(*matrix.grad_result(up_parts, table), bf16)
    attn_sum = plan.reduce(*matrix.grad_result(attn_parts, table), bf16)
    input_sum, output_sum = unpack_attention(attn_sum)

    columns = norm_first.shape[1]
    small = jnp.concatenate(
        [
            sums_one,
            sums_two[:2],
            up_bias_grad.reshape(units, width),
            from_pairs(query_sums)[None],
            from_pairs(value_sums)[None],
            sums_two[2:],
        ],
        axis=0,
    )
    lines = small.shape[0]
    blocks = small.reshape(lines, -1, 4, columns).transpose(2, 1, 0, 3).reshape(-1, lines * columns)
    blocks = jnp.take(blocks, table, axis=0)
    half = blocks.shape[0] // 2
    small_sum = plan.reduce(blocks[:half], blocks[half:], f32).reshape(lines, columns)
    norm_sum, bias_sum = small_sum[:4], small_sum[4:]

    reduced = (attn_sum, up_sum, down_sum, small_sum)
    squares = sum(jnp.sum(grad * grad) for grad in reduced)
    grad_norm = jnp.sqrt(plan.all_sum(squares.reshape(1, 1))[0, 0])
    factor = jnp.minimum(1.0, clip_limit / (grad_norm + 1e-06))
    own_norm = lax.dynamic_slice_in_dim(norm_params, group * columns, columns, 1)
    own_bias = lax.dynamic_slice_in_dim(bias_params, group * columns, columns, 1)
    results = [block_output, input_grad, grad_norm]
    matrices = (
        (attn_input, attn_input_first, attn_input_second, input_sum),
        (attn_output, attn_output_first, attn_output_second, output_sum),
        (mlp_up, mlp_up_first, mlp_up_second, up_sum),
        (mlp_down, mlp_down_first, mlp_down_second, down_sum),
    )
    for weight, first, second, grad in matrices:
        clipped = grad * factor
        new, first_new, second_new = adam_step(
            weight, first, second, clipped, matrix_rate, matrix_decay
        )
        results += [clipped, new, first_new, second_new, new.astype(bf16)]
    smalls = (
        (own_norm, norm_first, norm_second, norm_sum),
        (own_bias, bias_first, bias_second, bias_sum),
    )
    for weight, first, second, grad in smalls:
        clipped = grad * factor
        new, first_new, second_new = adam_step(weight, first, second, clipped, small_rate, 0.0)
        results += [clipped, new, first_new, second_new]
    return tuple(results)


def solution(mesh):
    dp, mp = mesh.shape["dp"], mesh.shape["mp"]
    dims = (dp // 2, 2, mp // 2, 2)
    fine = Mesh(np.asarray(mesh.devices).reshape(dims), AXES)
    plan = Plan(dims)
    d, m = ("z", "x"), ("y", "c")
    every = d + m
    rows = P(every, None)
    cube = P(d, None, m)
    flat = P(d, m)
    small = P(None, every)
    return jax.shard_map(
        functools.partial(body, plan),
        mesh=fine,
        in_specs=(rows, rows, P(d)) + (cube,) * 3 + (flat,) * 9 + (P(), small, small) * 2,
        out_specs=(rows, rows, P()) + (cube,) * 5 + (flat,) * 15 + (small,) * 8,
        check_vma=False,
    )
```

```python
import functools
import math

import jax
import jax.numpy as jnp
import numpy as np
from jax import lax
from jax.experimental import pallas as pl
from jax.experimental.pallas import tpu as pltpu
from jax.sharding import Mesh, PartitionSpec as P

HEAD = 64
STEP = 10

norm_eps = 1e-06
beta_first = 0.5
beta_second = 0.5
adam_eps = 1e-08
matrix_rate = 0.03
small_rate = 0.3
matrix_decay = 0.01
clip_limit = 1.0
masked_score = -1e30

f32 = jnp.float32
bf16 = jnp.bfloat16
AXES = ("z", "x", "y", "c")
PAIR = 2 * HEAD
GELU_A = math.sqrt(2.0 / math.pi)
GELU_B = 0.044715


def sync(*values):
    return lax.optimization_barrier(values)


def up(value):
    return value.astype(f32)


def join(*values):
    return jnp.concatenate(values, axis=0)


class Plan:
    def __init__(self, dims):
        self.dims = dims
        self.z = dims[0]
        self.zbits = [1 << i for i in range(int(math.log2(self.z)))]
        self.places = [tuple(p) for p in np.ndindex(*dims)]
        self.index = {p: i for i, p in enumerate(self.places)}
        self.core = self.perm(lambda z, x, y, c: (z, x, y, 1 - c))
        self.a = self.perm(lambda z, x, y, c: (z, x ^ (1 - c), y ^ c, c))
        self.b = self.perm(lambda z, x, y, c: (z, x ^ c, y ^ (1 - c), c))
        self.ab = self.perm(lambda z, x, y, c: (z, x ^ 1, y ^ 1, c))
        each = [(br, ar) for br in range(2) for ar in range(2)]
        self.order_az = [(br, ar, zr) for br, ar in each for zr in range(self.z)]
        self.order_za = [
            (br, ar, zr) for br in range(2) for zr in range(self.z) for ar in range(2)
        ]

    def perm(self, move):
        return [(self.index[p], self.index[move(*p)]) for p in self.places]

    def zmove(self, mask):
        return self.perm(lambda z, x, y, c: (z ^ mask, x, y, c))

    def send(self, value, perm):
        return lax.ppermute(value, AXES, perm)

    def send_z(self, value, mask):
        return self.send(value, self.zmove(mask))

    def spread(self, block, bits):
        for bit in bits:
            block = join(block, self.send_z(block, bit))
        return block

    def fold(self, total, bits):
        for bit in reversed(bits):
            half = total.shape[0] // 2
            total = total[:half] + up(self.send_z(total[half:].astype(bf16), bit))
        return total

    def table(self, place, slots):
        pc, br, ar, zr = (jnp.asarray(v, jnp.int32) for v in zip(*slots))
        core = place[3] ^ pc
        x = place[1] ^ jnp.where(core == 0, ar, br)
        yr = jnp.where(core == 0, br, ar)
        dp = (place[0] ^ zr) * self.dims[1] + x
        return (2 * pc + yr) * (self.z * self.dims[1]) + dp

    def slots(self, pc, **fixed):
        z_first = fixed.pop("z_first", False)
        order = self.order_za if z_first else self.order_az
        names = ("br", "ar", "zr")
        return [
            (pc,) + slot
            for slot in order
            if all(slot[names.index(name)] == value for name, value in fixed.items())
        ]


def dot(left, right):
    return lax.dot_general(left, right, (((1,), (0,)), ((), ())), preferred_element_type=f32)


def dot_cols(left, right):
    return lax.dot_general(left, right, (((1,), (1,)), ((), ())), preferred_element_type=f32)


def dot_rows(left, right):
    return lax.dot_general(left, right, (((0,), (0,)), ((), ())), preferred_element_type=f32)


def low_lanes(shape):
    return lax.broadcasted_iota(jnp.int32, shape, len(shape) - 1) < HEAD


def swap(value):
    return pltpu.roll(value, HEAD, axis=1)


def moments(rows):
    center = jnp.mean(rows, axis=1, keepdims=True)
    centered = rows - center
    spread = jnp.mean(centered * centered, axis=1, keepdims=True)
    inverse = lax.rsqrt(spread + norm_eps)
    return centered * inverse, inverse


def norm_back(grad_rows, normed, inverse, gain):
    scaled = grad_rows * gain
    return inverse * (
        scaled
        - jnp.mean(scaled, axis=1, keepdims=True)
        - normed * jnp.mean(scaled * normed, axis=1, keepdims=True)
    )


class Matrix:
    def __init__(self, plan, place, width, rows):
        self.plan = plan
        self.place = place
        self.width = width
        self.rows = rows
        self.direct = rows % 16 == 0
        self.blocks_dp = plan.dims[0] * plan.dims[1]

    def whole(self, pieces):
        order = [slot for _, slots in pieces for slot in slots]
        blocks = join(*[array for array, _ in pieces])
        turn = jnp.argsort(self.plan.table(self.place, order))
        return jnp.take(blocks, turn, axis=0).reshape(4, self.width, blocks.shape[-1])

    def place_blocks(self, place, refs, slots, weight):
        for ref, of_ref in zip(refs, slots):
            for i, (pc, br, ar, zr) in enumerate(of_ref):
                core = place[3] ^ pc
                xr = jnp.where(core == 0, ar, br)
                yr = jnp.where(core == 0, br, ar)
                dp = (place[0] ^ zr) * self.plan.dims[1] + (place[1] ^ xr)
                row = pl.multiple_of(dp * self.rows, 16)
                weight[2 * pc + yr, pl.ds(row, self.rows), :] = ref[i]

    def weight_args(self, pieces):
        if self.direct:
            slots = [of for _, of in pieces]
            return [array for array, _ in pieces], functools.partial(self.fill, slots)
        return [self.whole(pieces)], lambda place, refs, weight: self.copy(refs, weight)

    def fill(self, slots, place, refs, weight):
        self.place_blocks(place, refs, slots, weight)

    def copy(self, refs, weight):
        weight[...] = refs[0][...]

    def grad_shapes(self, cols):
        if self.direct:
            return [jax.ShapeDtypeStruct((4 * self.plan.z, self.rows, cols), bf16)]
        return [jax.ShapeDtypeStruct((2, self.width, cols), bf16)]

    def store(self, place, parts, yr, order, out):
        if not self.direct:
            for at, part in parts:
                out[yr, :, at : at + part.shape[1]] = part.astype(bf16)
            return
        z = self.plan.z
        core = place[3]
        for dp in range(self.blocks_dp):
            zr = place[0] ^ (dp // self.plan.dims[1])
            xr = place[1] ^ (dp % self.plan.dims[1])
            ar = jnp.where(core == 0, xr, yr)
            br = jnp.where(core == 0, yr, xr)
            if order is self.plan.order_az:
                slot = br * (2 * z) + ar * z + zr
            else:
                slot = br * (2 * z) + zr * 2 + ar
            rows = slice(dp * self.rows, (dp + 1) * self.rows)
            for at, part in parts:
                out[slot, :, at : at + part.shape[1]] = part[rows, :].astype(bf16)

    def grad_result(self, grad, order):
        if self.direct:
            return grad
        whole = grad.reshape(2 * self.blocks_dp, self.rows, grad.shape[-1])
        table = self.plan.table(self.place, [(0,) + slot for slot in order])
        return jnp.take(whole, table, axis=0)


def call(kernel, name, scalars, arrays, outs, scratch=(), mib=16, hbm=()):
    scalars, arrays, outs = list(scalars), list(arrays), list(outs)
    hbm = [pltpu.with_memory_space_constraint(part, pltpu.HBM) for part in hbm]
    counts = (len(scalars), len(arrays), len(hbm), len(outs), len(hbm), min(len(hbm), 1))

    def split(*refs):
        parts, at = [], 0
        for n in counts:
            parts.append(list(refs[at : at + n]))
            at += n
        copies = [
            pltpu.make_async_copy(source, target, parts[5][0].at[i])
            for i, (source, target) in enumerate(zip(parts[2], parts[4]))
        ]
        for copy in copies:
            copy.start()
        for copy in copies:
            copy.wait()
        kernel(parts[0], parts[1] + parts[4], parts[3], *refs[at:])

    vmem = pl.BlockSpec(memory_space=pltpu.VMEM)
    specs = [pl.BlockSpec(memory_space=pltpu.SMEM)] * len(scalars) + [vmem] * len(arrays)
    specs += [pl.BlockSpec(memory_space=pltpu.HBM)] * len(hbm)
    own = [pltpu.VMEM(part.shape, part.dtype) for part in hbm]
    if hbm:
        own.append(pltpu.SemaphoreType.DMA((len(hbm),)))
    return pl.pallas_call(
        split,
        name=name,
        out_shape=outs,
        in_specs=specs,
        out_specs=[vmem] * len(outs),
        scratch_shapes=own + list(scratch),
        compiler_params=pltpu.CompilerParams(vmem_limit_bytes=mib * 2**20),
        cost_estimate=pl.CostEstimate(flops=1, bytes_accessed=1, transcendentals=0),
    )(*scalars, *arrays, *hbm)


def shape(dims, kind):
    return jax.ShapeDtypeStruct(tuple(dims), kind)


def rank_of(place):
    return place[2] * 2 + place[3]


def block_of(place, step):
    return rank_of(place) ^ (2 * (step % 2) + step // 2)


def row_blocks(count):
    size = 256 if count % 256 == 0 else count
    return [slice(r, r + size) for r in range(0, count, size)]


def joined(name, matrix, *groups):
    if not matrix.direct:
        return [join(*group) for group in groups]

    def kernel(scalars, arrays, outs):
        at = 0
        for group, out in zip(groups, outs):
            row = 0
            for _ in group:
                for i in range(arrays[at].shape[0]):
                    out[row] = arrays[at][i]
                    row += 1
                at += 1

    outs = []
    for group in groups:
        rows = sum(part.shape[0] for part in group)
        outs.append(shape((rows,) + group[0].shape[1:], group[0].dtype))
    arrays = [part for group in groups for part in group]
    return call(kernel, name, [], arrays, outs, mib=8)


def added(name, matrix, *sums):
    if not matrix.direct:
        return [
            sum(up(part[at : at + count]) for part, at in terms).astype(kind)
            for count, kind, terms in sums
        ]
    arrays = []
    for _, _, terms in sums:
        for part, _ in terms:
            if not any(part is other for other in arrays):
                arrays.append(part)

    def where(part):
        return next(i for i, other in enumerate(arrays) if part is other)

    def kernel(scalars, refs, outs):
        for (count, kind, terms), out in zip(sums, outs):
            for i in range(count):
                total = up(refs[where(terms[0][0])][terms[0][1] + i])
                for part, at in terms[1:]:
                    total = total + up(refs[where(part)][at + i])
                out[i] = total.astype(kind)

    outs = [shape((count,) + terms[0][0].shape[1:], kind) for count, kind, terms in sums]
    return call(kernel, name, [], arrays, outs, mib=8)


def pack_attention(inputs, output):
    rows = output.shape[0]

    def kernel(scalars, arrays, outs):
        in_ref, out_ref = arrays
        parts = [in_ref[t].astype(bf16) for t in range(3)] + [out_ref[...].astype(bf16)]
        for i, part in enumerate(pack_tiles(parts)):
            outs[0][0, :, i * PAIR : (i + 1) * PAIR] = part

    outs = [shape((1, rows, 6 * PAIR), bf16)]
    return call(kernel, "pack_attention", [], [], outs, mib=8, hbm=[inputs, output])[0]


def pack_mlp(above, down):
    def kernel(scalars, arrays, outs):
        for ref, out in zip(arrays, outs):
            out[0] = ref[...].astype(bf16)

    outs = [shape((1,) + above.shape, bf16)] * 2
    return call(kernel, "pack_mlp", [], [], outs, mib=8, hbm=[above, down])


def prepare(scalars, hbm):
    count, width = hbm[0].shape
    units = hbm[3].shape[0] - 4

    def kernel(scalars, arrays, outs):
        place, lens = scalars
        x_ref, cot_ref, norm_ref, bias_ref = arrays
        n1_ref, glow_ref, head_ref = outs
        size = width // 4
        for t in range(2):
            for mp in range(4):
                line = bias_ref[units + t : units + t + 1, mp * size : (mp + 1) * size]
                head_ref[4 * t + mp : 4 * t + mp + 1, 0:size] = line
        gain1, shift1 = norm_ref[0:1, :], norm_ref[1:2, :]
        for at in row_blocks(count):
            normed, _ = moments(up(x_ref[at, :]))
            n1_ref[at, :] = (normed * gain1 + shift1).astype(bf16)
        captions = lens.shape[0] // 4
        length = count // captions
        for j in range(captions):
            at = slice(j * length, (j + 1) * length)
            limit = lens[rank_of(place) * captions + j]
            keep = lax.broadcasted_iota(jnp.int32, (length, width), 0) < limit
            glow_ref[at, :] = jnp.where(keep, up(cot_ref[at, :]), 0.0).astype(bf16)

    outs = [shape((count, width), bf16)] * 2 + [shape((8, 2 * PAIR), f32)]
    return call(kernel, "prepare", scalars, [], outs, hbm=hbm)


def project(scalars, arrays, pieces, fill):
    count, width = arrays[0].shape

    def kernel(scalars, arrays, outs):
        (place,) = scalars
        n1_ref, head_bias = arrays[:2]
        q_ref, k_ref, v_ref, weight = outs
        fill(place, arrays[2:], weight)
        bias = []
        for step in range(4):
            mp = block_of(place, step)
            bias.append((head_bias[pl.ds(mp, 1), :], head_bias[pl.ds(mp + 4, 1), :]))
        low_line = low_lanes((1, PAIR))
        for yr in range(2):
            pair = 4 + yr
            third = [
                jnp.where(low_line, bias[yr][t][:, PAIR:], swap(bias[2 + yr][t][:, PAIR:]))
                for t in range(2)
            ]
            for at in row_blocks(count):
                joined = []
                for step in (yr, 2 + yr):
                    part = dot(n1_ref[at, :], weight[step, :, 0 : 5 * PAIR])
                    query_bias, value_bias = bias[step]
                    q_ref[step, at, :] = (part[:, 0:PAIR] + query_bias[:, :PAIR]).astype(bf16)
                    k_ref[step, at, :] = part[:, PAIR : 2 * PAIR].astype(bf16)
                    v_ref[step, at, :] = (part[:, 2 * PAIR : 3 * PAIR] + value_bias[:, :PAIR]).astype(bf16)
                    joined.append((part[:, 3 * PAIR : 4 * PAIR], part[:, 4 * PAIR :]))
                (own3, own4), (other3, other4) = joined
                low = low_lanes(own3.shape)
                query = jnp.where(low, own3, swap(other3)) + third[0]
                value = jnp.where(low, own4, swap(other4)) + third[1]
                q_ref[pair, at, :] = query.astype(bf16)
                k_ref[pair, at, :] = jnp.where(low, swap(own3), other3).astype(bf16)
                v_ref[pair, at, :] = value.astype(bf16)

    heads = shape((6, count, PAIR), bf16)
    outs = [heads, heads, heads, shape((4, width, 6 * PAIR), bf16)]
    return call(kernel, "project", scalars, list(arrays) + list(pieces), outs)


def attend(scalars, arrays):
    count, width = arrays[0].shape
    blocks = count // PAIR

    def kernel(scalars, arrays, outs, att):
        place, lens = scalars
        x_ref, norm_ref, bias_ref, q_ref, k_ref, v_ref, weight = arrays
        p_ref, own_ref, other_ref, mid_ref, n2_ref = outs
        first = rank_of(place) * (2 * blocks)
        lane = lax.broadcasted_iota(jnp.int32, (2 * PAIR, PAIR), 1)
        line = lax.broadcasted_iota(jnp.int32, (2 * PAIR, PAIR), 0)
        same = ((line // HEAD) % 2) == (lane // HEAD)
        low = low_lanes((PAIR, PAIR))
        zero = jnp.zeros((PAIR, PAIR), bf16)

        def block(r, _):
            at = pl.ds(pl.multiple_of(r * PAIR, PAIR), PAIR)
            limit = jnp.where(lane < HEAD, lens[first + 2 * r], lens[first + 2 * r + 1] + HEAD)
            keep = same & (lane < limit)
            for pair in range(6):
                query = q_ref[pair, at, :]
                stacked = join(jnp.where(low, query, zero), jnp.where(low, zero, query))
                scores = dot_cols(stacked, k_ref[pair, at, :]) * (HEAD ** (-0.5))
                scores = jnp.where(keep, scores, masked_score)
                expo = jnp.exp(scores - jnp.max(scores, axis=1, keepdims=True))
                probs = (expo / jnp.sum(expo, axis=1, keepdims=True)).astype(bf16)
                p_ref[pair, r] = probs
                out = dot(probs, v_ref[pair, at, :])
                att[pair, at, :] = jnp.where(low, out[0:PAIR], out[PAIR:])
            return 0

        lax.fori_loop(0, blocks, block, 0, unroll=2)
        low_all = low_lanes((count, PAIR))
        for step in range(4):
            pc, yr = step // 2, step % 2
            part_ref = (own_ref, other_ref)[pc]
            third = att[4 + yr] if pc else swap(att[4 + yr])
            part_ref[yr, :, 0:PAIR] = jnp.where(low_all, 0.0, third).astype(bf16)
            part_ref[yr, :, PAIR:] = att[step].astype(bf16)
        out_bias = bias_ref[bias_ref.shape[0] - 2 : bias_ref.shape[0] - 1, :]
        gain2, shift2 = norm_ref[2:3, :], norm_ref[3:4, :]
        for at in row_blocks(count):
            branch = up(x_ref[at, :]) + out_bias
            for step in range(4):
                part_ref = (own_ref, other_ref)[step // 2]
                branch = branch + dot_cols(part_ref[step % 2, at, :], weight[step, :, 4 * PAIR :])
            mid_ref[at, :] = branch
            normed, _ = moments(branch)
            n2_ref[at, :] = (normed * gain2 + shift2).astype(bf16)

    part = shape((2, count, 2 * PAIR), bf16)
    outs = [
        shape((6, blocks, 2 * PAIR, PAIR), bf16),
        part,
        part,
        shape((count, width), f32),
        shape((count, width), bf16),
    ]
    return call(kernel, "attend", scalars, arrays, outs, [pltpu.VMEM((6, count, PAIR), f32)])


def mlp_forward(scalars, arrays, pieces, fill):
    count, width = arrays[0].shape

    def kernel(scalars, arrays, outs):
        (place,) = scalars
        n2_ref, bias_ref = arrays[:2]
        gp_ref, weight = outs[4:]
        fill(place, arrays[2:], weight)
        for step in range(4):
            bias = bias_ref[pl.ds(block_of(place, step), 1), :]
            for at in row_blocks(count):
                value = dot(n2_ref[at, :], weight[step]) + bias
                square = value * value
                t = jnp.tanh((GELU_A * value) * (1.0 + GELU_B * square))
                half = 0.5 * (1.0 + t)
                outs[step][at, :] = (value * half).astype(bf16)
                slope = half + (0.5 * GELU_A) * value * (1.0 - t * t) * (1.0 + (3.0 * GELU_B) * square)
                gp_ref[step, at, :] = slope.astype(bf16)

    outs = [shape((count, width), bf16)] * 4
    outs += [shape((4, count, width), bf16), shape((4, width, width), bf16)]
    return call(kernel, "mlp_forward", scalars, list(arrays) + list(pieces), outs)


def gradient(matrix, order, name, scalars, lefts, rights):
    def kernel(scalars, arrays, outs):
        (place,) = scalars
        lefts, rights = arrays[:2], (arrays[2:4], arrays[4:6])
        for yr in range(2):
            total = dot_rows(lefts[0][...], rights[0][yr][...])
            total = total + dot_rows(lefts[1][...], rights[1][yr][...])
            matrix.store(place, [(0, total)], yr, order, outs[0])

    arrays = list(lefts) + list(rights[0]) + list(rights[1])
    (grad,) = call(kernel, name, scalars, arrays, matrix.grad_shapes(rights[0][0].shape[1]))
    return matrix.grad_result(grad, order)


def expanded_backward(scalars, arrays, pieces, fill):
    count, width = arrays[0].shape

    def kernel(scalars, arrays, outs):
        (place,) = scalars
        glow_ref, gp_ref = arrays[:2]
        ubg_ref, weight = outs[4:]
        fill(place, arrays[2:], weight)
        for step in range(4):
            total = jnp.zeros((1, width), f32)
            for at in row_blocks(count):
                grad = (dot(glow_ref[at, :], weight[step]) * up(gp_ref[step, at, :])).astype(bf16)
                outs[step][at, :] = grad
                total = total + jnp.sum(up(grad), axis=0, keepdims=True)
            ubg_ref[step] = total

    outs = [shape((count, width), bf16)] * 4
    outs += [shape((4, 1, width), f32), shape((4, width, width), bf16)]
    return call(kernel, "expanded_backward", scalars, list(arrays) + list(pieces), outs)


def middle_backward(arrays, parts):
    count, width = arrays[0].shape

    def kernel(scalars, arrays, outs):
        mid_ref, glow_ref, norm_ref, weight = arrays[:4]
        mg_ref, ml_ref, sums_ref = outs
        total = jnp.zeros((4, width), f32)
        for at in row_blocks(count):
            two = sum(dot_cols(part[at, :], weight[step]) for step, part in enumerate(arrays[4:]))
            normed, inverse = moments(mid_ref[at, :])
            out_grad = up(glow_ref[at, :])
            grad = out_grad + norm_back(two, normed, inverse, norm_ref[2:3, :])
            mg_ref[at, :] = grad
            ml_ref[at, :] = grad.astype(bf16)
            lines = [two * normed, two, grad, out_grad]
            total = total + join(*[jnp.sum(line, axis=0, keepdims=True) for line in lines])
        sums_ref[...] = total

    outs = [shape((count, width), f32), shape((count, width), bf16), shape((4, width), f32)]
    return call(kernel, "middle_backward", [], list(arrays) + list(parts), outs)


def block_out(arrays, parts):
    count, width = arrays[0].shape

    def kernel(scalars, arrays, outs):
        mid_ref, bias_ref, weight = arrays[:3]
        bias = bias_ref[bias_ref.shape[0] - 1 :, :]
        for at in row_blocks(count):
            total = sum(dot_cols(part[at, :], weight[step]) for step, part in enumerate(arrays[3:]))
            outs[0][at, :] = (mid_ref[at, :] + total + bias).astype(bf16)

    outs = [shape((count, width), bf16)]
    return call(kernel, "block_out", [], list(arrays) + list(parts), outs)[0]


def attention_backward(scalars, arrays):
    count, width = arrays[0].shape
    blocks = count // PAIR

    def kernel(scalars, arrays, outs, da, dq, dk, dv):
        (place,) = scalars
        ml_ref, q_ref, k_ref, v_ref, p_ref, weight = arrays
        lines_ref = outs[4]
        for yr in range(2):
            for at in row_blocks(count):
                ends = []
                for step in (yr, 2 + yr):
                    grad = dot(ml_ref[at, :], weight[step, :, 4 * PAIR :])
                    da[step, at, :] = grad[:, PAIR:].astype(bf16)
                    ends.append(grad[:, 0:PAIR])
                both = jnp.where(low_lanes(ends[0].shape), swap(ends[0]), ends[1])
                da[4 + yr, at, :] = both.astype(bf16)

        low = low_lanes((PAIR, PAIR))
        zero = jnp.zeros((PAIR, PAIR), bf16)
        scale = HEAD ** (-0.5)

        def stack(value):
            return join(jnp.where(low, value, zero), jnp.where(low, zero, value))

        def block(r, _):
            at = pl.ds(pl.multiple_of(r * PAIR, PAIR), PAIR)
            for pair in range(6):
                grad = stack(da[pair, at, :])
                low_probs = p_ref[pair, r]
                probs = up(low_probs)
                probs_grad = dot_cols(grad, v_ref[pair, at, :])
                shared = jnp.sum(probs * probs_grad, axis=1, keepdims=True)
                scores_grad = (probs * (probs_grad - shared)).astype(bf16)
                dv[pair, at, :] = dot_rows(low_probs, grad)
                both = dot(scores_grad, k_ref[pair, at, :])
                dq[pair, at, :] = jnp.where(low, both[0:PAIR], both[PAIR:]) * scale
                dk[pair, at, :] = dot_rows(scores_grad, stack(q_ref[pair, at, :])) * scale
            return 0

        lax.fori_loop(0, blocks, block, 0, unroll=2)
        low_all = low_lanes((count, PAIR))
        low_line = low_lanes((1, PAIR))

        def column_sum(value):
            return jnp.sum(up(value.astype(bf16)), axis=0, keepdims=True)

        for step in range(4):
            pc, yr = step // 2, step % 2
            pair = 4 + yr
            sums = []
            for value in (dq, dv):
                third = column_sum(value[pair])
                third = swap(third) if pc else third
                sums += [column_sum(value[step]), jnp.where(low_line, third, 0.0)]
            sums.append(jnp.zeros((1, width - 4 * PAIR), f32))
            lines_ref[pl.ds(block_of(place, step), 1), :] = jnp.concatenate(sums, axis=1)
            if pc:
                tail3 = jnp.where(low_all, swap(dq[pair]), dk[pair])
                tail4 = jnp.where(low_all, swap(dv[pair]), 0.0)
            else:
                tail3 = jnp.where(low_all, dq[pair], swap(dk[pair]))
                tail4 = jnp.where(low_all, dv[pair], 0.0)
            for i, part in enumerate((dq[step], dk[step], dv[step], tail3, tail4)):
                outs[step][:, i * PAIR : (i + 1) * PAIR] = part.astype(bf16)

    outs = [shape((count, 5 * PAIR), bf16)] * 4 + [shape((4, width), f32)]
    heads = (6, count, PAIR)
    scratch = [pltpu.VMEM(heads, bf16)] + [pltpu.VMEM(heads, f32)] * 3
    return call(kernel, "attention_backward", scalars, arrays, outs, scratch)


def attention_gradient(matrix, order, scalars, lefts, rights, outer_lefts, outer_rights):
    def kernel(scalars, arrays, outs):
        (place,) = scalars
        n1, ml, outer = arrays[0:2], arrays[2:4], arrays[4:6]
        rights = (arrays[6:8], arrays[8:10])
        for yr in range(2):
            first = dot_rows(n1[0][...], rights[0][yr][...])
            first = first + dot_rows(n1[1][...], rights[1][yr][...])
            second = dot_rows(ml[0][...], outer[0][yr]) + dot_rows(ml[1][...], outer[1][yr])
            shared = first[:, 4 * PAIR :] + second[:, 0:PAIR]
            parts = [(0, first[:, 0 : 4 * PAIR]), (4 * PAIR, shared), (5 * PAIR, second[:, PAIR:])]
            matrix.store(place, parts, yr, order, outs[0])

    arrays = list(lefts) + list(outer_lefts) + list(outer_rights) + list(rights[0]) + list(rights[1])
    outs = matrix.grad_shapes(6 * PAIR)
    (grad,) = call(kernel, "attention_gradient", scalars, arrays, outs)
    return matrix.grad_result(grad, order)


def input_backward(scalars, arrays, parts):
    count, width = arrays[0].shape

    def kernel(scalars, arrays, outs):
        (place,) = scalars
        x_ref, mg_ref, norm_ref, weight, sums_ref, ubg_ref, heads_ref = arrays[:7]
        out_ref, lines_ref = outs
        total = jnp.zeros((2, width), f32)
        for at in row_blocks(count):
            one = sum(
                dot_cols(part[at, :], weight[step, :, 0 : 5 * PAIR])
                for step, part in enumerate(arrays[7:])
            )
            normed, inverse = moments(up(x_ref[at, :]))
            out_ref[at, :] = mg_ref[at, :] + norm_back(one, normed, inverse, norm_ref[0:1, :])
            lines = [jnp.sum(one * normed, axis=0, keepdims=True), jnp.sum(one, axis=0, keepdims=True)]
            total = total + join(*lines)
        lines_ref[0:8, :] = join(total, sums_ref[...], jnp.zeros((2, width), f32))
        for step in range(4):
            lines_ref[pl.ds(8 + block_of(place, step), 1), :] = ubg_ref[step]
        lines_ref[12:16, :] = heads_ref[...]

    outs = [shape((count, width), f32), shape((16, width), f32)]
    return call(kernel, "input_backward", scalars, list(arrays) + list(parts), outs)


def adam_step(weight, first, second, grad, rate, decay):
    first_new = beta_first * first + (1.0 - beta_first) * grad
    second_new = beta_second * second + (1.0 - beta_second) * grad * grad
    first_hat = first_new / (1.0 - beta_first**STEP)
    second_hat = second_new / (1.0 - beta_second**STEP)
    weight_new = weight - rate * (first_hat / (jnp.sqrt(second_hat) + adam_eps) + decay * weight)
    return (weight_new, first_new, second_new)


def pack_tiles(parts):
    q, k, v, o = ((part[:, :PAIR], part[:, PAIR:]) for part in parts)
    tail3 = jnp.concatenate([q[1], k[1]], axis=1)
    tail4 = jnp.concatenate([v[1], o[1]], axis=1)
    return q[0], k[0], v[0], tail3, tail4, o[0]


def total_gradients(plan, scalars, parts, lines, params, matrices):
    rows, cols = parts[0][0].shape[1:]
    width = params[0].shape[1]
    columns = width // math.prod(plan.dims)
    counts = [len(part) for part in parts]
    held = sum(counts)

    def kernel(scalars, arrays, outs, small_ref):
        (place,) = scalars
        at, squares = 0, jnp.zeros((1, 1), f32)

        def square(value):
            return jnp.sum(jnp.sum(value * value, axis=1, keepdims=True), axis=0, keepdims=True)

        for m, n in enumerate(counts):
            total = up(arrays[at][0])
            for i in range(1, n):
                total = total + up(arrays[at + i][0])
            outs[0][m] = total
            squares = squares + square(total)
            at += n
        sums = arrays[held][0]
        for ref in arrays[held + 1 : held + len(lines)]:
            sums = sums + ref[0]
        state = arrays[held + len(lines) :]
        size = width // 4
        small_ref[0:4, :] = sums[0:4]
        small_ref[4:8, :] = sums[8:12]
        for t in range(2):
            for mp in range(4):
                line = sums[12 + mp : 13 + mp, 2 * PAIR * t : 2 * PAIR * t + size]
                small_ref[8 + t : 9 + t, mp * size : (mp + 1) * size] = line
        small_ref[10:12, :] = sums[4:6]
        small_ref[12:16, :] = state[12][...]
        small_ref[16:24, :] = state[13][...]
        group = (place[0] * plan.dims[1] + place[1]) * 4 + rank_of(place)
        turn = lax.rem(width - group * columns, width)
        own = pltpu.roll(small_ref[...], turn, axis=1)[:, 0:columns]
        squares = squares + square(own[0:12])
        for out, at, n in zip(outs[3:], (0, 4, 12, 16), (4, 8, 4, 8)):
            out[...] = own[at : at + n]
        outs[1][...] = squares
        for t in range(3):
            parts = [state[t][i] for i in range(3)] + [state[3 + t][...]]
            for i, part in enumerate(pack_tiles(parts)):
                outs[2][t, :, i * PAIR : (i + 1) * PAIR] = part
            outs[2][3 + t] = state[6 + t][...]
            outs[2][6 + t] = state[9 + t][...]

    arrays = [part for group in parts for part in group] + list(lines)
    outs = [shape((3, rows, cols), f32), shape((1, 1), f32), shape((9, rows, cols), f32)]
    outs += [shape((n, columns), f32) for n in (4, 8, 4, 8)]
    state = [value for group in matrices for value in group] + list(params)
    scratch = [pltpu.VMEM((24, width), f32)]
    return call(kernel, "total_gradients", scalars, arrays, outs, scratch, 12, state)


def update(squares, grads, state, small, smalls, shapes):
    def kernel(scalars, arrays, outs):
        norm = jnp.sqrt(arrays[0][...])
        factor = jnp.minimum(1.0, clip_limit / (norm + 1e-06))
        outs[0][...] = norm
        grad_ref, state_ref = arrays[1:3]

        def step(weight, first, second, grad, rate, decay):
            grad = grad * factor
            new, first, second = adam_step(weight, first, second, grad, rate, decay)
            return [grad, new, first, second, new.astype(bf16)]

        for m in range(3):
            values = [state_ref[3 * m + t] for t in range(3)] + [grad_ref[m]]
            values = step(*values, matrix_rate, matrix_decay)
            for i, value in enumerate(values):
                if m:
                    outs[6 + 5 * m + i][...] = value
                    continue
                tiles = [value[:, t * PAIR : (t + 1) * PAIR] for t in range(6)]
                wide = [tiles[3], tiles[4]] if value.dtype == f32 else [up(t) for t in tiles[3:5]]
                tails = [part for t in wide for part in (t, swap(t))]
                for t in range(4):
                    ref = outs[1 + i] if t < 3 else outs[6 + i]
                    head = tiles[t] if t < 3 else tiles[5]
                    tail = tails[t][:, :HEAD].astype(value.dtype)
                    if t < 3:
                        ref[t, :, :PAIR] = head
                        ref[t, :, PAIR:] = tail
                    else:
                        ref[:, :PAIR] = head
                        ref[:, PAIR:] = tail
        for m in range(2):
            weight, first, second = (ref[...] for ref in arrays[5 + 3 * m : 8 + 3 * m])
            values = step(weight, first, second, arrays[3 + m][...], small_rate, 0.0)
            for i in range(4):
                outs[21 + 4 * m + i][...] = values[i]

    arrays = [squares, grads, state] + list(small)
    outs = [shape((1, 1), f32)]
    for dims in shapes:
        outs += [shape(dims, f32)] * 4 + [shape(dims, bf16)]
    for group in smalls:
        arrays += list(group)
        outs += [shape(group[0].shape, f32)] * 4
    return call(kernel, "update", [], arrays, outs)


def body(
    plan,
    block_input,
    cotangent,
    lengths,
    attn_input,
    attn_input_first,
    attn_input_second,
    attn_output,
    attn_output_first,
    attn_output_second,
    mlp_up,
    mlp_up_first,
    mlp_up_second,
    mlp_down,
    mlp_down_first,
    mlp_down_second,
    norm_params,
    norm_first,
    norm_second,
    bias_params,
    bias_first,
    bias_second,
):
    width = norm_params.shape[1]
    place = jnp.stack([lax.axis_index(axis) for axis in AXES]).astype(jnp.int32)
    matrix = Matrix(plan, place, width, attn_input.shape[0])
    send, send_z = plan.send, plan.send_z
    az, za = plan.order_az, plan.order_za
    low_bits, high_bits = plan.zbits[:2], plan.zbits[2:]
    def turned(value):
        return value.transpose(1, 0, 2)

    attn = pack_attention(turned(attn_input), attn_output)
    attn_z = [send_z(attn, mask) for mask in (1, 2, 3)]
    above, down = pack_mlp(mlp_up, mlp_down)
    above_z = send_z(above, 1)
    down_a = send(down, plan.a)
    n1, grad_low, head_bias = prepare(
        [place, lengths], [block_input, cotangent, norm_params, bias_params]
    )
    attn, *attn_z, above, above_z, down, down_a, n1, grad_low, head_bias = sync(
        attn, *attn_z, above, above_z, down, down_a, n1, grad_low, head_bias
    )

    attn, above, down = joined(
        "join_one", matrix, [attn, *attn_z], [above, above_z], [down, down_a]
    )
    attn = plan.spread(attn, high_bits)
    attn_a, attn_b = send(attn, plan.a), send(attn, plan.b)
    above_z = send_z(above, 2)
    down_z = send_z(down, 1)
    attn_c = [send(attn, plan.core)]
    attn, attn_a, attn_b, above, above_z, down, down_z, *attn_c = sync(
        attn, attn_a, attn_b, above, above_z, down, down_z, *attn_c
    )

    def blocks(planes, *fixed, **more):
        return [
            (array, plan.slots(pc, **what, **more))
            for pc, arrays in enumerate(planes)
            for array, what in zip(arrays, fixed)
        ]

    corners = [dict(br=0, ar=0), dict(br=0, ar=1), dict(br=1, ar=0), dict(br=1, ar=1)]
    above, down = joined("join_two", matrix, [above, above_z], [down, down_z])
    above = plan.spread(above, high_bits)
    attn_ab = send(attn_a, plan.b)
    above_a = send(above, plan.a)
    down_z0 = send_z(down[:2], 2)
    attn_c += [send(attn_a, plan.core), send(attn_b, plan.core)]
    attn_ab, above, above_a, down, down_z0, *attn_c[1:] = sync(
        attn_ab, above, above_a, down, down_z0, *attn_c[1:]
    )

    above_b = send(above, plan.b)
    above_ab = send(above_a, plan.b)
    down_z1 = send_z(down[2:], 2)
    above_c = [send(piece, plan.core) for piece in (above, above_a)]
    attn_c.append(send(attn_ab, plan.core))
    pieces = blocks([[attn, attn_a, attn_b, attn_ab], attn_c], *corners)
    pieces, fill = matrix.weight_args(pieces)
    q, k, v, weight_attn = project([place], [n1, head_bias], pieces, fill)
    probs, att_own, att_other, middle, n2 = attend(
        [place, lengths], [block_input, norm_params, bias_params, q, k, v, weight_attn]
    )
    above, above_a, above_b, above_ab, down, down_z0, down_z1, att_other, n2, *above_c = sync(
        above, above_a, above_b, above_ab, down, down_z0, down_z1, att_other, n2, *above_c
    )

    (down,) = joined("join_three", matrix, [down, down_z0, down_z1])
    down = plan.spread(down, high_bits)
    down_b = send(down, plan.b)
    above_c += [send(piece, plan.core) for piece in (above_b, above_ab)]
    pieces = blocks([[above, above_a, above_b, above_ab], above_c], *corners)
    pieces, fill = matrix.weight_args(pieces)
    *hidden, slope, weight_up = mlp_forward([place], [n2, bias_params], pieces, fill)
    n2_c, att_c = send(n2, plan.core), send(att_other, plan.core)
    grad_low_c = send(grad_low, plan.core)
    down_c = [send(down, plan.core)]
    down_b, n2_c, att_c, grad_low_c, down_c[0], *hidden = sync(
        down_b, n2_c, att_c, grad_low_c, down_c[0], *hidden
    )

    down_c.append(send(down_b, plan.core))
    hidden_c = [send(part, plan.core) for part in hidden[2:]]
    pieces = blocks([[down, down_b], down_c], dict(br=0), dict(br=1), z_first=True)

    down_g = gradient(
        matrix, za, "down_gradient", [place], [grad_low, grad_low_c], [hidden[:2], hidden_c]
    )
    pieces, fill = matrix.weight_args(pieces)
    down_g, *pieces = sync(down_g, *pieces)

    half = down_g.shape[0] // 2
    down_gb = send(down_g[half:], plan.b)
    *grads, up_bias_grad, weight_down = expanded_backward(
        [place], [grad_low, slope], pieces, fill
    )
    grads_c = [send(part, plan.core) for part in grads[2:]]
    middle_grad, middle_low, sums_two = middle_backward(
        [middle, grad_low, norm_params, weight_up], grads
    )
    up_g = gradient(matrix, az, "up_gradient", [place], [n2, n2_c], [grads[:2], grads_c])
    block_output = block_out([middle, bias_params, weight_down], hidden)
    up_g, block_output, down_gb, middle_low = sync(up_g, block_output, down_gb, middle_low)

    up_gb = send(up_g[half:], plan.b)
    terms = [down_g, down_gb]
    if high_bits:
        terms = [plan.fold(up(down_g[:half]) + up(down_gb), high_bits)]
    down_s, down_0, down_1 = added(
        "add_one",
        matrix,
        (4, f32, [(part, 0) for part in terms]),
        (2, bf16, [(part, 4) for part in terms]),
        (2, bf16, [(part, 6) for part in terms]),
    )
    down_z0 = send_z(down_0, 2)
    middle_low_c, n1_c = send(middle_low, plan.core), send(n1, plan.core)
    *joint, head_lines = attention_backward(
        [place], [middle_low, q, k, v, probs, weight_attn]
    )
    joint_c = [send(part, plan.core) for part in joint[2:]]
    input_grad, lines = input_backward(
        [place],
        [block_input, middle_grad, norm_params, weight_attn, sums_two, up_bias_grad, head_lines],
        joint,
    )
    input_grad, lines, middle_low_c, n1_c, up_gb, down_z0, *joint_c = sync(
        input_grad, lines[None], middle_low_c, n1_c, up_gb, down_z0, *joint_c
    )

    fourth = half // 2
    (up_0,) = added("add_two", matrix, (fourth, bf16, [(up_g, fourth), (up_gb, fourth)]))
    up_ga = send(up_0, plan.a)
    down_z1 = send_z(down_1, 2)
    lines_c = send(lines, plan.core)
    attn_g = attention_gradient(
        matrix, az, [place], [n1, n1_c], [joint[:2], joint_c],
        [middle_low, middle_low_c], [att_own, att_c],
    )
    attn_gb = send(attn_g[half:], plan.b)
    (lines,) = added("add_lines", matrix, (1, f32, [(lines, 0), (lines_c, 0)]))
    lines_a = send(lines, plan.a)
    terms = [up_g, up_gb, up_ga]
    if high_bits:
        terms = [plan.fold(sum(up(part[:fourth]) for part in terms), high_bits)]
    up_s, up_0, lines = added(
        "add_three",
        matrix,
        (2, f32, [(part, 0) for part in terms]),
        (2, bf16, [(part, 2) for part in terms]),
        (1, f32, [(lines, 0), (lines_a, 0)]),
    )
    up_z = send_z(up_0, 2)
    lines_b = send(lines, plan.b)
    attn_gb, down_z1, lines_b, up_z = sync(attn_gb, down_z1, lines_b, up_z)

    attn_0, down_s, down_0, lines = added(
        "add_four",
        matrix,
        (fourth, bf16, [(attn_g, fourth), (attn_gb, fourth)]),
        (2, f32, [(down_s, 0), (down_z0, 0)]),
        (2, bf16, [(down_s, 2), (down_z1, 0)]),
        (1, f32, [(lines, 0), (lines_b, 0)]),
    )
    attn_ga = send(attn_0, plan.a)
    down_z = send_z(down_0, 1)
    lines_z = send_z(lines, 1)
    up_s, up_0 = added(
        "add_up",
        matrix,
        (1, f32, [(up_s, 0), (up_z, 0)]),
        (1, bf16, [(up_s, 1), (up_z, 1)]),
    )
    up_z = send_z(up_0, 1)
    attn_ga, down_z, lines_z, up_z = sync(attn_ga, down_z, lines_z, up_z)

    terms = [attn_g, attn_gb, attn_ga]
    if high_bits:
        terms = [plan.fold(sum(up(part[:fourth]) for part in terms), high_bits)]
    attn_s, attn_1, attn_2, attn_3, down_s, down_0, lines = added(
        "add_five",
        matrix,
        (1, f32, [(part, 0) for part in terms]),
        (1, bf16, [(part, 1) for part in terms]),
        (1, bf16, [(part, 2) for part in terms]),
        (1, bf16, [(part, 3) for part in terms]),
        (1, f32, [(down_s, 0), (down_z, 0)]),
        (1, bf16, [(down_s, 1), (down_z, 1)]),
        (1, f32, [(lines, 0), (lines_z, 0)]),
    )
    attn_z = [send_z(part, mask) for part, mask in ((attn_1, 1), (attn_2, 2), (attn_3, 3))]
    down_ga = send(down_0, plan.a)
    lines_z = send_z(lines, 2)
    for bit in high_bits:
        lines = lines + lines_z
        lines_z = send_z(lines, bit)
    *attn_z, down_ga, lines_z = sync(*attn_z, down_ga, lines_z)

    matrices = (
        (turned(attn_input), turned(attn_input_first), turned(attn_input_second)),
        (attn_output, attn_output_first, attn_output_second),
        (mlp_up, mlp_up_first, mlp_up_second),
        (mlp_down, mlp_down_first, mlp_down_second),
    )
    sums, squares, state, norm_sum, bias_sum, own_norm, own_bias = total_gradients(
        plan,
        [place],
        [[attn_s, *attn_z], [up_s, up_z], [down_s, down_ga]],
        [lines, lines_z],
        [norm_params, bias_params],
        matrices,
    )
    squares = squares + send(squares, plan.core)
    to_a, to_b, to_ab = (send(squares, perm) for perm in (plan.a, plan.b, plan.ab))
    squares = (squares + to_a) + (to_b + to_ab)
    to_1, to_2, to_3 = (send_z(squares, mask) for mask in (1, 2, 3))
    squares = (squares + to_1) + (to_2 + to_3)
    for bit in high_bits:
        squares = squares + send_z(squares, bit)
    grad_norm, *results = update(
        squares,
        sums,
        state,
        [norm_sum, bias_sum],
        ((own_norm, norm_first, norm_second), (own_bias, bias_first, bias_second)),
        [group[0].shape for group in matrices],
    )
    results[:5] = [turned(value) for value in results[:5]]
    return (block_output, input_grad, grad_norm[0, 0], *results)


def solution(mesh):
    dp, mp = mesh.shape["dp"], mesh.shape["mp"]
    dims = (dp // 2, 2, mp // 2, 2)
    fine = Mesh(np.asarray(mesh.devices).reshape(dims), AXES)
    plan = Plan(dims)
    d, m = ("z", "x"), ("y", "c")
    every = d + m
    rows = P(every, None)
    cube = P(d, None, m)
    flat = P(d, m)
    small = P(None, every)
    return jax.shard_map(
        functools.partial(body, plan),
        mesh=fine,
        in_specs=(rows, rows, P(d)) + (cube,) * 3 + (flat,) * 9 + (P(), small, small) * 2,
        out_specs=(rows, rows, P()) + (cube,) * 5 + (flat,) * 15 + (small,) * 8,
        check_vma=False,
    )
```

```python
import functools
import math

import jax
import jax.numpy as jnp
import numpy as np
from jax import lax
from jax.experimental import pallas as pl
from jax.experimental.pallas import tpu as pltpu
from jax.sharding import Mesh, PartitionSpec as P

HEAD = 64
STEP = 10

norm_eps = 1e-06
beta_first = 0.5
beta_second = 0.5
adam_eps = 1e-08
matrix_rate = 0.03
small_rate = 0.3
matrix_decay = 0.01
clip_limit = 1.0
masked_score = -1e30

f32 = jnp.float32
bf16 = jnp.bfloat16
AXES = ("z", "x", "y", "c")
PAIR = 2 * HEAD
GELU_A = math.sqrt(2.0 / math.pi)
GELU_B = 0.044715


def sync(*values):
    return lax.optimization_barrier(values)


def up(value):
    return value.astype(f32)


def join(*values):
    return jnp.concatenate(values, axis=0)


class Plan:
    def __init__(self, dims):
        self.dims = dims
        self.z = dims[0]
        self.zbits = [1 << i for i in range(int(math.log2(self.z)))]
        self.places = [tuple(p) for p in np.ndindex(*dims)]
        self.index = {p: i for i, p in enumerate(self.places)}
        self.core = self.perm(lambda z, x, y, c: (z, x, y, 1 - c))
        self.a = self.perm(lambda z, x, y, c: (z, x ^ (1 - c), y ^ c, c))
        self.b = self.perm(lambda z, x, y, c: (z, x ^ c, y ^ (1 - c), c))
        self.cross = self.perm(lambda z, x, y, c: (z, x ^ c, y ^ (1 - c), 1 - c))
        each = [(br, ar) for br in range(2) for ar in range(2)]
        turned = sorted(range(self.z), key=self.turn)
        self.plain = [(br, ar, zr) for br, ar in each for zr in range(self.z)]
        self.order_az = [(br, ar, zr) for br, ar in each for zr in turned]
        self.order_za = [(br, ar, zr) for br in range(2) for zr in turned for ar in range(2)]

    def turn(self, zr):
        return (zr >> 2) * 4 + (zr & 1) * 2 + ((zr >> 1) & 1)

    def perm(self, move):
        return [(self.index[p], self.index[move(*p)]) for p in self.places]

    def zmove(self, mask):
        return self.perm(lambda z, x, y, c: (z ^ mask, x, y, c))

    def send(self, value, perm):
        return lax.ppermute(value, AXES, perm)

    def send_z(self, value, mask):
        return self.send(value, self.zmove(mask))

    def spread(self, block, bits):
        for bit in bits:
            block = join(block, self.send_z(block, bit))
        return block

    def fold(self, total, bits):
        for bit in bits[::-1]:
            half = total.shape[0] // 2
            total = total[:half] + up(self.send_z(total[half:].astype(bf16), bit))
        return total

    def table(self, place, slots):
        pc, br, ar, zr = (jnp.asarray(v, jnp.int32) for v in zip(*slots))
        core = place[3] ^ pc
        x = place[1] ^ jnp.where(core == 0, ar, br)
        yr = jnp.where(core == 0, br, ar)
        dp = (place[0] ^ zr) * self.dims[1] + x
        return (2 * pc + yr) * (self.z * self.dims[1]) + dp

    def slots(self, pc, order, **fixed):
        names = ("br", "ar", "zr")
        return [
            (pc,) + slot
            for slot in order
            if all(slot[names.index(name)] == value for name, value in fixed.items())
        ]


def dot(left, right):
    return lax.dot_general(left, right, (((1,), (0,)), ((), ())), preferred_element_type=f32)


def dot_cols(left, right):
    return lax.dot_general(left, right, (((1,), (1,)), ((), ())), preferred_element_type=f32)


def dot_rows(left, right):
    return lax.dot_general(left, right, (((0,), (0,)), ((), ())), preferred_element_type=f32)


def low_lanes(shape):
    return lax.broadcasted_iota(jnp.int32, shape, len(shape) - 1) < HEAD


def swap(value):
    return pltpu.roll(value, HEAD, axis=1)


def moments(rows):
    center = jnp.mean(rows, axis=1, keepdims=True)
    centered = rows - center
    spread = jnp.mean(centered * centered, axis=1, keepdims=True)
    inverse = lax.rsqrt(spread + norm_eps)
    return centered * inverse, inverse


def norm_back(grad_rows, normed, inverse, gain):
    scaled = grad_rows * gain
    return inverse * (
        scaled
        - jnp.mean(scaled, axis=1, keepdims=True)
        - normed * jnp.mean(scaled * normed, axis=1, keepdims=True)
    )


class Matrix:
    def __init__(self, plan, place, width, rows):
        self.plan = plan
        self.place = place
        self.width = width
        self.rows = rows
        self.direct = rows % 16 == 0
        self.blocks_dp = plan.dims[0] * plan.dims[1]

    def whole(self, pieces):
        order = [slot for _, slots in pieces for slot in slots]
        blocks = join(*[array for array, _ in pieces])
        turn = jnp.argsort(self.plan.table(self.place, order))
        return jnp.take(blocks, turn, axis=0).reshape(4, self.width, blocks.shape[-1])

    def place_blocks(self, place, refs, slots, weight):
        for ref, of_ref in zip(refs, slots):
            for i, (pc, br, ar, zr) in enumerate(of_ref):
                core = place[3] ^ pc
                xr = jnp.where(core == 0, ar, br)
                yr = jnp.where(core == 0, br, ar)
                dp = (place[0] ^ zr) * self.plan.dims[1] + (place[1] ^ xr)
                row = pl.multiple_of(dp * self.rows, 16)
                weight[2 * pc + yr, pl.ds(row, self.rows), :] = ref[i]

    def weight_args(self, pieces):
        if self.direct:
            slots = [of for _, of in pieces]
            return [array for array, _ in pieces], functools.partial(self.fill, slots)
        return [self.whole(pieces)], lambda place, refs, weight: self.copy(refs, weight)

    def fill(self, slots, place, refs, weight):
        self.place_blocks(place, refs, slots, weight)

    def copy(self, refs, weight):
        weight[...] = refs[0][...]

    def grad_shapes(self, cols):
        if self.direct:
            return [jax.ShapeDtypeStruct((4 * self.plan.z, self.rows, cols), bf16)]
        return [jax.ShapeDtypeStruct((2, self.width, cols), bf16)]

    def store(self, place, parts, yr, order, out):
        if not self.direct:
            for at, part in parts:
                out[yr, :, at : at + part.shape[1]] = part.astype(bf16)
            return
        z = self.plan.z
        core = place[3]
        for dp in range(self.blocks_dp):
            zr = place[0] ^ (dp // self.plan.dims[1])
            xr = place[1] ^ (dp % self.plan.dims[1])
            ar = jnp.where(core == 0, xr, yr)
            br = jnp.where(core == 0, yr, xr)
            zi = self.plan.turn(zr)
            if order is self.plan.order_az:
                slot = br * (2 * z) + ar * z + zi
            else:
                slot = br * (2 * z) + zi * 2 + ar
            rows = slice(dp * self.rows, (dp + 1) * self.rows)
            for at, part in parts:
                out[slot, :, at : at + part.shape[1]] = part[rows, :].astype(bf16)

    def grad_result(self, grad, order):
        if self.direct:
            return grad
        whole = grad.reshape(2 * self.blocks_dp, self.rows, grad.shape[-1])
        table = self.plan.table(self.place, [(0,) + slot for slot in order])
        return jnp.take(whole, table, axis=0)


def call(kernel, name, scalars, arrays, outs, scratch=(), mib=16, hbm=()):
    scalars, arrays, outs = list(scalars), list(arrays), list(outs)
    hbm = [pltpu.with_memory_space_constraint(part, pltpu.HBM) for part in hbm]
    counts = (len(scalars), len(arrays), len(hbm), len(outs), len(hbm), min(len(hbm), 1))

    def split(*refs):
        parts, at = [], 0
        for n in counts:
            parts.append(list(refs[at : at + n]))
            at += n
        copies = [
            pltpu.make_async_copy(source, target, parts[5][0].at[i])
            for i, (source, target) in enumerate(zip(parts[2], parts[4]))
        ]
        for copy in copies:
            copy.start()
        for copy in copies:
            copy.wait()
        kernel(parts[0], parts[1] + parts[4], parts[3], *refs[at:])

    vmem = pl.BlockSpec(memory_space=pltpu.VMEM)
    specs = [pl.BlockSpec(memory_space=pltpu.SMEM)] * len(scalars) + [vmem] * len(arrays)
    specs += [pl.BlockSpec(memory_space=pltpu.HBM)] * len(hbm)
    own = [pltpu.VMEM(part.shape, part.dtype) for part in hbm]
    if hbm:
        own.append(pltpu.SemaphoreType.DMA((len(hbm),)))
    return pl.pallas_call(
        split,
        name=name,
        out_shape=outs,
        in_specs=specs,
        out_specs=[vmem] * len(outs),
        scratch_shapes=own + list(scratch),
        compiler_params=pltpu.CompilerParams(vmem_limit_bytes=mib * 2**20),
        cost_estimate=pl.CostEstimate(flops=1, bytes_accessed=1, transcendentals=0),
    )(*scalars, *arrays, *hbm)


def shape(dims, kind):
    return jax.ShapeDtypeStruct(tuple(dims), kind)


def rank_of(place):
    return place[2] * 2 + place[3]


def block_of(place, step):
    return rank_of(place) ^ (2 * (step % 2) + step // 2)


def row_blocks(count):
    size = 256 if count % 256 == 0 else count
    return [slice(r, r + size) for r in range(0, count, size)]


def joined(name, matrix, *groups):
    if not matrix.direct:
        return [join(*group) for group in groups]

    def kernel(scalars, arrays, outs):
        at = 0
        for group, out in zip(groups, outs):
            row = 0
            for _ in group:
                for i in range(arrays[at].shape[0]):
                    out[row] = arrays[at][i]
                    row += 1
                at += 1

    outs = []
    for group in groups:
        rows = sum(part.shape[0] for part in group)
        outs.append(shape((rows,) + group[0].shape[1:], group[0].dtype))
    arrays = [part for group in groups for part in group]
    return call(kernel, name, [], arrays, outs, mib=8)


def added(name, matrix, *sums):
    sums = [each if isinstance(each, list) else [each] for each in sums]
    if not matrix.direct:
        return [
            join(*[
                sum(up(part[at : at + count]) for part, at in terms).astype(kind)
                for count, kind, terms in each
            ])
            for each in sums
        ]
    arrays = []
    for each in sums:
        for _, _, terms in each:
            for part, _ in terms:
                if not any(part is other for other in arrays):
                    arrays.append(part)

    def where(part):
        return next(i for i, other in enumerate(arrays) if part is other)

    def kernel(scalars, refs, outs):
        for each, out in zip(sums, outs):
            row = 0
            for count, kind, terms in each:
                for i in range(count):
                    total = up(refs[where(terms[0][0])][terms[0][1] + i])
                    for part, at in terms[1:]:
                        total = total + up(refs[where(part)][at + i])
                    out[row] = total.astype(kind)
                    row += 1

    outs = [
        shape((sum(one[0] for one in each),) + each[0][2][0][0].shape[1:], each[0][1])
        for each in sums
    ]
    return call(kernel, name, [], arrays, outs, mib=8)


def pack_attention(inputs, output):
    rows = output.shape[0]

    def kernel(scalars, arrays, outs):
        in_ref, out_ref = arrays
        parts = [in_ref[t].astype(bf16) for t in range(3)] + [out_ref[...].astype(bf16)]
        for i, part in enumerate(pack_tiles(parts)):
            outs[0][0, :, i * PAIR : (i + 1) * PAIR] = part

    outs = [shape((1, rows, 6 * PAIR), bf16)]
    return call(kernel, "pack_attention", [], [], outs, mib=8, hbm=[inputs, output])[0]


def pack_mlp(above, down):
    def kernel(scalars, arrays, outs):
        for ref, out in zip(arrays, outs):
            out[0] = ref[...].astype(bf16)

    outs = [shape((1,) + above.shape, bf16)] * 2
    return call(kernel, "pack_mlp", [], [], outs, mib=8, hbm=[above, down])


def prepare(scalars, hbm):
    count, width = hbm[0].shape
    units = hbm[3].shape[0] - 4

    def kernel(scalars, arrays, outs):
        place, lens = scalars
        x_ref, cot_ref, norm_ref, bias_ref = arrays
        n1_ref, glow_ref, head_ref = outs
        size = width // 4
        for t in range(2):
            for mp in range(4):
                line = bias_ref[units + t : units + t + 1, mp * size : (mp + 1) * size]
                head_ref[4 * t + mp : 4 * t + mp + 1, 0:size] = line
        gain1, shift1 = norm_ref[0:1, :], norm_ref[1:2, :]
        for at in row_blocks(count):
            normed, _ = moments(up(x_ref[at, :]))
            n1_ref[at, :] = (normed * gain1 + shift1).astype(bf16)
        captions = lens.shape[0] // 4
        length = count // captions
        for j in range(captions):
            at = slice(j * length, (j + 1) * length)
            limit = lens[rank_of(place) * captions + j]
            keep = lax.broadcasted_iota(jnp.int32, (length, width), 0) < limit
            glow_ref[at, :] = jnp.where(keep, up(cot_ref[at, :]), 0.0).astype(bf16)

    outs = [shape((count, width), bf16)] * 2 + [shape((8, 2 * PAIR), f32)]
    return call(kernel, "prepare", scalars, [], outs, hbm=hbm)


def project(scalars, arrays, pieces, fill):
    count, width = arrays[0].shape

    def kernel(scalars, arrays, outs):
        (place,) = scalars
        n1_ref, head_bias = arrays[:2]
        q_ref, k_ref, v_ref, weight = outs
        fill(place, arrays[2:], weight)
        bias = []
        for step in range(4):
            mp = block_of(place, step)
            bias.append((head_bias[pl.ds(mp, 1), :], head_bias[pl.ds(mp + 4, 1), :]))
        low_line = low_lanes((1, PAIR))
        for yr in range(2):
            pair = 4 + yr
            third = [
                jnp.where(low_line, bias[yr][t][:, PAIR:], swap(bias[2 + yr][t][:, PAIR:]))
                for t in range(2)
            ]
            for at in row_blocks(count):
                joined = []
                for step in (yr, 2 + yr):
                    part = dot(n1_ref[at, :], weight[step, :, 0 : 5 * PAIR])
                    query_bias, value_bias = bias[step]
                    q_ref[step, at, :] = (part[:, 0:PAIR] + query_bias[:, :PAIR]).astype(bf16)
                    k_ref[step, at, :] = part[:, PAIR : 2 * PAIR].astype(bf16)
                    v_ref[step, at, :] = (part[:, 2 * PAIR : 3 * PAIR] + value_bias[:, :PAIR]).astype(bf16)
                    joined.append((part[:, 3 * PAIR : 4 * PAIR], part[:, 4 * PAIR :]))
                (own3, own4), (other3, other4) = joined
                low = low_lanes(own3.shape)
                query = jnp.where(low, own3, swap(other3)) + third[0]
                value = jnp.where(low, own4, swap(other4)) + third[1]
                q_ref[pair, at, :] = query.astype(bf16)
                k_ref[pair, at, :] = jnp.where(low, swap(own3), other3).astype(bf16)
                v_ref[pair, at, :] = value.astype(bf16)

    heads = shape((6, count, PAIR), bf16)
    outs = [heads, heads, heads, shape((4, width, 6 * PAIR), bf16)]
    return call(kernel, "project", scalars, list(arrays) + list(pieces), outs)


def attend(scalars, arrays):
    count, width = arrays[0].shape
    blocks = count // PAIR

    def kernel(scalars, arrays, outs, att):
        place, lens = scalars
        x_ref, norm_ref, bias_ref, q_ref, k_ref, v_ref, weight = arrays
        p_ref, own_ref, other_ref, mid_ref, n2_ref = outs
        first = rank_of(place) * (2 * blocks)
        lane = lax.broadcasted_iota(jnp.int32, (2 * PAIR, PAIR), 1)
        line = lax.broadcasted_iota(jnp.int32, (2 * PAIR, PAIR), 0)
        same = ((line // HEAD) % 2) == (lane // HEAD)
        low = low_lanes((PAIR, PAIR))
        zero = jnp.zeros((PAIR, PAIR), bf16)

        def block(r, _):
            at = pl.ds(pl.multiple_of(r * PAIR, PAIR), PAIR)
            limit = jnp.where(lane < HEAD, lens[first + 2 * r], lens[first + 2 * r + 1] + HEAD)
            keep = same & (lane < limit)
            for pair in range(6):
                query = q_ref[pair, at, :]
                stacked = join(jnp.where(low, query, zero), jnp.where(low, zero, query))
                scores = dot_cols(stacked, k_ref[pair, at, :]) * (HEAD ** (-0.5))
                scores = jnp.where(keep, scores, masked_score)
                expo = jnp.exp(scores - jnp.max(scores, axis=1, keepdims=True))
                probs = (expo / jnp.sum(expo, axis=1, keepdims=True)).astype(bf16)
                p_ref[pair, r] = probs
                out = dot(probs, v_ref[pair, at, :])
                att[pair, at, :] = jnp.where(low, out[0:PAIR], out[PAIR:])
            return 0

        lax.fori_loop(0, blocks, block, 0, unroll=2)
        low_all = low_lanes((count, PAIR))
        for step in range(4):
            pc, yr = step // 2, step % 2
            part_ref = (own_ref, other_ref)[pc]
            third = att[4 + yr] if pc else swap(att[4 + yr])
            part_ref[yr, :, 0:PAIR] = jnp.where(low_all, 0.0, third).astype(bf16)
            part_ref[yr, :, PAIR:] = att[step].astype(bf16)
        out_bias = bias_ref[bias_ref.shape[0] - 2 : bias_ref.shape[0] - 1, :]
        gain2, shift2 = norm_ref[2:3, :], norm_ref[3:4, :]
        for at in row_blocks(count):
            branch = up(x_ref[at, :]) + out_bias
            for step in range(4):
                part_ref = (own_ref, other_ref)[step // 2]
                branch = branch + dot_cols(part_ref[step % 2, at, :], weight[step, :, 4 * PAIR :])
            mid_ref[at, :] = branch
            normed, _ = moments(branch)
            n2_ref[at, :] = (normed * gain2 + shift2).astype(bf16)

    part = shape((2, count, 2 * PAIR), bf16)
    outs = [
        shape((6, blocks, 2 * PAIR, PAIR), bf16),
        part,
        part,
        shape((count, width), f32),
        shape((count, width), bf16),
    ]
    return call(kernel, "attend", scalars, arrays, outs, [pltpu.VMEM((6, count, PAIR), f32)])


def mlp_forward(scalars, arrays, pieces, fill):
    count, width = arrays[0].shape

    def kernel(scalars, arrays, outs):
        (place,) = scalars
        n2_ref, bias_ref = arrays[:2]
        gp_ref, weight = outs[4:]
        fill(place, arrays[2:], weight)
        for step in range(4):
            bias = bias_ref[pl.ds(block_of(place, step), 1), :]
            for at in row_blocks(count):
                value = dot(n2_ref[at, :], weight[step]) + bias
                square = value * value
                t = jnp.tanh((GELU_A * value) * (1.0 + GELU_B * square))
                half = 0.5 * (1.0 + t)
                outs[step][at, :] = (value * half).astype(bf16)
                slope = half + (0.5 * GELU_A) * value * (1.0 - t * t) * (1.0 + (3.0 * GELU_B) * square)
                gp_ref[step, at, :] = slope.astype(bf16)

    outs = [shape((count, width), bf16)] * 4
    outs += [shape((4, count, width), bf16), shape((4, width, width), bf16)]
    return call(kernel, "mlp_forward", scalars, list(arrays) + list(pieces), outs)


def gradient(matrix, order, name, scalars, lefts, rights):
    def kernel(scalars, arrays, outs):
        (place,) = scalars
        lefts, rights = arrays[:2], (arrays[2:4], arrays[4:6])
        for yr in range(2):
            total = dot_rows(lefts[0][...], rights[0][yr][...])
            total = total + dot_rows(lefts[1][...], rights[1][yr][...])
            matrix.store(place, [(0, total)], yr, order, outs[0])

    arrays = list(lefts) + list(rights[0]) + list(rights[1])
    (grad,) = call(kernel, name, scalars, arrays, matrix.grad_shapes(rights[0][0].shape[1]))
    return matrix.grad_result(grad, order)


def expanded_backward(scalars, arrays, pieces, fill):
    count, width = arrays[0].shape

    def kernel(scalars, arrays, outs):
        (place,) = scalars
        glow_ref, gp_ref = arrays[:2]
        ubg_ref, weight = outs[4:]
        fill(place, arrays[2:], weight)
        for step in range(4):
            total = jnp.zeros((1, width), f32)
            for at in row_blocks(count):
                grad = (dot(glow_ref[at, :], weight[step]) * up(gp_ref[step, at, :])).astype(bf16)
                outs[step][at, :] = grad
                total = total + jnp.sum(up(grad), axis=0, keepdims=True)
            ubg_ref[step] = total

    outs = [shape((count, width), bf16)] * 4
    outs += [shape((4, 1, width), f32), shape((4, width, width), bf16)]
    return call(kernel, "expanded_backward", scalars, list(arrays) + list(pieces), outs)


def middle_backward(arrays, parts):
    count, width = arrays[0].shape

    def kernel(scalars, arrays, outs):
        mid_ref, glow_ref, norm_ref, weight = arrays[:4]
        mg_ref, ml_ref, sums_ref = outs
        total = jnp.zeros((4, width), f32)
        for at in row_blocks(count):
            two = sum(dot_cols(part[at, :], weight[step]) for step, part in enumerate(arrays[4:]))
            normed, inverse = moments(mid_ref[at, :])
            out_grad = up(glow_ref[at, :])
            grad = out_grad + norm_back(two, normed, inverse, norm_ref[2:3, :])
            mg_ref[at, :] = grad
            ml_ref[at, :] = grad.astype(bf16)
            lines = [two * normed, two, grad, out_grad]
            total = total + join(*[jnp.sum(line, axis=0, keepdims=True) for line in lines])
        sums_ref[...] = total

    outs = [shape((count, width), f32), shape((count, width), bf16), shape((4, width), f32)]
    return call(kernel, "middle_backward", [], list(arrays) + list(parts), outs)


def block_out(arrays, parts):
    count, width = arrays[0].shape

    def kernel(scalars, arrays, outs):
        mid_ref, bias_ref, weight = arrays[:3]
        bias = bias_ref[bias_ref.shape[0] - 1 :, :]
        for at in row_blocks(count):
            total = sum(dot_cols(part[at, :], weight[step]) for step, part in enumerate(arrays[3:]))
            outs[0][at, :] = (mid_ref[at, :] + total + bias).astype(bf16)

    outs = [shape((count, width), bf16)]
    return call(kernel, "block_out", [], list(arrays) + list(parts), outs)[0]


def attention_backward(scalars, arrays):
    count, width = arrays[0].shape
    blocks = count // PAIR

    def kernel(scalars, arrays, outs, da, dq, dk, dv):
        (place,) = scalars
        ml_ref, q_ref, k_ref, v_ref, p_ref, weight = arrays
        lines_ref = outs[4]
        for yr in range(2):
            for at in row_blocks(count):
                ends = []
                for step in (yr, 2 + yr):
                    grad = dot(ml_ref[at, :], weight[step, :, 4 * PAIR :])
                    da[step, at, :] = grad[:, PAIR:].astype(bf16)
                    ends.append(grad[:, 0:PAIR])
                both = jnp.where(low_lanes(ends[0].shape), swap(ends[0]), ends[1])
                da[4 + yr, at, :] = both.astype(bf16)

        low = low_lanes((PAIR, PAIR))
        zero = jnp.zeros((PAIR, PAIR), bf16)
        scale = HEAD ** (-0.5)

        def stack(value):
            return join(jnp.where(low, value, zero), jnp.where(low, zero, value))

        def block(r, _):
            at = pl.ds(pl.multiple_of(r * PAIR, PAIR), PAIR)
            for pair in range(6):
                grad = stack(da[pair, at, :])
                low_probs = p_ref[pair, r]
                probs = up(low_probs)
                probs_grad = dot_cols(grad, v_ref[pair, at, :])
                shared = jnp.sum(probs * probs_grad, axis=1, keepdims=True)
                scores_grad = (probs * (probs_grad - shared)).astype(bf16)
                dv[pair, at, :] = dot_rows(low_probs, grad)
                both = dot(scores_grad, k_ref[pair, at, :])
                dq[pair, at, :] = jnp.where(low, both[0:PAIR], both[PAIR:]) * scale
                dk[pair, at, :] = dot_rows(scores_grad, stack(q_ref[pair, at, :])) * scale
            return 0

        lax.fori_loop(0, blocks, block, 0, unroll=2)
        low_all = low_lanes((count, PAIR))
        low_line = low_lanes((1, PAIR))

        def column_sum(value):
            return jnp.sum(up(value.astype(bf16)), axis=0, keepdims=True)

        for step in range(4):
            pc, yr = step // 2, step % 2
            pair = 4 + yr
            sums = []
            for value in (dq, dv):
                third = column_sum(value[pair])
                third = swap(third) if pc else third
                sums += [column_sum(value[step]), jnp.where(low_line, third, 0.0)]
            sums.append(jnp.zeros((1, width - 4 * PAIR), f32))
            lines_ref[pl.ds(block_of(place, step), 1), :] = jnp.concatenate(sums, axis=1)
            if pc:
                tail3 = jnp.where(low_all, swap(dq[pair]), dk[pair])
                tail4 = jnp.where(low_all, swap(dv[pair]), 0.0)
            else:
                tail3 = jnp.where(low_all, dq[pair], swap(dk[pair]))
                tail4 = jnp.where(low_all, dv[pair], 0.0)
            for i, part in enumerate((dq[step], dk[step], dv[step], tail3, tail4)):
                outs[step][:, i * PAIR : (i + 1) * PAIR] = part.astype(bf16)

    outs = [shape((count, 5 * PAIR), bf16)] * 4 + [shape((4, width), f32)]
    heads = (6, count, PAIR)
    scratch = [pltpu.VMEM(heads, bf16)] + [pltpu.VMEM(heads, f32)] * 3
    return call(kernel, "attention_backward", scalars, arrays, outs, scratch)


def attention_gradient(matrix, order, scalars, lefts, rights, outer_lefts, outer_rights):
    def kernel(scalars, arrays, outs):
        (place,) = scalars
        n1, ml, outer = arrays[0:2], arrays[2:4], arrays[4:6]
        rights = (arrays[6:8], arrays[8:10])
        for yr in range(2):
            first = dot_rows(n1[0][...], rights[0][yr][...])
            first = first + dot_rows(n1[1][...], rights[1][yr][...])
            second = dot_rows(ml[0][...], outer[0][yr]) + dot_rows(ml[1][...], outer[1][yr])
            shared = first[:, 4 * PAIR :] + second[:, 0:PAIR]
            parts = [(0, first[:, 0 : 4 * PAIR]), (4 * PAIR, shared), (5 * PAIR, second[:, PAIR:])]
            matrix.store(place, parts, yr, order, outs[0])

    arrays = list(lefts) + list(outer_lefts) + list(outer_rights) + list(rights[0]) + list(rights[1])
    outs = matrix.grad_shapes(6 * PAIR)
    (grad,) = call(kernel, "attention_gradient", scalars, arrays, outs)
    return matrix.grad_result(grad, order)


def input_backward(scalars, arrays, parts):
    count, width = arrays[0].shape

    def kernel(scalars, arrays, outs):
        (place,) = scalars
        x_ref, mg_ref, norm_ref, weight, sums_ref, ubg_ref, heads_ref = arrays[:7]
        out_ref, lines_ref = outs
        total = jnp.zeros((2, width), f32)
        for at in row_blocks(count):
            one = sum(
                dot_cols(part[at, :], weight[step, :, 0 : 5 * PAIR])
                for step, part in enumerate(arrays[7:])
            )
            normed, inverse = moments(up(x_ref[at, :]))
            out_ref[at, :] = mg_ref[at, :] + norm_back(one, normed, inverse, norm_ref[0:1, :])
            lines = [jnp.sum(one * normed, axis=0, keepdims=True), jnp.sum(one, axis=0, keepdims=True)]
            total = total + join(*lines)
        lines_ref[0:8, :] = join(total, sums_ref[...], jnp.zeros((2, width), f32))
        for step in range(4):
            lines_ref[pl.ds(8 + block_of(place, step), 1), :] = ubg_ref[step]
        lines_ref[12:16, :] = heads_ref[...]

    outs = [shape((count, width), f32), shape((16, width), f32)]
    return call(kernel, "input_backward", scalars, list(arrays) + list(parts), outs)


def adam_step(weight, first, second, grad, rate, decay):
    first_new = beta_first * first + (1.0 - beta_first) * grad
    second_new = beta_second * second + (1.0 - beta_second) * grad * grad
    first_hat = first_new / (1.0 - beta_first**STEP)
    second_hat = second_new / (1.0 - beta_second**STEP)
    weight_new = weight - rate * (first_hat / (jnp.sqrt(second_hat) + adam_eps) + decay * weight)
    return (weight_new, first_new, second_new)


def pack_tiles(parts):
    q, k, v, o = ((part[:, :PAIR], part[:, PAIR:]) for part in parts)
    tail3 = jnp.concatenate([q[1], k[1]], axis=1)
    tail4 = jnp.concatenate([v[1], o[1]], axis=1)
    return q[0], k[0], v[0], tail3, tail4, o[0]


def own_columns(plan, place, value):
    width = value.shape[1]
    columns = width // math.prod(plan.dims)
    group = (place[0] * plan.dims[1] + place[1]) * 4 + rank_of(place)
    turn = lax.rem(width - group * columns, width)
    return pltpu.roll(value, turn, axis=1)[:, 0:columns]


def hold(plan, scalars, params, matrices):
    rows, cols = matrices[2][0].shape
    width = params[0].shape[1]
    columns = width // math.prod(plan.dims)

    def kernel(scalars, state, outs, small_ref):
        for t in range(3):
            parts = [state[t][i] for i in range(3)] + [state[3 + t][...]]
            for i, part in enumerate(pack_tiles(parts)):
                outs[0][t, :, i * PAIR : (i + 1) * PAIR] = part
            outs[0][3 + t] = state[6 + t][...]
            outs[0][6 + t] = state[9 + t][...]
        small_ref[0:8, :] = state[13][...]
        small_ref[8:12, :] = state[12][...]
        small_ref[12:16, :] = state[12][...]
        own = own_columns(plan, scalars[0], small_ref[...])
        outs[1][...] = own[8:12]
        outs[2][...] = own[0:8]

    outs = [shape((9, rows, cols), f32), shape((4, columns), f32), shape((8, columns), f32)]
    state = [value for group in matrices for value in group] + list(params)
    return call(kernel, "hold", scalars, [], outs, [pltpu.VMEM((16, width), f32)], 12, state)


def total_gradients(plan, scalars, parts, lines):
    rows, cols = parts[0][0].shape[1:]
    width = lines[0].shape[2]
    devices = math.prod(plan.dims)
    columns = width // devices
    counts = [len(part) for part in parts]
    held = sum(counts)

    def kernel(scalars, arrays, outs, small_ref):
        at, squares = 0, jnp.zeros((1, 1), f32)

        def square(value):
            return jnp.sum(jnp.sum(value * value, axis=1, keepdims=True), axis=0, keepdims=True)

        for m, n in enumerate(counts):
            total = up(arrays[at][0])
            for i in range(1, n):
                total = total + up(arrays[at + i][0])
            outs[0][m] = total
            squares = squares + square(total)
            at += n
        sums = arrays[held][0]
        for ref in arrays[held + 1 :]:
            sums = sums + ref[0]
        size = width // 4
        small_ref[0:4, :] = sums[0:4]
        small_ref[4:8, :] = sums[8:12]
        for t in range(2):
            for mp in range(4):
                line = sums[12 + mp : 13 + mp, 2 * PAIR * t : 2 * PAIR * t + size]
                small_ref[8 + t : 9 + t, mp * size : (mp + 1) * size] = line
        small_ref[10:12, :] = sums[4:6]
        small_ref[12:16, :] = jnp.zeros((4, width), f32)
        own = own_columns(plan, scalars[0], small_ref[...])
        squares = squares + square(own)
        outs[1][...] = jnp.broadcast_to(squares[None], (devices, 1, 1))
        outs[2][...] = own[0:4]
        outs[3][...] = own[4:12]

    arrays = [part for group in parts for part in group] + list(lines)
    outs = [shape((3, rows, cols), f32), shape((devices, 1, 1), f32)]
    outs += [shape((n, columns), f32) for n in (4, 8)]
    scratch = [pltpu.VMEM((16, width), f32)]
    return call(kernel, "total_gradients", scalars, arrays, outs, scratch, 12)


def update(squares, grads, state, small, smalls, shapes):
    def kernel(scalars, arrays, outs):
        norm = jnp.sqrt(jnp.sum(arrays[0][...], axis=0))
        factor = jnp.minimum(1.0, clip_limit / (norm + 1e-06))
        outs[0][...] = norm
        grad_ref, state_ref = arrays[1:3]

        def step(weight, first, second, grad, rate, decay):
            grad = grad * factor
            new, first, second = adam_step(weight, first, second, grad, rate, decay)
            return [grad, new, first, second, new.astype(bf16)]

        for m in range(3):
            values = [state_ref[3 * m + t] for t in range(3)] + [grad_ref[m]]
            values = step(*values, matrix_rate, matrix_decay)
            for i, value in enumerate(values):
                if m:
                    outs[6 + 5 * m + i][...] = value
                    continue
                tiles = [value[:, t * PAIR : (t + 1) * PAIR] for t in range(6)]
                wide = [tiles[3], tiles[4]] if value.dtype == f32 else [up(t) for t in tiles[3:5]]
                tails = [part for t in wide for part in (t, swap(t))]
                for t in range(4):
                    ref = outs[1 + i] if t < 3 else outs[6 + i]
                    head = tiles[t] if t < 3 else tiles[5]
                    tail = tails[t][:, :HEAD].astype(value.dtype)
                    if t < 3:
                        ref[t, :, :PAIR] = head
                        ref[t, :, PAIR:] = tail
                    else:
                        ref[:, :PAIR] = head
                        ref[:, PAIR:] = tail
        for m in range(2):
            weight, first, second = (ref[...] for ref in arrays[5 + 3 * m : 8 + 3 * m])
            values = step(weight, first, second, arrays[3 + m][...], small_rate, 0.0)
            for i in range(4):
                outs[21 + 4 * m + i][...] = values[i]

    arrays = [squares, grads, state] + list(small)
    outs = [shape((1, 1), f32)]
    for dims in shapes:
        outs += [shape(dims, f32)] * 4 + [shape(dims, bf16)]
    for group in smalls:
        arrays += list(group)
        outs += [shape(group[0].shape, f32)] * 4
    return call(kernel, "update", [], arrays, outs)


def body(
    plan,
    block_input,
    cotangent,
    lengths,
    attn_input,
    attn_input_first,
    attn_input_second,
    attn_output,
    attn_output_first,
    attn_output_second,
    mlp_up,
    mlp_up_first,
    mlp_up_second,
    mlp_down,
    mlp_down_first,
    mlp_down_second,
    norm_params,
    norm_first,
    norm_second,
    bias_params,
    bias_first,
    bias_second,
):
    width = norm_params.shape[1]
    place = jnp.stack([lax.axis_index(axis) for axis in AXES]).astype(jnp.int32)
    matrix = Matrix(plan, place, width, attn_input.shape[0])
    send, send_z = plan.send, plan.send_z
    az, za = plan.order_az, plan.order_za
    low_bits, high_bits = plan.zbits[:2], plan.zbits[2:]
    def turned(value):
        return value.transpose(1, 0, 2)

    attn = pack_attention(turned(attn_input), attn_output)
    attn_z = [send_z(attn, mask) for mask in (1, 2, 3)]
    above, down = pack_mlp(mlp_up, mlp_down)
    above_z = send_z(above, 1)
    down_a = send(down, plan.a)
    n1, grad_low, head_bias = prepare(
        [place, lengths], [block_input, cotangent, norm_params, bias_params]
    )
    attn, *attn_z, above, above_z, down, down_a, n1, grad_low, head_bias = sync(
        attn, *attn_z, above, above_z, down, down_a, n1, grad_low, head_bias
    )

    attn, above, down = joined(
        "join_one", matrix, [attn, *attn_z], [above, above_z], [down, down_a]
    )
    attn = plan.spread(attn, high_bits)
    attn_a, attn_b = send(attn, plan.a), send(attn, plan.b)
    above_z = send_z(above, 2)
    attn_c = [send(attn, plan.core)]
    attn, attn_a, attn_b, above, above_z, down, *attn_c = sync(
        attn, attn_a, attn_b, above, above_z, down, *attn_c
    )

    def blocks(planes, order, *fixed):
        return [
            (array, plan.slots(pc, order, **what))
            for pc, arrays in enumerate(planes)
            for array, what in zip(arrays, fixed)
        ]

    corners = [dict(br=0, ar=0), dict(br=0, ar=1), dict(br=1, ar=0), dict(br=1, ar=1)]
    (above,) = joined("join_two", matrix, [above, above_z])
    above = plan.spread(above, high_bits)
    attn_ab = send(attn_a, plan.b)
    above_a = send(above, plan.a)
    down_z = send_z(down, 2)
    attn_c += [send(attn_a, plan.core), send(attn_b, plan.core)]
    attn_ab, above, above_a, down, down_z, *attn_c[1:] = sync(
        attn_ab, above, above_a, down, down_z, *attn_c[1:]
    )

    (down,) = joined("join_three", matrix, [down, down_z])
    above_b = send(above, plan.b)
    above_ab = send(above_a, plan.b)
    down_z = send_z(down, 1)
    above_c = [send(piece, plan.core) for piece in (above, above_a)]
    attn_c.append(send(attn_ab, plan.core))
    pieces = blocks([[attn, attn_a, attn_b, attn_ab], attn_c], plan.plain, *corners)
    pieces, fill = matrix.weight_args(pieces)
    q, k, v, weight_attn = project([place], [n1, head_bias], pieces, fill)
    probs, att_own, att_other, middle, n2 = attend(
        [place, lengths], [block_input, norm_params, bias_params, q, k, v, weight_attn]
    )
    above, above_a, above_b, above_ab, down, down_z, att_other, n2, *above_c = sync(
        above, above_a, above_b, above_ab, down, down_z, att_other, n2, *above_c
    )

    (down,) = joined("join_four", matrix, [down, down_z])
    down = plan.spread(down, high_bits)
    down_b = send(down, plan.b)
    above_c += [send(piece, plan.core) for piece in (above_b, above_ab)]
    pieces = blocks([[above, above_a, above_b, above_ab], above_c], plan.plain, *corners)
    pieces, fill = matrix.weight_args(pieces)
    *hidden, slope, weight_up = mlp_forward([place], [n2, bias_params], pieces, fill)
    n2_c, att_c = send(n2, plan.core), send(att_other, plan.core)
    grad_low_c = send(grad_low, plan.core)
    down_c = [send(down, plan.core)]
    hidden_c = [send(part, plan.core) for part in hidden[2:]]
    down_b, n2_c, att_c, grad_low_c, down_c[0], *hidden_c = sync(
        down_b, n2_c, att_c, grad_low_c, down_c[0], *hidden_c
    )

    down_c.append(send(down_b, plan.core))
    down_g = gradient(
        matrix, za, "down_gradient", [place], [grad_low, grad_low_c], [hidden[:2], hidden_c]
    )
    pieces = blocks([[down, down_b], down_c], za, dict(br=0), dict(br=1))
    pieces, fill = matrix.weight_args(pieces)
    down_g, *pieces = sync(down_g, *pieces)

    half = down_g.shape[0] // 2
    down_gb = send(down_g[half:], plan.b)
    *grads, up_bias_grad, weight_down = expanded_backward(
        [place], [grad_low, slope], pieces, fill
    )
    grads_c = [send(part, plan.core) for part in grads[2:]]
    middle_grad, middle_low, sums_two = middle_backward(
        [middle, grad_low, norm_params, weight_up], grads
    )
    up_g = gradient(matrix, az, "up_gradient", [place], [n2, n2_c], [grads[:2], grads_c])
    block_output = block_out([middle, bias_params, weight_down], hidden)
    up_g, block_output, down_gb, middle_low = sync(up_g, block_output, down_gb, middle_low)

    up_gb = send(up_g[half:], plan.b)
    terms = [down_g, down_gb]
    if high_bits:
        terms = [plan.fold(up(down_g[:half]) + up(down_gb), high_bits)]
    down_s, down_0 = added(
        "add_one",
        matrix,
        (4, f32, [(part, 0) for part in terms]),
        (4, bf16, [(part, 4) for part in terms]),
    )
    down_s, down_0, middle_low = sync(down_s, down_0, middle_low)

    down_z = send_z(down_0, 1)
    *joint, head_lines = attention_backward(
        [place], [middle_low, q, k, v, probs, weight_attn]
    )
    input_grad, lines = input_backward(
        [place],
        [block_input, middle_grad, norm_params, weight_attn, sums_two, up_bias_grad, head_lines],
        joint,
    )
    lines = lines[None]
    input_grad, lines, up_gb, down_z, *joint = sync(input_grad, lines, up_gb, down_z, *joint)

    fourth = half // 2
    up_0, down_s, down_0, down_1 = added(
        "add_two",
        matrix,
        (fourth, bf16, [(up_g, fourth), (up_gb, fourth)]),
        (2, f32, [(down_s, 0), (down_z, 0)]),
        (1, bf16, [(down_s, 2), (down_z, 2)]),
        (1, bf16, [(down_s, 3), (down_z, 3)]),
    )
    up_ga = send(up_0, plan.a)
    down_z0 = send_z(down_0, 2)
    lines_z = send_z(lines, 1)
    joint_c = [send(part, plan.core) for part in joint[2:]]
    middle_low_c, n1_c = send(middle_low, plan.core), send(n1, plan.core)
    attn_g = attention_gradient(
        matrix, az, [place], [n1, n1_c], [joint[:2], joint_c],
        [middle_low, middle_low_c], [att_own, att_c],
    )
    attn_g, up_ga, down_z0, lines_z = sync(attn_g, up_ga, down_z0, lines_z)

    attn_gb = send(attn_g[half:], plan.b)
    terms = [up_g, up_gb, up_ga]
    if high_bits:
        terms = [plan.fold(sum(up(part[:fourth]) for part in terms), high_bits)]
    up_s, up_0, lines = added(
        "add_three",
        matrix,
        (2, f32, [(part, 0) for part in terms]),
        (2, bf16, [(part, 2) for part in terms]),
        (1, f32, [(lines, 0), (lines_z, 0)]),
    )
    up_z = send_z(up_0, 1)
    down_z1 = send_z(down_1, 2)
    lines_a = send(lines, plan.a)
    attn_gb, down_z1, up_z, lines_a = sync(attn_gb, down_z1, up_z, lines_a)

    attn_0, down_s, down_0, up_s, up_0, lines = added(
        "add_four",
        matrix,
        (fourth, bf16, [(attn_g, fourth), (attn_gb, fourth)]),
        (1, f32, [(down_s, 0), (down_z0, 0)]),
        (1, bf16, [(down_s, 1), (down_z1, 0)]),
        (1, f32, [(up_s, 0), (up_z, 0)]),
        (1, bf16, [(up_s, 1), (up_z, 1)]),
        (1, f32, [(lines, 0), (lines_a, 0)]),
    )
    attn_ga = send(attn_0, plan.a)
    up_z = send_z(up_0, 2)
    lines_z = send_z(lines, 2)
    for bit in high_bits:
        lines = lines + lines_z
        lines_z = send_z(lines, bit)
    attn_ga, up_z, lines_z, down_0 = sync(attn_ga, up_z, lines_z, down_0)

    terms = [attn_g, attn_gb, attn_ga]
    if high_bits:
        terms = [plan.fold(sum(up(part[:fourth]) for part in terms), high_bits)]
    attn_s, *attn_0, lines = added(
        "add_five",
        matrix,
        (1, f32, [(part, 0) for part in terms]),
        (1, bf16, [(part, 1) for part in terms]),
        (1, bf16, [(part, 2) for part in terms]),
        (1, bf16, [(part, 3) for part in terms]),
        (1, f32, [(lines, 0), (lines_z, 0)]),
    )
    attn_z = [send_z(part, mask) for part, mask in zip(attn_0, (2, 1, 3))]
    matrices = (
        (turned(attn_input), turned(attn_input_first), turned(attn_input_second)),
        (attn_output, attn_output_first, attn_output_second),
        (mlp_up, mlp_up_first, mlp_up_second),
        (mlp_down, mlp_down_first, mlp_down_second),
    )
    state, own_norm, own_bias = hold(plan, [place], [norm_params, bias_params], matrices)
    down_ga = send(down_0, plan.a)
    rest = [send(lines, perm) for perm in (plan.b, plan.core, plan.cross)]
    state, down_ga, *rest = sync(state, down_ga, *rest, *attn_z)
    rest, attn_z = rest[:3], rest[3:]

    sums, squares, norm_sum, bias_sum = total_gradients(
        plan, [place], [[attn_s, *attn_z], [up_s, up_z], [down_s, down_ga]], [lines, *rest]
    )
    squares = lax.all_to_all(squares, AXES, 0, 0, tiled=True)
    grad_norm, *results = update(
        squares,
        sums,
        state,
        [norm_sum, bias_sum],
        ((own_norm, norm_first, norm_second), (own_bias, bias_first, bias_second)),
        [group[0].shape for group in matrices],
    )
    results[:5] = [turned(value) for value in results[:5]]
    return (block_output, input_grad, grad_norm[0, 0], *results)


def solution(mesh):
    dp, mp = mesh.shape["dp"], mesh.shape["mp"]
    dims = (dp // 2, 2, mp // 2, 2)
    fine = Mesh(np.asarray(mesh.devices).reshape(dims), AXES)
    plan = Plan(dims)
    d, m = ("z", "x"), ("y", "c")
    every = d + m
    rows = P(every, None)
    cube = P(d, None, m)
    flat = P(d, m)
    small = P(None, every)
    return jax.shard_map(
        functools.partial(body, plan),
        mesh=fine,
        in_specs=(rows, rows, P(d)) + (cube,) * 3 + (flat,) * 9 + (P(), small, small) * 2,
        out_specs=(rows, rows, P()) + (cube,) * 5 + (flat,) * 15 + (small,) * 8,
        check_vma=False,
    )
```

```python
import functools
import math

import jax
import jax.numpy as jnp
import numpy as np
from jax import lax
from jax.experimental import pallas as pl
from jax.experimental.pallas import tpu as pltpu
from jax.sharding import Mesh, PartitionSpec as P

HEAD = 64
STEP = 10

norm_eps = 1e-06
beta_first = 0.5
beta_second = 0.5
adam_eps = 1e-08
matrix_rate = 0.03
small_rate = 0.3
matrix_decay = 0.01
clip_limit = 1.0
masked_score = -1e30

f32 = jnp.float32
bf16 = jnp.bfloat16
AXES = ("z", "x", "y", "c")
PAIR = 2 * HEAD
GELU_A = math.sqrt(2.0 / math.pi)
GELU_B = 0.044715


def sync(*values):
    return lax.optimization_barrier(values)


def up(value):
    return value.astype(f32)


def join(*values):
    return jnp.concatenate(values, axis=0)


class Plan:
    def __init__(self, dims):
        self.dims = dims
        self.z = dims[0]
        self.zbits = [1 << i for i in range(int(math.log2(self.z)))]
        self.places = [tuple(p) for p in np.ndindex(*dims)]
        self.index = {p: i for i, p in enumerate(self.places)}
        self.core = self.perm(lambda z, x, y, c: (z, x, y, 1 - c))
        self.a = self.perm(lambda z, x, y, c: (z, x ^ (1 - c), y ^ c, c))
        self.b = self.perm(lambda z, x, y, c: (z, x ^ c, y ^ (1 - c), c))
        self.cross = self.perm(lambda z, x, y, c: (z, x ^ c, y ^ (1 - c), 1 - c))
        each = [(br, ar) for br in range(2) for ar in range(2)]
        turned = sorted(range(self.z), key=self.turn)
        self.plain = [(br, ar, zr) for br, ar in each for zr in range(self.z)]
        self.order_az = [(br, ar, zr) for br, ar in each for zr in turned]
        self.order_za = [(br, ar, zr) for br in range(2) for zr in turned for ar in range(2)]

    def turn(self, zr):
        return (zr >> 2) * 4 + (zr & 1) * 2 + ((zr >> 1) & 1)

    def perm(self, move):
        return [(self.index[p], self.index[move(*p)]) for p in self.places]

    def zmove(self, mask):
        return self.perm(lambda z, x, y, c: (z ^ mask, x, y, c))

    def send(self, value, perm):
        return lax.ppermute(value, AXES, perm)

    def send_z(self, value, mask):
        return self.send(value, self.zmove(mask))

    def spread(self, block, bits):
        for bit in bits:
            block = join(block, self.send_z(block, bit))
        return block

    def fold(self, total, bits):
        for bit in bits[::-1]:
            half = total.shape[0] // 2
            total = total[:half] + up(self.send_z(total[half:].astype(bf16), bit))
        return total

    def table(self, place, slots):
        pc, br, ar, zr = (jnp.asarray(v, jnp.int32) for v in zip(*slots))
        core = place[3] ^ pc
        x = place[1] ^ jnp.where(core == 0, ar, br)
        yr = jnp.where(core == 0, br, ar)
        dp = (place[0] ^ zr) * self.dims[1] + x
        return (2 * pc + yr) * (self.z * self.dims[1]) + dp

    def slots(self, pc, order, **fixed):
        names = ("br", "ar", "zr")
        return [
            (pc,) + slot
            for slot in order
            if all(slot[names.index(name)] == value for name, value in fixed.items())
        ]


def dot(left, right):
    return lax.dot_general(left, right, (((1,), (0,)), ((), ())), preferred_element_type=f32)


def dot_cols(left, right):
    return lax.dot_general(left, right, (((1,), (1,)), ((), ())), preferred_element_type=f32)


def dot_rows(left, right):
    return lax.dot_general(left, right, (((0,), (0,)), ((), ())), preferred_element_type=f32)


def low_lanes(shape):
    return lax.broadcasted_iota(jnp.int32, shape, len(shape) - 1) < HEAD


def swap(value):
    return pltpu.roll(value, HEAD, axis=1)


def moments(rows):
    center = jnp.mean(rows, axis=1, keepdims=True)
    centered = rows - center
    spread = jnp.mean(centered * centered, axis=1, keepdims=True)
    inverse = lax.rsqrt(spread + norm_eps)
    return centered * inverse, inverse


def norm_back(grad_rows, normed, inverse, gain):
    scaled = grad_rows * gain
    return inverse * (
        scaled
        - jnp.mean(scaled, axis=1, keepdims=True)
        - normed * jnp.mean(scaled * normed, axis=1, keepdims=True)
    )


class Matrix:
    def __init__(self, plan, place, width, rows):
        self.plan = plan
        self.place = place
        self.width = width
        self.rows = rows
        self.direct = rows % 16 == 0
        self.blocks_dp = plan.dims[0] * plan.dims[1]

    def whole(self, pieces):
        order = [slot for _, slots in pieces for slot in slots]
        blocks = join(*[array for array, _ in pieces])
        turn = jnp.argsort(self.plan.table(self.place, order))
        return jnp.take(blocks, turn, axis=0).reshape(4, self.width, blocks.shape[-1])

    def place_blocks(self, place, refs, slots, weight):
        for ref, of_ref in zip(refs, slots):
            for i, (pc, br, ar, zr) in enumerate(of_ref):
                core = place[3] ^ pc
                xr = jnp.where(core == 0, ar, br)
                yr = jnp.where(core == 0, br, ar)
                dp = (place[0] ^ zr) * self.plan.dims[1] + (place[1] ^ xr)
                row = pl.multiple_of(dp * self.rows, 16)
                weight[2 * pc + yr, pl.ds(row, self.rows), :] = ref[i]

    def weight_args(self, pieces):
        if self.direct:
            slots = [of for _, of in pieces]
            return [array for array, _ in pieces], functools.partial(self.fill, slots)
        return [self.whole(pieces)], lambda place, refs, weight: self.copy(refs, weight)

    def fill(self, slots, place, refs, weight):
        self.place_blocks(place, refs, slots, weight)

    def copy(self, refs, weight):
        weight[...] = refs[0][...]

    def grad_shapes(self, cols):
        if self.direct:
            return [jax.ShapeDtypeStruct((4 * self.plan.z, self.rows, cols), bf16)]
        return [jax.ShapeDtypeStruct((2, self.width, cols), bf16)]

    def store(self, place, parts, yr, order, out):
        if not self.direct:
            for at, part in parts:
                out[yr, :, at : at + part.shape[1]] = part.astype(bf16)
            return
        z = self.plan.z
        core = place[3]
        for dp in range(self.blocks_dp):
            zr = place[0] ^ (dp // self.plan.dims[1])
            xr = place[1] ^ (dp % self.plan.dims[1])
            ar = jnp.where(core == 0, xr, yr)
            br = jnp.where(core == 0, yr, xr)
            zi = self.plan.turn(zr)
            if order is self.plan.order_az:
                slot = br * (2 * z) + ar * z + zi
            else:
                slot = br * (2 * z) + zi * 2 + ar
            rows = slice(dp * self.rows, (dp + 1) * self.rows)
            for at, part in parts:
                out[slot, :, at : at + part.shape[1]] = part[rows, :].astype(bf16)

    def grad_result(self, grad, order):
        if self.direct:
            return grad
        whole = grad.reshape(2 * self.blocks_dp, self.rows, grad.shape[-1])
        table = self.plan.table(self.place, [(0,) + slot for slot in order])
        return jnp.take(whole, table, axis=0)


def call(kernel, name, scalars, arrays, outs, scratch=(), mib=16, hbm=(), micros=0):
    scalars, arrays, outs = list(scalars), list(arrays), list(outs)
    hbm = [pltpu.with_memory_space_constraint(part, pltpu.HBM) for part in hbm]
    counts = (len(scalars), len(arrays), len(hbm), len(outs), len(hbm), min(len(hbm), 1))

    def split(*refs):
        parts, at = [], 0
        for n in counts:
            parts.append(list(refs[at : at + n]))
            at += n
        copies = [
            pltpu.make_async_copy(source, target, parts[5][0].at[i])
            for i, (source, target) in enumerate(zip(parts[2], parts[4]))
        ]
        for copy in copies:
            copy.start()
        for copy in copies:
            copy.wait()
        kernel(parts[0], parts[1] + parts[4], parts[3], *refs[at:])

    vmem = pl.BlockSpec(memory_space=pltpu.VMEM)
    specs = [pl.BlockSpec(memory_space=pltpu.SMEM)] * len(scalars) + [vmem] * len(arrays)
    specs += [pl.BlockSpec(memory_space=pltpu.HBM)] * len(hbm)
    own = [pltpu.VMEM(part.shape, part.dtype) for part in hbm]
    if hbm:
        own.append(pltpu.SemaphoreType.DMA((len(hbm),)))
    return pl.pallas_call(
        split,
        name=name,
        out_shape=outs,
        in_specs=specs,
        out_specs=[vmem] * len(outs),
        scratch_shapes=own + list(scratch),
        compiler_params=pltpu.CompilerParams(vmem_limit_bytes=mib * 2**20),
        cost_estimate=pl.CostEstimate(
            flops=1 + int(micros * 1.15e9), bytes_accessed=1, transcendentals=0
        ),
    )(*scalars, *arrays, *hbm)


def shape(dims, kind):
    return jax.ShapeDtypeStruct(tuple(dims), kind)


def rank_of(place):
    return place[2] * 2 + place[3]


def block_of(place, step):
    return rank_of(place) ^ (2 * (step % 2) + step // 2)


def row_blocks(count):
    size = 256 if count % 256 == 0 else count
    return [slice(r, r + size) for r in range(0, count, size)]


def joined(name, matrix, *groups, micros=0):
    if not matrix.direct:
        return [join(*group) for group in groups]

    def kernel(scalars, arrays, outs):
        at = 0
        for group, out in zip(groups, outs):
            row = 0
            for _ in group:
                for i in range(arrays[at].shape[0]):
                    out[row] = arrays[at][i]
                    row += 1
                at += 1

    outs = []
    for group in groups:
        rows = sum(part.shape[0] for part in group)
        outs.append(shape((rows,) + group[0].shape[1:], group[0].dtype))
    arrays = [part for group in groups for part in group]
    return call(kernel, name, [], arrays, outs, mib=8, micros=micros)


def added(name, matrix, *sums, micros=0):
    sums = [each if isinstance(each, list) else [each] for each in sums]
    if not matrix.direct:
        return [
            join(*[
                sum(up(part[at : at + count]) for part, at in terms).astype(kind)
                for count, kind, terms in each
            ])
            for each in sums
        ]
    arrays = []
    for each in sums:
        for _, _, terms in each:
            for part, _ in terms:
                if not any(part is other for other in arrays):
                    arrays.append(part)

    def where(part):
        return next(i for i, other in enumerate(arrays) if part is other)

    def kernel(scalars, refs, outs):
        for each, out in zip(sums, outs):
            row = 0
            for count, kind, terms in each:
                for i in range(count):
                    total = up(refs[where(terms[0][0])][terms[0][1] + i])
                    for part, at in terms[1:]:
                        total = total + up(refs[where(part)][at + i])
                    out[row] = total.astype(kind)
                    row += 1

    outs = [
        shape((sum(one[0] for one in each),) + each[0][2][0][0].shape[1:], each[0][1])
        for each in sums
    ]
    return call(kernel, name, [], arrays, outs, mib=8, micros=micros)


def pack_attention(inputs, output):
    rows = output.shape[0]

    def kernel(scalars, arrays, outs):
        in_ref, out_ref = arrays
        parts = [in_ref[t].astype(bf16) for t in range(3)] + [out_ref[...].astype(bf16)]
        for i, part in enumerate(pack_tiles(parts)):
            outs[0][0, :, i * PAIR : (i + 1) * PAIR] = part

    outs = [shape((1, rows, 6 * PAIR), bf16)]
    return call(kernel, "pack_attention", [], [], outs, mib=8, hbm=[inputs, output])[0]


def pack_mlp(above, down):
    def kernel(scalars, arrays, outs):
        for ref, out in zip(arrays, outs):
            out[0] = ref[...].astype(bf16)

    outs = [shape((1,) + above.shape, bf16)] * 2
    return call(kernel, "pack_mlp", [], [], outs, mib=8, hbm=[above, down])


def prepare(scalars, hbm):
    count, width = hbm[0].shape
    units = hbm[3].shape[0] - 4

    def kernel(scalars, arrays, outs):
        place, lens = scalars
        x_ref, cot_ref, norm_ref, bias_ref = arrays
        n1_ref, glow_ref, head_ref = outs
        size = width // 4
        for t in range(2):
            for mp in range(4):
                line = bias_ref[units + t : units + t + 1, mp * size : (mp + 1) * size]
                head_ref[4 * t + mp : 4 * t + mp + 1, 0:size] = line
        gain1, shift1 = norm_ref[0:1, :], norm_ref[1:2, :]
        for at in row_blocks(count):
            normed, _ = moments(up(x_ref[at, :]))
            n1_ref[at, :] = (normed * gain1 + shift1).astype(bf16)
        captions = lens.shape[0] // 4
        length = count // captions
        for j in range(captions):
            at = slice(j * length, (j + 1) * length)
            limit = lens[rank_of(place) * captions + j]
            keep = lax.broadcasted_iota(jnp.int32, (length, width), 0) < limit
            glow_ref[at, :] = jnp.where(keep, up(cot_ref[at, :]), 0.0).astype(bf16)

    outs = [shape((count, width), bf16)] * 2 + [shape((8, 2 * PAIR), f32)]
    return call(kernel, "prepare", scalars, [], outs, hbm=hbm)


def project(scalars, arrays, pieces, fill):
    count, width = arrays[0].shape

    def kernel(scalars, arrays, outs):
        (place,) = scalars
        n1_ref, head_bias = arrays[:2]
        q_ref, k_ref, v_ref, weight = outs
        fill(place, arrays[2:], weight)
        bias = []
        for step in range(4):
            mp = block_of(place, step)
            bias.append((head_bias[pl.ds(mp, 1), :], head_bias[pl.ds(mp + 4, 1), :]))
        low_line = low_lanes((1, PAIR))
        for yr in range(2):
            pair = 4 + yr
            third = [
                jnp.where(low_line, bias[yr][t][:, PAIR:], swap(bias[2 + yr][t][:, PAIR:]))
                for t in range(2)
            ]
            for at in row_blocks(count):
                joined = []
                for step in (yr, 2 + yr):
                    part = dot(n1_ref[at, :], weight[step, :, 0 : 5 * PAIR])
                    query_bias, value_bias = bias[step]
                    q_ref[step, at, :] = (part[:, 0:PAIR] + query_bias[:, :PAIR]).astype(bf16)
                    k_ref[step, at, :] = part[:, PAIR : 2 * PAIR].astype(bf16)
                    v_ref[step, at, :] = (part[:, 2 * PAIR : 3 * PAIR] + value_bias[:, :PAIR]).astype(bf16)
                    joined.append((part[:, 3 * PAIR : 4 * PAIR], part[:, 4 * PAIR :]))
                (own3, own4), (other3, other4) = joined
                low = low_lanes(own3.shape)
                query = jnp.where(low, own3, swap(other3)) + third[0]
                value = jnp.where(low, own4, swap(other4)) + third[1]
                q_ref[pair, at, :] = query.astype(bf16)
                k_ref[pair, at, :] = jnp.where(low, swap(own3), other3).astype(bf16)
                v_ref[pair, at, :] = value.astype(bf16)

    heads = shape((6, count, PAIR), bf16)
    outs = [heads, heads, heads, shape((4, width, 6 * PAIR), bf16)]
    return call(kernel, "project", scalars, list(arrays) + list(pieces), outs)


def attend(scalars, arrays):
    count, width = arrays[0].shape
    blocks = count // PAIR

    def kernel(scalars, arrays, outs, att):
        place, lens = scalars
        x_ref, norm_ref, bias_ref, q_ref, k_ref, v_ref, weight = arrays
        p_ref, own_ref, other_ref, mid_ref, n2_ref = outs
        first = rank_of(place) * (2 * blocks)
        lane = lax.broadcasted_iota(jnp.int32, (2 * PAIR, PAIR), 1)
        line = lax.broadcasted_iota(jnp.int32, (2 * PAIR, PAIR), 0)
        same = ((line // HEAD) % 2) == (lane // HEAD)
        low = low_lanes((PAIR, PAIR))
        zero = jnp.zeros((PAIR, PAIR), bf16)

        def block(r, _):
            at = pl.ds(pl.multiple_of(r * PAIR, PAIR), PAIR)
            limit = jnp.where(lane < HEAD, lens[first + 2 * r], lens[first + 2 * r + 1] + HEAD)
            keep = same & (lane < limit)
            for pair in range(6):
                query = q_ref[pair, at, :]
                stacked = join(jnp.where(low, query, zero), jnp.where(low, zero, query))
                scores = dot_cols(stacked, k_ref[pair, at, :]) * (HEAD ** (-0.5))
                scores = jnp.where(keep, scores, masked_score)
                expo = jnp.exp(scores - jnp.max(scores, axis=1, keepdims=True))
                probs = (expo / jnp.sum(expo, axis=1, keepdims=True)).astype(bf16)
                p_ref[pair, r] = probs
                out = dot(probs, v_ref[pair, at, :])
                att[pair, at, :] = jnp.where(low, out[0:PAIR], out[PAIR:])
            return 0

        lax.fori_loop(0, blocks, block, 0, unroll=2)
        low_all = low_lanes((count, PAIR))
        for step in range(4):
            pc, yr = step // 2, step % 2
            part_ref = (own_ref, other_ref)[pc]
            third = att[4 + yr] if pc else swap(att[4 + yr])
            part_ref[yr, :, 0:PAIR] = jnp.where(low_all, 0.0, third).astype(bf16)
            part_ref[yr, :, PAIR:] = att[step].astype(bf16)
        out_bias = bias_ref[bias_ref.shape[0] - 2 : bias_ref.shape[0] - 1, :]
        gain2, shift2 = norm_ref[2:3, :], norm_ref[3:4, :]
        for at in row_blocks(count):
            branch = up(x_ref[at, :]) + out_bias
            for step in range(4):
                part_ref = (own_ref, other_ref)[step // 2]
                branch = branch + dot_cols(part_ref[step % 2, at, :], weight[step, :, 4 * PAIR :])
            mid_ref[at, :] = branch
            normed, _ = moments(branch)
            n2_ref[at, :] = (normed * gain2 + shift2).astype(bf16)

    part = shape((2, count, 2 * PAIR), bf16)
    outs = [
        shape((6, blocks, 2 * PAIR, PAIR), bf16),
        part,
        part,
        shape((count, width), f32),
        shape((count, width), bf16),
    ]
    return call(kernel, "attend", scalars, arrays, outs, [pltpu.VMEM((6, count, PAIR), f32)])


def mlp_forward(scalars, arrays, pieces, fill):
    count, width = arrays[0].shape

    def kernel(scalars, arrays, outs):
        (place,) = scalars
        n2_ref, bias_ref = arrays[:2]
        gp_ref, weight = outs[4:]
        fill(place, arrays[2:], weight)
        for step in range(4):
            bias = bias_ref[pl.ds(block_of(place, step), 1), :]
            for at in row_blocks(count):
                value = dot(n2_ref[at, :], weight[step]) + bias
                square = value * value
                t = jnp.tanh((GELU_A * value) * (1.0 + GELU_B * square))
                half = 0.5 * (1.0 + t)
                outs[step][at, :] = (value * half).astype(bf16)
                slope = half + (0.5 * GELU_A) * value * (1.0 - t * t) * (1.0 + (3.0 * GELU_B) * square)
                gp_ref[step, at, :] = slope.astype(bf16)

    outs = [shape((count, width), bf16)] * 4
    outs += [shape((4, count, width), bf16), shape((4, width, width), bf16)]
    return call(kernel, "mlp_forward", scalars, list(arrays) + list(pieces), outs)


def gradient(matrix, order, name, scalars, lefts, rights):
    def kernel(scalars, arrays, outs):
        (place,) = scalars
        lefts, rights = arrays[:2], (arrays[2:4], arrays[4:6])
        for yr in range(2):
            total = dot_rows(lefts[0][...], rights[0][yr][...])
            total = total + dot_rows(lefts[1][...], rights[1][yr][...])
            matrix.store(place, [(0, total)], yr, order, outs[0])

    arrays = list(lefts) + list(rights[0]) + list(rights[1])
    (grad,) = call(kernel, name, scalars, arrays, matrix.grad_shapes(rights[0][0].shape[1]))
    return matrix.grad_result(grad, order)


def expanded_backward(scalars, arrays, pieces, fill):
    count, width = arrays[0].shape

    def kernel(scalars, arrays, outs):
        (place,) = scalars
        glow_ref, gp_ref = arrays[:2]
        ubg_ref, weight = outs[4:]
        fill(place, arrays[2:], weight)
        for step in range(4):
            total = jnp.zeros((1, width), f32)
            for at in row_blocks(count):
                grad = (dot(glow_ref[at, :], weight[step]) * up(gp_ref[step, at, :])).astype(bf16)
                outs[step][at, :] = grad
                total = total + jnp.sum(up(grad), axis=0, keepdims=True)
            ubg_ref[step] = total

    outs = [shape((count, width), bf16)] * 4
    outs += [shape((4, 1, width), f32), shape((4, width, width), bf16)]
    return call(kernel, "expanded_backward", scalars, list(arrays) + list(pieces), outs)


def middle_backward(arrays, parts):
    count, width = arrays[0].shape

    def kernel(scalars, arrays, outs):
        mid_ref, glow_ref, norm_ref, weight = arrays[:4]
        mg_ref, ml_ref, sums_ref = outs
        total = jnp.zeros((4, width), f32)
        for at in row_blocks(count):
            two = sum(dot_cols(part[at, :], weight[step]) for step, part in enumerate(arrays[4:]))
            normed, inverse = moments(mid_ref[at, :])
            out_grad = up(glow_ref[at, :])
            grad = out_grad + norm_back(two, normed, inverse, norm_ref[2:3, :])
            mg_ref[at, :] = grad
            ml_ref[at, :] = grad.astype(bf16)
            lines = [two * normed, two, grad, out_grad]
            total = total + join(*[jnp.sum(line, axis=0, keepdims=True) for line in lines])
        sums_ref[...] = total

    outs = [shape((count, width), f32), shape((count, width), bf16), shape((4, width), f32)]
    return call(kernel, "middle_backward", [], list(arrays) + list(parts), outs)


def block_out(arrays, parts):
    count, width = arrays[0].shape

    def kernel(scalars, arrays, outs):
        mid_ref, bias_ref, weight = arrays[:3]
        bias = bias_ref[bias_ref.shape[0] - 1 :, :]
        for at in row_blocks(count):
            total = sum(dot_cols(part[at, :], weight[step]) for step, part in enumerate(arrays[3:]))
            outs[0][at, :] = (mid_ref[at, :] + total + bias).astype(bf16)

    outs = [shape((count, width), bf16)]
    return call(kernel, "block_out", [], list(arrays) + list(parts), outs)[0]


def attention_backward(scalars, arrays):
    count, width = arrays[0].shape
    blocks = count // PAIR

    def kernel(scalars, arrays, outs, da, dq, dk, dv):
        (place,) = scalars
        ml_ref, q_ref, k_ref, v_ref, p_ref, weight = arrays
        lines_ref = outs[4]
        for yr in range(2):
            for at in row_blocks(count):
                ends = []
                for step in (yr, 2 + yr):
                    grad = dot(ml_ref[at, :], weight[step, :, 4 * PAIR :])
                    da[step, at, :] = grad[:, PAIR:].astype(bf16)
                    ends.append(grad[:, 0:PAIR])
                both = jnp.where(low_lanes(ends[0].shape), swap(ends[0]), ends[1])
                da[4 + yr, at, :] = both.astype(bf16)

        low = low_lanes((PAIR, PAIR))
        zero = jnp.zeros((PAIR, PAIR), bf16)
        scale = HEAD ** (-0.5)

        def stack(value):
            return join(jnp.where(low, value, zero), jnp.where(low, zero, value))

        def block(r, _):
            at = pl.ds(pl.multiple_of(r * PAIR, PAIR), PAIR)
            for pair in range(6):
                grad = stack(da[pair, at, :])
                low_probs = p_ref[pair, r]
                probs = up(low_probs)
                probs_grad = dot_cols(grad, v_ref[pair, at, :])
                shared = jnp.sum(probs * probs_grad, axis=1, keepdims=True)
                scores_grad = (probs * (probs_grad - shared)).astype(bf16)
                dv[pair, at, :] = dot_rows(low_probs, grad)
                both = dot(scores_grad, k_ref[pair, at, :])
                dq[pair, at, :] = jnp.where(low, both[0:PAIR], both[PAIR:]) * scale
                dk[pair, at, :] = dot_rows(scores_grad, stack(q_ref[pair, at, :])) * scale
            return 0

        lax.fori_loop(0, blocks, block, 0, unroll=2)
        low_all = low_lanes((count, PAIR))
        low_line = low_lanes((1, PAIR))

        def column_sum(value):
            return jnp.sum(up(value.astype(bf16)), axis=0, keepdims=True)

        for step in range(4):
            pc, yr = step // 2, step % 2
            pair = 4 + yr
            sums = []
            for value in (dq, dv):
                third = column_sum(value[pair])
                third = swap(third) if pc else third
                sums += [column_sum(value[step]), jnp.where(low_line, third, 0.0)]
            sums.append(jnp.zeros((1, width - 4 * PAIR), f32))
            lines_ref[pl.ds(block_of(place, step), 1), :] = jnp.concatenate(sums, axis=1)
            if pc:
                tail3 = jnp.where(low_all, swap(dq[pair]), dk[pair])
                tail4 = jnp.where(low_all, swap(dv[pair]), 0.0)
            else:
                tail3 = jnp.where(low_all, dq[pair], swap(dk[pair]))
                tail4 = jnp.where(low_all, dv[pair], 0.0)
            for i, part in enumerate((dq[step], dk[step], dv[step], tail3, tail4)):
                outs[step][:, i * PAIR : (i + 1) * PAIR] = part.astype(bf16)

    outs = [shape((count, 5 * PAIR), bf16)] * 4 + [shape((4, width), f32)]
    heads = (6, count, PAIR)
    scratch = [pltpu.VMEM(heads, bf16)] + [pltpu.VMEM(heads, f32)] * 3
    return call(kernel, "attention_backward", scalars, arrays, outs, scratch, micros=0)


def attention_gradient(matrix, order, scalars, lefts, rights, outer_lefts, outer_rights):
    def kernel(scalars, arrays, outs):
        (place,) = scalars
        n1, ml, outer = arrays[0:2], arrays[2:4], arrays[4:6]
        rights = (arrays[6:8], arrays[8:10])
        for yr in range(2):
            first = dot_rows(n1[0][...], rights[0][yr][...])
            first = first + dot_rows(n1[1][...], rights[1][yr][...])
            second = dot_rows(ml[0][...], outer[0][yr]) + dot_rows(ml[1][...], outer[1][yr])
            shared = first[:, 4 * PAIR :] + second[:, 0:PAIR]
            parts = [(0, first[:, 0 : 4 * PAIR]), (4 * PAIR, shared), (5 * PAIR, second[:, PAIR:])]
            matrix.store(place, parts, yr, order, outs[0])

    arrays = list(lefts) + list(outer_lefts) + list(outer_rights) + list(rights[0]) + list(rights[1])
    outs = matrix.grad_shapes(6 * PAIR)
    (grad,) = call(kernel, "attention_gradient", scalars, arrays, outs)
    return matrix.grad_result(grad, order)


def input_backward(scalars, arrays, parts):
    count, width = arrays[0].shape

    def kernel(scalars, arrays, outs):
        (place,) = scalars
        x_ref, mg_ref, norm_ref, weight, sums_ref, ubg_ref, heads_ref = arrays[:7]
        out_ref, lines_ref = outs
        total = jnp.zeros((2, width), f32)
        for at in row_blocks(count):
            one = sum(
                dot_cols(part[at, :], weight[step, :, 0 : 5 * PAIR])
                for step, part in enumerate(arrays[7:])
            )
            normed, inverse = moments(up(x_ref[at, :]))
            out_ref[at, :] = mg_ref[at, :] + norm_back(one, normed, inverse, norm_ref[0:1, :])
            lines = [jnp.sum(one * normed, axis=0, keepdims=True), jnp.sum(one, axis=0, keepdims=True)]
            total = total + join(*lines)
        lines_ref[0:8, :] = join(total, sums_ref[...], jnp.zeros((2, width), f32))
        for step in range(4):
            lines_ref[pl.ds(8 + block_of(place, step), 1), :] = ubg_ref[step]
        lines_ref[12:16, :] = heads_ref[...]

    outs = [shape((count, width), f32), shape((16, width), f32)]
    return call(kernel, "input_backward", scalars, list(arrays) + list(parts), outs)


def adam_step(weight, first, second, grad, rate, decay):
    first_new = beta_first * first + (1.0 - beta_first) * grad
    second_new = beta_second * second + (1.0 - beta_second) * grad * grad
    first_hat = first_new / (1.0 - beta_first**STEP)
    second_hat = second_new / (1.0 - beta_second**STEP)
    weight_new = weight - rate * (first_hat / (jnp.sqrt(second_hat) + adam_eps) + decay * weight)
    return (weight_new, first_new, second_new)


def pack_tiles(parts):
    q, k, v, o = ((part[:, :PAIR], part[:, PAIR:]) for part in parts)
    tail3 = jnp.concatenate([q[1], k[1]], axis=1)
    tail4 = jnp.concatenate([v[1], o[1]], axis=1)
    return q[0], k[0], v[0], tail3, tail4, o[0]


def own_columns(plan, place, value):
    width = value.shape[1]
    columns = width // math.prod(plan.dims)
    group = (place[0] * plan.dims[1] + place[1]) * 4 + rank_of(place)
    turn = lax.rem(width - group * columns, width)
    return pltpu.roll(value, turn, axis=1)[:, 0:columns]


def hold(plan, scalars, params, matrices):
    rows, cols = matrices[2][0].shape
    width = params[0].shape[1]
    columns = width // math.prod(plan.dims)

    def kernel(scalars, state, outs, small_ref):
        for t in range(3):
            parts = [state[t][i] for i in range(3)] + [state[3 + t][...]]
            for i, part in enumerate(pack_tiles(parts)):
                outs[0][t, :, i * PAIR : (i + 1) * PAIR] = part
            outs[0][3 + t] = state[6 + t][...]
            outs[0][6 + t] = state[9 + t][...]
        small_ref[0:8, :] = state[13][...]
        small_ref[8:12, :] = state[12][...]
        small_ref[12:16, :] = state[12][...]
        own = own_columns(plan, scalars[0], small_ref[...])
        outs[1][...] = own[8:12]
        outs[2][...] = own[0:8]

    outs = [shape((9, rows, cols), f32), shape((4, columns), f32), shape((8, columns), f32)]
    state = [value for group in matrices for value in group] + list(params)
    scratch = [pltpu.VMEM((16, width), f32)]
    return call(kernel, "hold", scalars, [], outs, scratch, 12, state, micros=10)


def total_gradients(plan, scalars, parts, lines):
    rows, cols = parts[0][0].shape[1:]
    width = lines[0].shape[2]
    devices = math.prod(plan.dims)
    columns = width // devices
    counts = [len(part) for part in parts]
    held = sum(counts)

    def kernel(scalars, arrays, outs, small_ref):
        at, squares = 0, jnp.zeros((1, 1), f32)

        def square(value):
            return jnp.sum(jnp.sum(value * value, axis=1, keepdims=True), axis=0, keepdims=True)

        for m, n in enumerate(counts):
            total = up(arrays[at][0])
            for i in range(1, n):
                total = total + up(arrays[at + i][0])
            outs[0][m] = total
            squares = squares + square(total)
            at += n
        sums = arrays[held][0]
        for ref in arrays[held + 1 :]:
            sums = sums + ref[0]
        size = width // 4
        small_ref[0:4, :] = sums[0:4]
        small_ref[4:8, :] = sums[8:12]
        for t in range(2):
            for mp in range(4):
                line = sums[12 + mp : 13 + mp, 2 * PAIR * t : 2 * PAIR * t + size]
                small_ref[8 + t : 9 + t, mp * size : (mp + 1) * size] = line
        small_ref[10:12, :] = sums[4:6]
        small_ref[12:16, :] = jnp.zeros((4, width), f32)
        own = own_columns(plan, scalars[0], small_ref[...])
        squares = squares + square(own)
        outs[1][...] = jnp.broadcast_to(squares[None], (devices, 1, 1))
        outs[2][...] = own[0:4]
        outs[3][...] = own[4:12]

    arrays = [part for group in parts for part in group] + list(lines)
    outs = [shape((3, rows, cols), f32), shape((devices, 1, 1), f32)]
    outs += [shape((n, columns), f32) for n in (4, 8)]
    scratch = [pltpu.VMEM((16, width), f32)]
    return call(kernel, "total_gradients", scalars, arrays, outs, scratch, 12)


def update(squares, grads, state, small, smalls, shapes):
    def kernel(scalars, arrays, outs):
        norm = jnp.sqrt(jnp.sum(arrays[0][...], axis=0))
        factor = jnp.minimum(1.0, clip_limit / (norm + 1e-06))
        outs[0][...] = norm
        grad_ref, state_ref = arrays[1:3]

        def step(weight, first, second, grad, rate, decay):
            grad = grad * factor
            new, first, second = adam_step(weight, first, second, grad, rate, decay)
            return [grad, new, first, second, new.astype(bf16)]

        for m in range(3):
            values = [state_ref[3 * m + t] for t in range(3)] + [grad_ref[m]]
            values = step(*values, matrix_rate, matrix_decay)
            for i, value in enumerate(values):
                if m:
                    outs[6 + 5 * m + i][...] = value
                    continue
                tiles = [value[:, t * PAIR : (t + 1) * PAIR] for t in range(6)]
                wide = [tiles[3], tiles[4]] if value.dtype == f32 else [up(t) for t in tiles[3:5]]
                tails = [part for t in wide for part in (t, swap(t))]
                for t in range(4):
                    ref = outs[1 + i] if t < 3 else outs[6 + i]
                    head = tiles[t] if t < 3 else tiles[5]
                    tail = tails[t][:, :HEAD].astype(value.dtype)
                    if t < 3:
                        ref[t, :, :PAIR] = head
                        ref[t, :, PAIR:] = tail
                    else:
                        ref[:, :PAIR] = head
                        ref[:, PAIR:] = tail
        for m in range(2):
            weight, first, second = (ref[...] for ref in arrays[5 + 3 * m : 8 + 3 * m])
            values = step(weight, first, second, arrays[3 + m][...], small_rate, 0.0)
            for i in range(4):
                outs[21 + 4 * m + i][...] = values[i]

    arrays = [squares, grads, state] + list(small)
    outs = [shape((1, 1), f32)]
    for dims in shapes:
        outs += [shape(dims, f32)] * 4 + [shape(dims, bf16)]
    for group in smalls:
        arrays += list(group)
        outs += [shape(group[0].shape, f32)] * 4
    return call(kernel, "update", [], arrays, outs)


def body(
    plan,
    block_input,
    cotangent,
    lengths,
    attn_input,
    attn_input_first,
    attn_input_second,
    attn_output,
    attn_output_first,
    attn_output_second,
    mlp_up,
    mlp_up_first,
    mlp_up_second,
    mlp_down,
    mlp_down_first,
    mlp_down_second,
    norm_params,
    norm_first,
    norm_second,
    bias_params,
    bias_first,
    bias_second,
):
    width = norm_params.shape[1]
    place = jnp.stack([lax.axis_index(axis) for axis in AXES]).astype(jnp.int32)
    matrix = Matrix(plan, place, width, attn_input.shape[0])
    send, send_z = plan.send, plan.send_z
    az, za = plan.order_az, plan.order_za
    low_bits, high_bits = plan.zbits[:2], plan.zbits[2:]
    def turned(value):
        return value.transpose(1, 0, 2)

    attn = pack_attention(turned(attn_input), attn_output)
    attn_z = [send_z(attn, mask) for mask in (1, 2, 3)]
    above, down = pack_mlp(mlp_up, mlp_down)
    above_z = send_z(above, 1)
    down_a = send(down, plan.a)
    n1, grad_low, head_bias = prepare(
        [place, lengths], [block_input, cotangent, norm_params, bias_params]
    )
    attn, *attn_z, above, above_z, down, down_a, n1, grad_low, head_bias = sync(
        attn, *attn_z, above, above_z, down, down_a, n1, grad_low, head_bias
    )

    attn, above, down = joined(
        "join_one", matrix, [attn, *attn_z], [above, above_z], [down, down_a]
    )
    attn = plan.spread(attn, high_bits)
    attn_a, attn_b = send(attn, plan.a), send(attn, plan.b)
    above_z = send_z(above, 2)
    attn_c = [send(attn, plan.core)]
    (above,) = joined("join_two", matrix, [above, above_z], micros=5)
    above = plan.spread(above, high_bits)
    above_a = send(above, plan.a)
    attn, attn_a, attn_b, above, down, *attn_c = sync(
        attn, attn_a, attn_b, above, down, *attn_c
    )

    def blocks(planes, order, *fixed):
        return [
            (array, plan.slots(pc, order, **what))
            for pc, arrays in enumerate(planes)
            for array, what in zip(arrays, fixed)
        ]

    corners = [dict(br=0, ar=0), dict(br=0, ar=1), dict(br=1, ar=0), dict(br=1, ar=1)]
    attn_ab = send(attn_a, plan.b)
    down_z = send_z(down, 2)
    attn_c += [send(attn_a, plan.core), send(attn_b, plan.core)]
    attn_ab, above, above_a, down, down_z, *attn_c[1:] = sync(
        attn_ab, above, above_a, down, down_z, *attn_c[1:]
    )

    (down,) = joined("join_three", matrix, [down, down_z])
    above_b = send(above, plan.b)
    above_ab = send(above_a, plan.b)
    down_z = send_z(down, 1)
    above_c = [send(piece, plan.core) for piece in (above, above_a)]
    attn_c.append(send(attn_ab, plan.core))
    pieces = blocks([[attn, attn_a, attn_b, attn_ab], attn_c], plan.plain, *corners)
    pieces, fill = matrix.weight_args(pieces)
    q, k, v, weight_attn = project([place], [n1, head_bias], pieces, fill)
    probs, att_own, att_other, middle, n2 = attend(
        [place, lengths], [block_input, norm_params, bias_params, q, k, v, weight_attn]
    )
    above, above_a, above_b, above_ab, down, down_z, att_other, n2, *above_c = sync(
        above, above_a, above_b, above_ab, down, down_z, att_other, n2, *above_c
    )

    (down,) = joined("join_four", matrix, [down, down_z])
    down = plan.spread(down, high_bits)
    down_b = send(down, plan.b)
    above_c += [send(piece, plan.core) for piece in (above_b, above_ab)]
    pieces = blocks([[above, above_a, above_b, above_ab], above_c], plan.plain, *corners)
    pieces, fill = matrix.weight_args(pieces)
    *hidden, slope, weight_up = mlp_forward([place], [n2, bias_params], pieces, fill)
    n2_c, att_c = send(n2, plan.core), send(att_other, plan.core)
    grad_low_c = send(grad_low, plan.core)
    down_c = [send(down, plan.core)]
    hidden_c = [send(part, plan.core) for part in hidden[2:]]
    down_b, n2_c, att_c, grad_low_c, down_c[0], *hidden_c = sync(
        down_b, n2_c, att_c, grad_low_c, down_c[0], *hidden_c
    )

    down_c.append(send(down_b, plan.core))
    down_g = gradient(
        matrix, za, "down_gradient", [place], [grad_low, grad_low_c], [hidden[:2], hidden_c]
    )
    pieces = blocks([[down, down_b], down_c], za, dict(br=0), dict(br=1))
    pieces, fill = matrix.weight_args(pieces)
    down_g, *pieces = sync(down_g, *pieces)

    half = down_g.shape[0] // 2
    down_gb = send(down_g[half:], plan.b)
    *grads, up_bias_grad, weight_down = expanded_backward(
        [place], [grad_low, slope], pieces, fill
    )
    grads_c = [send(part, plan.core) for part in grads[2:]]
    middle_grad, middle_low, sums_two = middle_backward(
        [middle, grad_low, norm_params, weight_up], grads
    )
    up_g = gradient(matrix, az, "up_gradient", [place], [n2, n2_c], [grads[:2], grads_c])
    n1_c = send(n1, plan.core)
    up_g, middle_low, n1_c = sync(up_g, middle_low, n1_c)

    up_gb = send(up_g[half:], plan.b)
    terms = [down_g, down_gb]
    if high_bits:
        terms = [plan.fold(up(down_g[:half]) + up(down_gb), high_bits)]
    down_s, down_0 = added(
        "add_one",
        matrix,
        (4, f32, [(part, 0) for part in terms]),
        (4, bf16, [(part, 4) for part in terms]),
    )
    down_s, down_0, middle_low = sync(down_s, down_0, middle_low)

    down_z = send_z(down_0, 1)
    middle_low_c = send(middle_low, plan.core)
    *joint, head_lines = attention_backward(
        [place], [middle_low, q, k, v, probs, weight_attn]
    )
    joint_c = [send(part, plan.core) for part in joint[2:]]
    down_s, down_0, down_1 = added(
        "add_down",
        matrix,
        (2, f32, [(down_s, 0), (down_z, 0)]),
        (1, bf16, [(down_s, 2), (down_z, 2)]),
        (1, bf16, [(down_s, 3), (down_z, 3)]),
        micros=2,
    )
    middle_low_c, up_gb, down_s, down_0, down_1, *rest = sync(
        middle_low_c, up_gb, down_s, down_0, down_1, *joint, *joint_c
    )
    joint, joint_c = rest[:4], rest[4:]

    fourth = half // 2
    (up_0,) = added("add_two", matrix, (fourth, bf16, [(up_g, fourth), (up_gb, fourth)]))
    up_ga = send(up_0, plan.a)
    attn_g = attention_gradient(
        matrix, az, [place], [n1, n1_c], [joint[:2], joint_c],
        [middle_low, middle_low_c], [att_own, att_c],
    )
    attn_gb = send(attn_g[half:], plan.b)
    down_z0, down_z1 = send_z(down_0, 2), send_z(down_1, 2)
    input_grad, lines = input_backward(
        [place],
        [block_input, middle_grad, norm_params, weight_attn, sums_two, up_bias_grad, head_lines],
        joint,
    )
    lines = lines[None]
    terms = [up_g, up_gb, up_ga]
    if high_bits:
        terms = [plan.fold(sum(up(part[:fourth]) for part in terms), high_bits)]
    up_s, up_0 = added(
        "add_three",
        matrix,
        (2, f32, [(part, 0) for part in terms]),
        (2, bf16, [(part, 2) for part in terms]),
    )
    up_z = send_z(up_0, 1)
    lines, up_s = sync(lines, up_s)
    lines_a = send(lines, plan.a)
    (lines,) = added("add_lines", matrix, (1, f32, [(lines, 0), (lines_a, 0)]))
    lines_z = send_z(lines, 1)
    matrices = (
        (turned(attn_input), turned(attn_input_first), turned(attn_input_second)),
        (attn_output, attn_output_first, attn_output_second),
        (mlp_up, mlp_up_first, mlp_up_second),
        (mlp_down, mlp_down_first, mlp_down_second),
    )
    up_s, norms = sync(up_s, norm_params)
    down_z0, norms = sync(down_z0, norms)
    state, own_norm, own_bias = hold(plan, [place], [norms, bias_params], matrices)
    attn_gb, down_z1, up_z, lines_z, state, input_grad = sync(
        attn_gb, down_z1, up_z, lines_z, state, input_grad
    )

    attn_0, down_s, down_0, up_s, up_0, lines = added(
        "add_four",
        matrix,
        (fourth, bf16, [(attn_g, fourth), (attn_gb, fourth)]),
        (1, f32, [(down_s, 0), (down_z0, 0)]),
        (1, bf16, [(down_s, 1), (down_z1, 0)]),
        (1, f32, [(up_s, 0), (up_z, 0)]),
        (1, bf16, [(up_s, 1), (up_z, 1)]),
        (1, f32, [(lines, 0), (lines_z, 0)]),
    )
    attn_ga = send(attn_0, plan.a)
    up_z = send_z(up_0, 2)
    lines_z = send_z(lines, 2)
    for bit in high_bits:
        lines = lines + lines_z
        lines_z = send_z(lines, bit)
    block_output = block_out([middle, bias_params, weight_down], hidden)
    attn_ga, up_z, lines_z, down_0, block_output = sync(
        attn_ga, up_z, lines_z, down_0, block_output
    )

    terms = [attn_g, attn_gb, attn_ga]
    if high_bits:
        terms = [plan.fold(sum(up(part[:fourth]) for part in terms), high_bits)]
    attn_s, *attn_0, lines = added(
        "add_five",
        matrix,
        (1, f32, [(part, 0) for part in terms]),
        (1, bf16, [(part, 1) for part in terms]),
        (1, bf16, [(part, 2) for part in terms]),
        (1, bf16, [(part, 3) for part in terms]),
        (1, f32, [(lines, 0), (lines_z, 0)]),
    )
    attn_z = [send_z(part, mask) for part, mask in zip(attn_0, (2, 1, 3))]
    down_ga = send(down_0, plan.a)
    rest = [send(lines, perm) for perm in (plan.b, plan.core, plan.cross)]
    state, down_ga, *rest = sync(state, down_ga, *rest, *attn_z)
    rest, attn_z = rest[:3], rest[3:]

    sums, squares, norm_sum, bias_sum = total_gradients(
        plan, [place], [[attn_s, *attn_z], [up_s, up_z], [down_s, down_ga]], [lines, *rest]
    )
    squares = lax.all_to_all(squares, AXES, 0, 0, tiled=True)
    grad_norm, *results = update(
        squares,
        sums,
        state,
        [norm_sum, bias_sum],
        ((own_norm, norm_first, norm_second), (own_bias, bias_first, bias_second)),
        [group[0].shape for group in matrices],
    )
    results[:5] = [turned(value) for value in results[:5]]
    return (block_output, input_grad, grad_norm[0, 0], *results)


def solution(mesh):
    dp, mp = mesh.shape["dp"], mesh.shape["mp"]
    dims = (dp // 2, 2, mp // 2, 2)
    fine = Mesh(np.asarray(mesh.devices).reshape(dims), AXES)
    plan = Plan(dims)
    d, m = ("z", "x"), ("y", "c")
    every = d + m
    rows = P(every, None)
    cube = P(d, None, m)
    flat = P(d, m)
    small = P(None, every)
    return jax.shard_map(
        functools.partial(body, plan),
        mesh=fine,
        in_specs=(rows, rows, P(d)) + (cube,) * 3 + (flat,) * 9 + (P(), small, small) * 2,
        out_specs=(rows, rows, P()) + (cube,) * 5 + (flat,) * 15 + (small,) * 8,
        check_vma=False,
    )
```

```python
import functools
import math

import jax
import jax.numpy as jnp
import numpy as np
from jax import lax
from jax.experimental import pallas as pl
from jax.experimental.pallas import tpu as pltpu
from jax.sharding import Mesh, PartitionSpec as P

HEAD = 64
STEP = 10

norm_eps = 1e-06
beta_first = 0.5
beta_second = 0.5
adam_eps = 1e-08
matrix_rate = 0.03
small_rate = 0.3
matrix_decay = 0.01
clip_limit = 1.0
masked_score = -1e30

f32 = jnp.float32
bf16 = jnp.bfloat16
AXES = ("z", "x", "y", "c")
PAIR = 2 * HEAD
GELU_A = math.sqrt(2.0 / math.pi)
GELU_B = 0.044715


def sync(*values):
    return lax.optimization_barrier(values)


def up(value):
    return value.astype(f32)


def join(*values):
    return jnp.concatenate(values, axis=0)


class Plan:
    def __init__(self, dims):
        self.dims = dims
        self.z = dims[0]
        self.zbits = [1 << i for i in range(int(math.log2(self.z)))]
        self.places = [tuple(p) for p in np.ndindex(*dims)]
        self.index = {p: i for i, p in enumerate(self.places)}
        self.core = self.perm(lambda z, x, y, c: (z, x, y, 1 - c))
        self.a = self.perm(lambda z, x, y, c: (z, x ^ (1 - c), y ^ c, c))
        self.b = self.perm(lambda z, x, y, c: (z, x ^ c, y ^ (1 - c), c))
        self.cross = self.perm(lambda z, x, y, c: (z, x ^ c, y ^ (1 - c), 1 - c))
        each = [(br, ar) for br in range(2) for ar in range(2)]
        turned = sorted(range(self.z), key=self.turn)
        self.plain = [(br, ar, zr) for br, ar in each for zr in range(self.z)]
        self.order_az = [(br, ar, zr) for br, ar in each for zr in turned]
        self.order_za = [(br, ar, zr) for br in range(2) for zr in turned for ar in range(2)]

    def turn(self, zr):
        return (zr >> 2) * 4 + (zr & 1) * 2 + ((zr >> 1) & 1)

    def perm(self, move):
        return [(self.index[p], self.index[move(*p)]) for p in self.places]

    def zmove(self, mask):
        return self.perm(lambda z, x, y, c: (z ^ mask, x, y, c))

    def send(self, value, perm):
        return lax.ppermute(value, AXES, perm)

    def send_z(self, value, mask):
        return self.send(value, self.zmove(mask))

    def spread(self, block, bits):
        for bit in bits:
            block = join(block, self.send_z(block, bit))
        return block

    def fold(self, total, bits):
        for bit in bits[::-1]:
            half = total.shape[0] // 2
            total = total[:half] + up(self.send_z(total[half:].astype(bf16), bit))
        return total

    def table(self, place, slots):
        pc, br, ar, zr = (jnp.asarray(v, jnp.int32) for v in zip(*slots))
        core = place[3] ^ pc
        x = place[1] ^ jnp.where(core == 0, ar, br)
        yr = jnp.where(core == 0, br, ar)
        dp = (place[0] ^ zr) * self.dims[1] + x
        return (2 * pc + yr) * (self.z * self.dims[1]) + dp

    def slots(self, pc, order, **fixed):
        names = ("br", "ar", "zr")
        return [
            (pc,) + slot
            for slot in order
            if all(slot[names.index(name)] == value for name, value in fixed.items())
        ]


def dot(left, right):
    return lax.dot_general(left, right, (((1,), (0,)), ((), ())), preferred_element_type=f32)


def dot_cols(left, right):
    return lax.dot_general(left, right, (((1,), (1,)), ((), ())), preferred_element_type=f32)


def dot_rows(left, right):
    return lax.dot_general(left, right, (((0,), (0,)), ((), ())), preferred_element_type=f32)


def low_lanes(shape):
    return lax.broadcasted_iota(jnp.int32, shape, len(shape) - 1) < HEAD


def swap(value):
    return pltpu.roll(value, HEAD, axis=1)


def moments(rows):
    center = jnp.mean(rows, axis=1, keepdims=True)
    centered = rows - center
    spread = jnp.mean(centered * centered, axis=1, keepdims=True)
    inverse = lax.rsqrt(spread + norm_eps)
    return centered * inverse, inverse


def norm_back(grad_rows, normed, inverse, gain):
    scaled = grad_rows * gain
    return inverse * (
        scaled
        - jnp.mean(scaled, axis=1, keepdims=True)
        - normed * jnp.mean(scaled * normed, axis=1, keepdims=True)
    )


class Matrix:
    def __init__(self, plan, place, width, rows):
        self.plan = plan
        self.place = place
        self.width = width
        self.rows = rows
        self.direct = rows % 16 == 0
        self.blocks_dp = plan.dims[0] * plan.dims[1]

    def whole(self, pieces):
        order = [slot for _, slots in pieces for slot in slots]
        blocks = join(*[array for array, _ in pieces])
        turn = jnp.argsort(self.plan.table(self.place, order))
        return jnp.take(blocks, turn, axis=0).reshape(4, self.width, blocks.shape[-1])

    def place_blocks(self, place, refs, slots, weight):
        for ref, of_ref in zip(refs, slots):
            for i, (pc, br, ar, zr) in enumerate(of_ref):
                core = place[3] ^ pc
                xr = jnp.where(core == 0, ar, br)
                yr = jnp.where(core == 0, br, ar)
                dp = (place[0] ^ zr) * self.plan.dims[1] + (place[1] ^ xr)
                row = pl.multiple_of(dp * self.rows, 16)
                weight[2 * pc + yr, pl.ds(row, self.rows), :] = ref[i]

    def weight_args(self, pieces):
        if self.direct:
            slots = [of for _, of in pieces]
            return [array for array, _ in pieces], functools.partial(self.fill, slots)
        return [self.whole(pieces)], lambda place, refs, weight: self.copy(refs, weight)

    def fill(self, slots, place, refs, weight):
        self.place_blocks(place, refs, slots, weight)

    def copy(self, refs, weight):
        weight[...] = refs[0][...]

    def grad_shapes(self, cols):
        if self.direct:
            return [jax.ShapeDtypeStruct((4 * self.plan.z, self.rows, cols), bf16)]
        return [jax.ShapeDtypeStruct((2, self.width, cols), bf16)]

    def store(self, place, parts, yr, order, out):
        if not self.direct:
            for at, part in parts:
                out[yr, :, at : at + part.shape[1]] = part.astype(bf16)
            return
        z = self.plan.z
        core = place[3]
        for dp in range(self.blocks_dp):
            zr = place[0] ^ (dp // self.plan.dims[1])
            xr = place[1] ^ (dp % self.plan.dims[1])
            ar = jnp.where(core == 0, xr, yr)
            br = jnp.where(core == 0, yr, xr)
            zi = self.plan.turn(zr)
            if order is self.plan.order_az:
                slot = br * (2 * z) + ar * z + zi
            else:
                slot = br * (2 * z) + zi * 2 + ar
            rows = slice(dp * self.rows, (dp + 1) * self.rows)
            for at, part in parts:
                out[slot, :, at : at + part.shape[1]] = part[rows, :].astype(bf16)

    def grad_result(self, grad, order):
        if self.direct:
            return grad
        whole = grad.reshape(2 * self.blocks_dp, self.rows, grad.shape[-1])
        table = self.plan.table(self.place, [(0,) + slot for slot in order])
        return jnp.take(whole, table, axis=0)


def call(kernel, name, scalars, arrays, outs, scratch=(), mib=16, hbm=(), micros=0):
    scalars, arrays, outs = list(scalars), list(arrays), list(outs)
    hbm = [pltpu.with_memory_space_constraint(part, pltpu.HBM) for part in hbm]
    counts = (len(scalars), len(arrays), len(hbm), len(outs), len(hbm), min(len(hbm), 1))

    def split(*refs):
        parts, at = [], 0
        for n in counts:
            parts.append(list(refs[at : at + n]))
            at += n
        copies = [
            pltpu.make_async_copy(source, target, parts[5][0].at[i])
            for i, (source, target) in enumerate(zip(parts[2], parts[4]))
        ]
        for copy in copies:
            copy.start()
        for copy in copies:
            copy.wait()
        kernel(parts[0], parts[1] + parts[4], parts[3], *refs[at:])

    vmem = pl.BlockSpec(memory_space=pltpu.VMEM)
    specs = [pl.BlockSpec(memory_space=pltpu.SMEM)] * len(scalars) + [vmem] * len(arrays)
    specs += [pl.BlockSpec(memory_space=pltpu.HBM)] * len(hbm)
    own = [pltpu.VMEM(part.shape, part.dtype) for part in hbm]
    if hbm:
        own.append(pltpu.SemaphoreType.DMA((len(hbm),)))
    return pl.pallas_call(
        split,
        name=name,
        out_shape=outs,
        in_specs=specs,
        out_specs=[vmem] * len(outs),
        scratch_shapes=own + list(scratch),
        compiler_params=pltpu.CompilerParams(vmem_limit_bytes=mib * 2**20),
        cost_estimate=pl.CostEstimate(
            flops=1 + int(micros * 1.15e9), bytes_accessed=1, transcendentals=0
        ),
    )(*scalars, *arrays, *hbm)


def shape(dims, kind):
    return jax.ShapeDtypeStruct(tuple(dims), kind)


def rank_of(place):
    return place[2] * 2 + place[3]


def block_of(place, step):
    return rank_of(place) ^ (2 * (step % 2) + step // 2)


def row_blocks(count):
    size = 256 if count % 256 == 0 else count
    return [slice(r, r + size) for r in range(0, count, size)]


def joined(name, matrix, *groups, micros=0):
    if not matrix.direct:
        return [join(*group) for group in groups]

    def kernel(scalars, arrays, outs):
        at = 0
        for group, out in zip(groups, outs):
            row = 0
            for _ in group:
                for i in range(arrays[at].shape[0]):
                    out[row] = arrays[at][i]
                    row += 1
                at += 1

    outs = []
    for group in groups:
        rows = sum(part.shape[0] for part in group)
        outs.append(shape((rows,) + group[0].shape[1:], group[0].dtype))
    arrays = [part for group in groups for part in group]
    return call(kernel, name, [], arrays, outs, mib=8, micros=micros)


def added(name, matrix, *sums, micros=0):
    sums = [each if isinstance(each, list) else [each] for each in sums]
    if not matrix.direct:
        return [
            join(*[
                sum(up(part[at : at + count]) for part, at in terms).astype(kind)
                for count, kind, terms in each
            ])
            for each in sums
        ]
    arrays = []
    for each in sums:
        for _, _, terms in each:
            for part, _ in terms:
                if not any(part is other for other in arrays):
                    arrays.append(part)

    def where(part):
        return next(i for i, other in enumerate(arrays) if part is other)

    def kernel(scalars, refs, outs):
        for each, out in zip(sums, outs):
            row = 0
            for count, kind, terms in each:
                for i in range(count):
                    total = up(refs[where(terms[0][0])][terms[0][1] + i])
                    for part, at in terms[1:]:
                        total = total + up(refs[where(part)][at + i])
                    out[row] = total.astype(kind)
                    row += 1

    outs = [
        shape((sum(one[0] for one in each),) + each[0][2][0][0].shape[1:], each[0][1])
        for each in sums
    ]
    return call(kernel, name, [], arrays, outs, mib=8, micros=micros)


def pack_attention(inputs, output):
    rows = output.shape[0]

    def kernel(scalars, arrays, outs):
        in_ref, out_ref = arrays
        parts = [in_ref[t].astype(bf16) for t in range(3)] + [out_ref[...].astype(bf16)]
        for i, part in enumerate(pack_tiles(parts)):
            outs[0][0, :, i * PAIR : (i + 1) * PAIR] = part

    outs = [shape((1, rows, 6 * PAIR), bf16)]
    return call(kernel, "pack_attention", [], [], outs, mib=8, hbm=[inputs, output])[0]


def pack_mlp(above, down):
    def kernel(scalars, arrays, outs):
        for ref, out in zip(arrays, outs):
            out[0] = ref[...].astype(bf16)

    outs = [shape((1,) + above.shape, bf16)] * 2
    return call(kernel, "pack_mlp", [], [], outs, mib=8, hbm=[above, down])


def prepare(scalars, hbm):
    count, width = hbm[0].shape
    units = hbm[3].shape[0] - 4

    def kernel(scalars, arrays, outs):
        place, lens = scalars
        x_ref, cot_ref, norm_ref, bias_ref = arrays
        n1_ref, glow_ref, head_ref = outs
        size = width // 4
        for t in range(2):
            for mp in range(4):
                line = bias_ref[units + t : units + t + 1, mp * size : (mp + 1) * size]
                head_ref[4 * t + mp : 4 * t + mp + 1, 0:size] = line
        gain1, shift1 = norm_ref[0:1, :], norm_ref[1:2, :]
        for at in row_blocks(count):
            normed, _ = moments(up(x_ref[at, :]))
            n1_ref[at, :] = (normed * gain1 + shift1).astype(bf16)
        captions = lens.shape[0] // 4
        length = count // captions
        for j in range(captions):
            at = slice(j * length, (j + 1) * length)
            limit = lens[rank_of(place) * captions + j]
            keep = lax.broadcasted_iota(jnp.int32, (length, width), 0) < limit
            glow_ref[at, :] = jnp.where(keep, up(cot_ref[at, :]), 0.0).astype(bf16)

    outs = [shape((count, width), bf16)] * 2 + [shape((8, 2 * PAIR), f32)]
    return call(kernel, "prepare", scalars, [], outs, hbm=hbm)


def project(scalars, arrays, pieces, fill):
    count, width = arrays[0].shape

    def kernel(scalars, arrays, outs):
        (place,) = scalars
        n1_ref, head_bias = arrays[:2]
        q_ref, k_ref, v_ref, weight = outs
        fill(place, arrays[2:], weight)
        bias = []
        for step in range(4):
            mp = block_of(place, step)
            bias.append((head_bias[pl.ds(mp, 1), :], head_bias[pl.ds(mp + 4, 1), :]))
        low_line = low_lanes((1, PAIR))
        for yr in range(2):
            pair = 4 + yr
            third = [
                jnp.where(low_line, bias[yr][t][:, PAIR:], swap(bias[2 + yr][t][:, PAIR:]))
                for t in range(2)
            ]
            for at in row_blocks(count):
                joined = []
                for step in (yr, 2 + yr):
                    part = dot(n1_ref[at, :], weight[step, :, 0 : 5 * PAIR])
                    query_bias, value_bias = bias[step]
                    q_ref[step, at, :] = (part[:, 0:PAIR] + query_bias[:, :PAIR]).astype(bf16)
                    k_ref[step, at, :] = part[:, PAIR : 2 * PAIR].astype(bf16)
                    v_ref[step, at, :] = (part[:, 2 * PAIR : 3 * PAIR] + value_bias[:, :PAIR]).astype(bf16)
                    joined.append((part[:, 3 * PAIR : 4 * PAIR], part[:, 4 * PAIR :]))
                (own3, own4), (other3, other4) = joined
                low = low_lanes(own3.shape)
                query = jnp.where(low, own3, swap(other3)) + third[0]
                value = jnp.where(low, own4, swap(other4)) + third[1]
                q_ref[pair, at, :] = query.astype(bf16)
                k_ref[pair, at, :] = jnp.where(low, swap(own3), other3).astype(bf16)
                v_ref[pair, at, :] = value.astype(bf16)

    heads = shape((6, count, PAIR), bf16)
    outs = [heads, heads, heads, shape((4, width, 6 * PAIR), bf16)]
    return call(kernel, "project", scalars, list(arrays) + list(pieces), outs)


def attend(scalars, arrays):
    count, width = arrays[0].shape
    blocks = count // PAIR

    def kernel(scalars, arrays, outs, att):
        place, lens = scalars
        x_ref, norm_ref, bias_ref, q_ref, k_ref, v_ref, weight = arrays
        p_ref, own_ref, other_ref, mid_ref, n2_ref = outs
        first = rank_of(place) * (2 * blocks)
        lane = lax.broadcasted_iota(jnp.int32, (2 * PAIR, PAIR), 1)
        line = lax.broadcasted_iota(jnp.int32, (2 * PAIR, PAIR), 0)
        same = ((line // HEAD) % 2) == (lane // HEAD)
        low = low_lanes((PAIR, PAIR))
        zero = jnp.zeros((PAIR, PAIR), bf16)

        def block(r, _):
            at = pl.ds(pl.multiple_of(r * PAIR, PAIR), PAIR)
            limit = jnp.where(lane < HEAD, lens[first + 2 * r], lens[first + 2 * r + 1] + HEAD)
            keep = same & (lane < limit)
            for pair in range(6):
                query = q_ref[pair, at, :]
                stacked = join(jnp.where(low, query, zero), jnp.where(low, zero, query))
                scores = dot_cols(stacked, k_ref[pair, at, :]) * (HEAD ** (-0.5))
                scores = jnp.where(keep, scores, masked_score)
                expo = jnp.exp(scores - jnp.max(scores, axis=1, keepdims=True))
                probs = (expo / jnp.sum(expo, axis=1, keepdims=True)).astype(bf16)
                p_ref[pair, r] = probs
                out = dot(probs, v_ref[pair, at, :])
                att[pair, at, :] = jnp.where(low, out[0:PAIR], out[PAIR:])
            return 0

        lax.fori_loop(0, blocks, block, 0, unroll=2)
        low_all = low_lanes((count, PAIR))
        for step in range(4):
            pc, yr = step // 2, step % 2
            part_ref = (own_ref, other_ref)[pc]
            third = att[4 + yr] if pc else swap(att[4 + yr])
            part_ref[yr, :, 0:PAIR] = jnp.where(low_all, 0.0, third).astype(bf16)
            part_ref[yr, :, PAIR:] = att[step].astype(bf16)
        out_bias = bias_ref[bias_ref.shape[0] - 2 : bias_ref.shape[0] - 1, :]
        gain2, shift2 = norm_ref[2:3, :], norm_ref[3:4, :]
        for at in row_blocks(count):
            branch = up(x_ref[at, :]) + out_bias
            for step in range(4):
                part_ref = (own_ref, other_ref)[step // 2]
                branch = branch + dot_cols(part_ref[step % 2, at, :], weight[step, :, 4 * PAIR :])
            mid_ref[at, :] = branch
            normed, _ = moments(branch)
            n2_ref[at, :] = (normed * gain2 + shift2).astype(bf16)

    part = shape((2, count, 2 * PAIR), bf16)
    outs = [
        shape((6, blocks, 2 * PAIR, PAIR), bf16),
        part,
        part,
        shape((count, width), f32),
        shape((count, width), bf16),
    ]
    return call(kernel, "attend", scalars, arrays, outs, [pltpu.VMEM((6, count, PAIR), f32)])


def mlp_forward(scalars, arrays, pieces, fill):
    count, width = arrays[0].shape

    def kernel(scalars, arrays, outs):
        (place,) = scalars
        n2_ref, bias_ref = arrays[:2]
        gp_ref, weight = outs[4:]
        fill(place, arrays[2:], weight)
        for step in range(4):
            bias = bias_ref[pl.ds(block_of(place, step), 1), :]
            for at in row_blocks(count):
                value = dot(n2_ref[at, :], weight[step]) + bias
                square = value * value
                t = jnp.tanh((GELU_A * value) * (1.0 + GELU_B * square))
                half = 0.5 * (1.0 + t)
                outs[step][at, :] = (value * half).astype(bf16)
                slope = half + (0.5 * GELU_A) * value * (1.0 - t * t) * (1.0 + (3.0 * GELU_B) * square)
                gp_ref[step, at, :] = slope.astype(bf16)

    outs = [shape((count, width), bf16)] * 4
    outs += [shape((4, count, width), bf16), shape((4, width, width), bf16)]
    return call(kernel, "mlp_forward", scalars, list(arrays) + list(pieces), outs)


def gradient(matrix, order, name, scalars, lefts, rights):
    def kernel(scalars, arrays, outs):
        (place,) = scalars
        lefts, rights = arrays[:2], (arrays[2:4], arrays[4:6])
        for yr in range(2):
            total = dot_rows(lefts[0][...], rights[0][yr][...])
            total = total + dot_rows(lefts[1][...], rights[1][yr][...])
            matrix.store(place, [(0, total)], yr, order, outs[0])

    arrays = list(lefts) + list(rights[0]) + list(rights[1])
    (grad,) = call(kernel, name, scalars, arrays, matrix.grad_shapes(rights[0][0].shape[1]))
    return matrix.grad_result(grad, order)


def expanded_backward(scalars, arrays, pieces, fill):
    count, width = arrays[0].shape

    def kernel(scalars, arrays, outs):
        (place,) = scalars
        glow_ref, gp_ref = arrays[:2]
        ubg_ref, weight = outs[4:]
        fill(place, arrays[2:], weight)
        for step in range(4):
            total = jnp.zeros((1, width), f32)
            for at in row_blocks(count):
                grad = (dot(glow_ref[at, :], weight[step]) * up(gp_ref[step, at, :])).astype(bf16)
                outs[step][at, :] = grad
                total = total + jnp.sum(up(grad), axis=0, keepdims=True)
            ubg_ref[step] = total

    outs = [shape((count, width), bf16)] * 4
    outs += [shape((4, 1, width), f32), shape((4, width, width), bf16)]
    return call(kernel, "expanded_backward", scalars, list(arrays) + list(pieces), outs)


def middle_backward(arrays, parts):
    count, width = arrays[0].shape

    def kernel(scalars, arrays, outs):
        mid_ref, glow_ref, norm_ref, weight = arrays[:4]
        mg_ref, ml_ref, sums_ref = outs
        total = jnp.zeros((4, width), f32)
        for at in row_blocks(count):
            two = sum(dot_cols(part[at, :], weight[step]) for step, part in enumerate(arrays[4:]))
            normed, inverse = moments(mid_ref[at, :])
            out_grad = up(glow_ref[at, :])
            grad = out_grad + norm_back(two, normed, inverse, norm_ref[2:3, :])
            mg_ref[at, :] = grad
            ml_ref[at, :] = grad.astype(bf16)
            lines = [two * normed, two, grad, out_grad]
            total = total + join(*[jnp.sum(line, axis=0, keepdims=True) for line in lines])
        sums_ref[...] = total

    outs = [shape((count, width), f32), shape((count, width), bf16), shape((4, width), f32)]
    return call(kernel, "middle_backward", [], list(arrays) + list(parts), outs)


def block_out(arrays, parts):
    count, width = arrays[0].shape

    def kernel(scalars, arrays, outs):
        mid_ref, bias_ref, weight = arrays[:3]
        bias = bias_ref[bias_ref.shape[0] - 1 :, :]
        for at in row_blocks(count):
            total = sum(dot_cols(part[at, :], weight[step]) for step, part in enumerate(arrays[3:]))
            outs[0][at, :] = (mid_ref[at, :] + total + bias).astype(bf16)

    outs = [shape((count, width), bf16)]
    return call(kernel, "block_out", [], list(arrays) + list(parts), outs)[0]


def attention_backward(scalars, arrays):
    count, width = arrays[0].shape
    blocks = count // PAIR

    def kernel(scalars, arrays, outs, da, dq, dk, dv):
        (place,) = scalars
        ml_ref, q_ref, k_ref, v_ref, p_ref, weight = arrays
        lines_ref = outs[4]
        for yr in range(2):
            for at in row_blocks(count):
                ends = []
                for step in (yr, 2 + yr):
                    grad = dot(ml_ref[at, :], weight[step, :, 4 * PAIR :])
                    da[step, at, :] = grad[:, PAIR:].astype(bf16)
                    ends.append(grad[:, 0:PAIR])
                both = jnp.where(low_lanes(ends[0].shape), swap(ends[0]), ends[1])
                da[4 + yr, at, :] = both.astype(bf16)

        low = low_lanes((PAIR, PAIR))
        zero = jnp.zeros((PAIR, PAIR), bf16)
        scale = HEAD ** (-0.5)

        def stack(value):
            return join(jnp.where(low, value, zero), jnp.where(low, zero, value))

        def block(r, _):
            at = pl.ds(pl.multiple_of(r * PAIR, PAIR), PAIR)
            for pair in range(6):
                grad = stack(da[pair, at, :])
                low_probs = p_ref[pair, r]
                probs = up(low_probs)
                probs_grad = dot_cols(grad, v_ref[pair, at, :])
                shared = jnp.sum(probs * probs_grad, axis=1, keepdims=True)
                scores_grad = (probs * (probs_grad - shared)).astype(bf16)
                dv[pair, at, :] = dot_rows(low_probs, grad)
                both = dot(scores_grad, k_ref[pair, at, :])
                dq[pair, at, :] = jnp.where(low, both[0:PAIR], both[PAIR:]) * scale
                dk[pair, at, :] = dot_rows(scores_grad, stack(q_ref[pair, at, :])) * scale
            return 0

        lax.fori_loop(0, blocks, block, 0, unroll=2)
        low_all = low_lanes((count, PAIR))
        low_line = low_lanes((1, PAIR))

        def column_sum(value):
            return jnp.sum(up(value.astype(bf16)), axis=0, keepdims=True)

        for step in range(4):
            pc, yr = step // 2, step % 2
            pair = 4 + yr
            sums = []
            for value in (dq, dv):
                third = column_sum(value[pair])
                third = swap(third) if pc else third
                sums += [column_sum(value[step]), jnp.where(low_line, third, 0.0)]
            sums.append(jnp.zeros((1, width - 4 * PAIR), f32))
            lines_ref[pl.ds(block_of(place, step), 1), :] = jnp.concatenate(sums, axis=1)
            if pc:
                tail3 = jnp.where(low_all, swap(dq[pair]), dk[pair])
                tail4 = jnp.where(low_all, swap(dv[pair]), 0.0)
            else:
                tail3 = jnp.where(low_all, dq[pair], swap(dk[pair]))
                tail4 = jnp.where(low_all, dv[pair], 0.0)
            for i, part in enumerate((dq[step], dk[step], dv[step], tail3, tail4)):
                outs[step][:, i * PAIR : (i + 1) * PAIR] = part.astype(bf16)

    outs = [shape((count, 5 * PAIR), bf16)] * 4 + [shape((4, width), f32)]
    heads = (6, count, PAIR)
    scratch = [pltpu.VMEM(heads, bf16)] + [pltpu.VMEM(heads, f32)] * 3
    return call(kernel, "attention_backward", scalars, arrays, outs, scratch, micros=0)


def attention_gradient(matrix, order, scalars, lefts, rights, outer_lefts, outer_rights):
    def kernel(scalars, arrays, outs):
        (place,) = scalars
        n1, ml, outer = arrays[0:2], arrays[2:4], arrays[4:6]
        rights = (arrays[6:8], arrays[8:10])
        for yr in range(2):
            first = dot_rows(n1[0][...], rights[0][yr][...])
            first = first + dot_rows(n1[1][...], rights[1][yr][...])
            second = dot_rows(ml[0][...], outer[0][yr]) + dot_rows(ml[1][...], outer[1][yr])
            shared = first[:, 4 * PAIR :] + second[:, 0:PAIR]
            parts = [(0, first[:, 0 : 4 * PAIR]), (4 * PAIR, shared), (5 * PAIR, second[:, PAIR:])]
            matrix.store(place, parts, yr, order, outs[0])

    arrays = list(lefts) + list(outer_lefts) + list(outer_rights) + list(rights[0]) + list(rights[1])
    outs = matrix.grad_shapes(6 * PAIR)
    (grad,) = call(kernel, "attention_gradient", scalars, arrays, outs)
    return matrix.grad_result(grad, order)


def input_backward(scalars, arrays, parts):
    count, width = arrays[0].shape

    def kernel(scalars, arrays, outs):
        (place,) = scalars
        x_ref, mg_ref, norm_ref, weight, sums_ref, ubg_ref, heads_ref = arrays[:7]
        out_ref, lines_ref = outs
        total = jnp.zeros((2, width), f32)
        for at in row_blocks(count):
            one = sum(
                dot_cols(part[at, :], weight[step, :, 0 : 5 * PAIR])
                for step, part in enumerate(arrays[7:])
            )
            normed, inverse = moments(up(x_ref[at, :]))
            out_ref[at, :] = mg_ref[at, :] + norm_back(one, normed, inverse, norm_ref[0:1, :])
            lines = [jnp.sum(one * normed, axis=0, keepdims=True), jnp.sum(one, axis=0, keepdims=True)]
            total = total + join(*lines)
        lines_ref[0:8, :] = join(total, sums_ref[...], jnp.zeros((2, width), f32))
        for step in range(4):
            lines_ref[pl.ds(8 + block_of(place, step), 1), :] = ubg_ref[step]
        lines_ref[12:16, :] = heads_ref[...]

    outs = [shape((count, width), f32), shape((16, width), f32)]
    return call(kernel, "input_backward", scalars, list(arrays) + list(parts), outs)


def adam_step(weight, first, second, grad, rate, decay):
    first_new = beta_first * first + (1.0 - beta_first) * grad
    second_new = beta_second * second + (1.0 - beta_second) * grad * grad
    first_hat = first_new / (1.0 - beta_first**STEP)
    second_hat = second_new / (1.0 - beta_second**STEP)
    weight_new = weight - rate * (first_hat / (jnp.sqrt(second_hat) + adam_eps) + decay * weight)
    return (weight_new, first_new, second_new)


def pack_tiles(parts):
    q, k, v, o = ((part[:, :PAIR], part[:, PAIR:]) for part in parts)
    tail3 = jnp.concatenate([q[1], k[1]], axis=1)
    tail4 = jnp.concatenate([v[1], o[1]], axis=1)
    return q[0], k[0], v[0], tail3, tail4, o[0]


def own_columns(plan, place, value):
    width = value.shape[1]
    columns = width // math.prod(plan.dims)
    group = (place[0] * plan.dims[1] + place[1]) * 4 + rank_of(place)
    turn = lax.rem(width - group * columns, width)
    return pltpu.roll(value, turn, axis=1)[:, 0:columns]


def hold(plan, scalars, params, matrices):
    rows, cols = matrices[2][0].shape
    width = params[0].shape[1]
    columns = width // math.prod(plan.dims)

    def kernel(scalars, state, outs, small_ref):
        for t in range(3):
            parts = [state[t][i] for i in range(3)] + [state[3 + t][...]]
            for i, part in enumerate(pack_tiles(parts)):
                outs[0][t, :, i * PAIR : (i + 1) * PAIR] = part
            outs[0][3 + t] = state[6 + t][...]
            outs[0][6 + t] = state[9 + t][...]
        small_ref[0:8, :] = state[13][...]
        small_ref[8:12, :] = state[12][...]
        small_ref[12:16, :] = state[12][...]
        own = own_columns(plan, scalars[0], small_ref[...])
        outs[1][...] = own[8:12]
        outs[2][...] = own[0:8]

    outs = [shape((9, rows, cols), f32), shape((4, columns), f32), shape((8, columns), f32)]
    state = [value for group in matrices for value in group] + list(params)
    scratch = [pltpu.VMEM((16, width), f32)]
    return call(kernel, "hold", scalars, [], outs, scratch, 12, state, micros=10)


def total_gradients(plan, scalars, parts, lines):
    rows, cols = parts[0][0].shape[1:]
    width = lines[0].shape[2]
    devices = math.prod(plan.dims)
    columns = width // devices
    counts = [len(part) for part in parts]
    held = sum(counts)

    def kernel(scalars, arrays, outs, small_ref):
        at, squares = 0, jnp.zeros((1, 1), f32)

        def square(value):
            return jnp.sum(jnp.sum(value * value, axis=1, keepdims=True), axis=0, keepdims=True)

        for m, n in enumerate(counts):
            total = up(arrays[at][0])
            for i in range(1, n):
                total = total + up(arrays[at + i][0])
            outs[0][m] = total
            squares = squares + square(total)
            at += n
        sums = arrays[held][0]
        for ref in arrays[held + 1 :]:
            sums = sums + ref[0]
        size = width // 4
        small_ref[0:4, :] = sums[0:4]
        small_ref[4:8, :] = sums[8:12]
        for t in range(2):
            for mp in range(4):
                line = sums[12 + mp : 13 + mp, 2 * PAIR * t : 2 * PAIR * t + size]
                small_ref[8 + t : 9 + t, mp * size : (mp + 1) * size] = line
        small_ref[10:12, :] = sums[4:6]
        small_ref[12:16, :] = jnp.zeros((4, width), f32)
        own = own_columns(plan, scalars[0], small_ref[...])
        squares = squares + square(own)
        outs[1][...] = jnp.broadcast_to(squares[None], (devices, 1, 1))
        outs[2][...] = own[0:4]
        outs[3][...] = own[4:12]

    arrays = [part for group in parts for part in group] + list(lines)
    outs = [shape((3, rows, cols), f32), shape((devices, 1, 1), f32)]
    outs += [shape((n, columns), f32) for n in (4, 8)]
    scratch = [pltpu.VMEM((16, width), f32)]
    return call(kernel, "total_gradients", scalars, arrays, outs, scratch, 12)


def update(squares, grads, state, small, smalls, shapes):
    def kernel(scalars, arrays, outs):
        norm = jnp.sqrt(jnp.sum(arrays[0][...], axis=0))
        factor = jnp.minimum(1.0, clip_limit / (norm + 1e-06))
        outs[0][...] = norm
        grad_ref, state_ref = arrays[1:3]

        def step(weight, first, second, grad, rate, decay):
            grad = grad * factor
            new, first, second = adam_step(weight, first, second, grad, rate, decay)
            return [grad, new, first, second, new.astype(bf16)]

        for m in range(3):
            values = [state_ref[3 * m + t] for t in range(3)] + [grad_ref[m]]
            values = step(*values, matrix_rate, matrix_decay)
            for i, value in enumerate(values):
                if m:
                    outs[6 + 5 * m + i][...] = value
                    continue
                tiles = [value[:, t * PAIR : (t + 1) * PAIR] for t in range(6)]
                wide = [tiles[3], tiles[4]] if value.dtype == f32 else [up(t) for t in tiles[3:5]]
                tails = [part for t in wide for part in (t, swap(t))]
                for t in range(4):
                    ref = outs[1 + i] if t < 3 else outs[6 + i]
                    head = tiles[t] if t < 3 else tiles[5]
                    tail = tails[t][:, :HEAD].astype(value.dtype)
                    if t < 3:
                        ref[t, :, :PAIR] = head
                        ref[t, :, PAIR:] = tail
                    else:
                        ref[:, :PAIR] = head
                        ref[:, PAIR:] = tail
        for m in range(2):
            weight, first, second = (ref[...] for ref in arrays[5 + 3 * m : 8 + 3 * m])
            values = step(weight, first, second, arrays[3 + m][...], small_rate, 0.0)
            for i in range(4):
                outs[21 + 4 * m + i][...] = values[i]

    arrays = [squares, grads, state] + list(small)
    outs = [shape((1, 1), f32)]
    for dims in shapes:
        outs += [shape(dims, f32)] * 4 + [shape(dims, bf16)]
    for group in smalls:
        arrays += list(group)
        outs += [shape(group[0].shape, f32)] * 4
    return call(kernel, "update", [], arrays, outs)


def body(
    plan,
    block_input,
    cotangent,
    lengths,
    attn_input,
    attn_input_first,
    attn_input_second,
    attn_output,
    attn_output_first,
    attn_output_second,
    mlp_up,
    mlp_up_first,
    mlp_up_second,
    mlp_down,
    mlp_down_first,
    mlp_down_second,
    norm_params,
    norm_first,
    norm_second,
    bias_params,
    bias_first,
    bias_second,
):
    width = norm_params.shape[1]
    place = jnp.stack([lax.axis_index(axis) for axis in AXES]).astype(jnp.int32)
    matrix = Matrix(plan, place, width, attn_input.shape[0])
    send, send_z = plan.send, plan.send_z
    az, za = plan.order_az, plan.order_za
    low_bits, high_bits = plan.zbits[:2], plan.zbits[2:]
    def turned(value):
        return value.transpose(1, 0, 2)

    attn = pack_attention(turned(attn_input), attn_output)
    attn_z = [send_z(attn, mask) for mask in (1, 2, 3)]
    above, down = pack_mlp(mlp_up, mlp_down)
    above_z = send_z(above, 1)
    down_a = send(down, plan.a)
    n1, grad_low, head_bias = prepare(
        [place, lengths], [block_input, cotangent, norm_params, bias_params]
    )
    attn, *attn_z, above, above_z, down, down_a, n1, grad_low, head_bias = sync(
        attn, *attn_z, above, above_z, down, down_a, n1, grad_low, head_bias
    )

    attn, above, down = joined(
        "join_one", matrix, [attn, *attn_z], [above, above_z], [down, down_a]
    )
    attn = plan.spread(attn, high_bits)
    attn_a, attn_b = send(attn, plan.a), send(attn, plan.b)
    above_z = send_z(above, 2)
    attn_c = [send(attn, plan.core)]
    (above,) = joined("join_two", matrix, [above, above_z], micros=5)
    above = plan.spread(above, high_bits)
    above_a = send(above, plan.a)
    attn, attn_a, attn_b, above, down, *attn_c = sync(
        attn, attn_a, attn_b, above, down, *attn_c
    )

    def blocks(planes, order, *fixed):
        return [
            (array, plan.slots(pc, order, **what))
            for pc, arrays in enumerate(planes)
            for array, what in zip(arrays, fixed)
        ]

    corners = [dict(br=0, ar=0), dict(br=0, ar=1), dict(br=1, ar=0), dict(br=1, ar=1)]
    attn_ab = send(attn_a, plan.b)
    down_z = send_z(down, 2)
    attn_c += [send(attn_a, plan.core), send(attn_b, plan.core)]
    attn_ab, above, above_a, down, down_z, *attn_c[1:] = sync(
        attn_ab, above, above_a, down, down_z, *attn_c[1:]
    )

    (down,) = joined("join_three", matrix, [down, down_z])
    above_b = send(above, plan.b)
    above_ab = send(above_a, plan.b)
    down_z = send_z(down, 1)
    above_c = [send(piece, plan.core) for piece in (above, above_a)]
    attn_c.append(send(attn_ab, plan.core))
    pieces = blocks([[attn, attn_a, attn_b, attn_ab], attn_c], plan.plain, *corners)
    pieces, fill = matrix.weight_args(pieces)
    q, k, v, weight_attn = project([place], [n1, head_bias], pieces, fill)
    probs, att_own, att_other, middle, n2 = attend(
        [place, lengths], [block_input, norm_params, bias_params, q, k, v, weight_attn]
    )
    above, above_a, above_b, above_ab, down, down_z, att_other, n2, *above_c = sync(
        above, above_a, above_b, above_ab, down, down_z, att_other, n2, *above_c
    )

    (down,) = joined("join_four", matrix, [down, down_z])
    down = plan.spread(down, high_bits)
    down_b = send(down, plan.b)
    above_c += [send(piece, plan.core) for piece in (above_b, above_ab)]
    pieces = blocks([[above, above_a, above_b, above_ab], above_c], plan.plain, *corners)
    pieces, fill = matrix.weight_args(pieces)
    *hidden, slope, weight_up = mlp_forward([place], [n2, bias_params], pieces, fill)
    grad_low_c = send(grad_low, plan.core)
    hidden_c = [send(part, plan.core) for part in hidden[2:]]

    down_g = gradient(
        matrix, za, "down_gradient", [place], [grad_low, grad_low_c], [hidden[:2], hidden_c]
    )
    down_b, down_g, n2, att_other = sync(down_b, down_g, n2, att_other)

    n2_c = send(n2, plan.core)
    down_c = [send(down, plan.core), send(down_b, plan.core)]
    pieces = blocks([[down, down_b], down_c], za, dict(br=0), dict(br=1))
    pieces, fill = matrix.weight_args(pieces)
    half = down_g.shape[0] // 2
    down_gb = send(down_g[half:], plan.b)
    *grads, up_bias_grad, weight_down = expanded_backward(
        [place], [grad_low, slope], pieces, fill
    )
    grads_c = [send(part, plan.core) for part in grads[2:]]
    middle_grad, middle_low, sums_two = middle_backward(
        [middle, grad_low, norm_params, weight_up], grads
    )
    up_g = gradient(matrix, az, "up_gradient", [place], [n2, n2_c], [grads[:2], grads_c])
    n1_c, att_c = send(n1, plan.core), send(att_other, plan.core)
    up_g, middle_low, n1_c, att_c = sync(up_g, middle_low, n1_c, att_c)

    up_gb = send(up_g[half:], plan.b)
    terms = [down_g, down_gb]
    if high_bits:
        terms = [plan.fold(up(down_g[:half]) + up(down_gb), high_bits)]
    down_s, down_0 = added(
        "add_one",
        matrix,
        (4, f32, [(part, 0) for part in terms]),
        (4, bf16, [(part, 4) for part in terms]),
    )
    down_s, down_0, middle_low = sync(down_s, down_0, middle_low)

    down_z = send_z(down_0, 1)
    middle_low_c = send(middle_low, plan.core)
    *joint, head_lines = attention_backward(
        [place], [middle_low, q, k, v, probs, weight_attn]
    )
    joint_c = [send(part, plan.core) for part in joint[2:]]
    down_s, down_0, down_1 = added(
        "add_down",
        matrix,
        (2, f32, [(down_s, 0), (down_z, 0)]),
        (1, bf16, [(down_s, 2), (down_z, 2)]),
        (1, bf16, [(down_s, 3), (down_z, 3)]),
        micros=2,
    )
    middle_low_c, up_gb, down_s, down_0, down_1, *rest = sync(
        middle_low_c, up_gb, down_s, down_0, down_1, *joint, *joint_c
    )
    joint, joint_c = rest[:4], rest[4:]

    fourth = half // 2
    (up_0,) = added("add_two", matrix, (fourth, bf16, [(up_g, fourth), (up_gb, fourth)]))
    up_ga = send(up_0, plan.a)
    attn_g = attention_gradient(
        matrix, az, [place], [n1, n1_c], [joint[:2], joint_c],
        [middle_low, middle_low_c], [att_own, att_c],
    )
    attn_gb = send(attn_g[half:], plan.b)
    down_z0, down_z1 = send_z(down_0, 2), send_z(down_1, 2)
    input_grad, lines = input_backward(
        [place],
        [block_input, middle_grad, norm_params, weight_attn, sums_two, up_bias_grad, head_lines],
        joint,
    )
    lines = lines[None]
    terms = [up_g, up_gb, up_ga]
    if high_bits:
        terms = [plan.fold(sum(up(part[:fourth]) for part in terms), high_bits)]
    up_s, up_0 = added(
        "add_three",
        matrix,
        (2, f32, [(part, 0) for part in terms]),
        (2, bf16, [(part, 2) for part in terms]),
    )
    up_z = send_z(up_0, 1)
    lines, up_s = sync(lines, up_s)
    lines_a = send(lines, plan.a)
    (lines,) = added("add_lines", matrix, (1, f32, [(lines, 0), (lines_a, 0)]))
    lines_z = send_z(lines, 1)
    matrices = (
        (turned(attn_input), turned(attn_input_first), turned(attn_input_second)),
        (attn_output, attn_output_first, attn_output_second),
        (mlp_up, mlp_up_first, mlp_up_second),
        (mlp_down, mlp_down_first, mlp_down_second),
    )
    up_s, norms = sync(up_s, norm_params)
    down_z0, norms = sync(down_z0, norms)
    state, own_norm, own_bias = hold(plan, [place], [norms, bias_params], matrices)
    attn_gb, down_z1, up_z, lines_z, state, input_grad = sync(
        attn_gb, down_z1, up_z, lines_z, state, input_grad
    )

    attn_0, down_s, down_0, up_s, up_0, lines = added(
        "add_four",
        matrix,
        (fourth, bf16, [(attn_g, fourth), (attn_gb, fourth)]),
        (1, f32, [(down_s, 0), (down_z0, 0)]),
        (1, bf16, [(down_s, 1), (down_z1, 0)]),
        (1, f32, [(up_s, 0), (up_z, 0)]),
        (1, bf16, [(up_s, 1), (up_z, 1)]),
        (1, f32, [(lines, 0), (lines_z, 0)]),
    )
    attn_ga = send(attn_0, plan.a)
    up_z = send_z(up_0, 2)
    lines_z = send_z(lines, 2)
    for bit in high_bits:
        lines = lines + lines_z
        lines_z = send_z(lines, bit)
    block_output = block_out([middle, bias_params, weight_down], hidden)
    attn_ga, up_z, lines_z, down_0, block_output = sync(
        attn_ga, up_z, lines_z, down_0, block_output
    )

    terms = [attn_g, attn_gb, attn_ga]
    if high_bits:
        terms = [plan.fold(sum(up(part[:fourth]) for part in terms), high_bits)]
    attn_s, *attn_0, lines = added(
        "add_five",
        matrix,
        (1, f32, [(part, 0) for part in terms]),
        (1, bf16, [(part, 1) for part in terms]),
        (1, bf16, [(part, 2) for part in terms]),
        (1, bf16, [(part, 3) for part in terms]),
        (1, f32, [(lines, 0), (lines_z, 0)]),
    )
    attn_z = [send_z(part, mask) for part, mask in zip(attn_0, (2, 1, 3))]
    down_ga = send(down_0, plan.a)
    rest = [send(lines, perm) for perm in (plan.b, plan.core, plan.cross)]
    state, down_ga, *rest = sync(state, down_ga, *rest, *attn_z)
    rest, attn_z = rest[:3], rest[3:]

    sums, squares, norm_sum, bias_sum = total_gradients(
        plan, [place], [[attn_s, *attn_z], [up_s, up_z], [down_s, down_ga]], [lines, *rest]
    )
    squares = lax.all_to_all(squares, AXES, 0, 0, tiled=True)
    grad_norm, *results = update(
        squares,
        sums,
        state,
        [norm_sum, bias_sum],
        ((own_norm, norm_first, norm_second), (own_bias, bias_first, bias_second)),
        [group[0].shape for group in matrices],
    )
    results[:5] = [turned(value) for value in results[:5]]
    return (block_output, input_grad, grad_norm[0, 0], *results)


def solution(mesh):
    dp, mp = mesh.shape["dp"], mesh.shape["mp"]
    dims = (dp // 2, 2, mp // 2, 2)
    fine = Mesh(np.asarray(mesh.devices).reshape(dims), AXES)
    plan = Plan(dims)
    d, m = ("z", "x"), ("y", "c")
    every = d + m
    rows = P(every, None)
    cube = P(d, None, m)
    flat = P(d, m)
    small = P(None, every)
    return jax.shard_map(
        functools.partial(body, plan),
        mesh=fine,
        in_specs=(rows, rows, P(d)) + (cube,) * 3 + (flat,) * 9 + (P(), small, small) * 2,
        out_specs=(rows, rows, P()) + (cube,) * 5 + (flat,) * 15 + (small,) * 8,
        check_vma=False,
    )
```

```python
import functools
import math

import jax
import jax.numpy as jnp
import numpy as np
from jax import lax
from jax.experimental import pallas as pl
from jax.experimental.pallas import tpu as pltpu
from jax.sharding import Mesh, PartitionSpec as P

HEAD = 64
STEP = 10

norm_eps = 1e-06
beta_first = 0.5
beta_second = 0.5
adam_eps = 1e-08
matrix_rate = 0.03
small_rate = 0.3
matrix_decay = 0.01
clip_limit = 1.0
masked_score = -1e30

f32 = jnp.float32
bf16 = jnp.bfloat16
AXES = ("z", "x", "y", "c")
PAIR = 2 * HEAD
GELU_A = math.sqrt(2.0 / math.pi)
GELU_B = 0.044715


def sync(*values):
    return lax.optimization_barrier(values)


def up(value):
    return value.astype(f32)


def join(*values):
    return jnp.concatenate(values, axis=0)


class Plan:
    def __init__(self, dims):
        self.dims = dims
        self.z = dims[0]
        self.zbits = [1 << i for i in range(int(math.log2(self.z)))]
        self.places = [tuple(p) for p in np.ndindex(*dims)]
        self.index = {p: i for i, p in enumerate(self.places)}
        self.core = self.perm(lambda z, x, y, c: (z, x, y, 1 - c))
        self.a = self.perm(lambda z, x, y, c: (z, x ^ (1 - c), y ^ c, c))
        self.b = self.perm(lambda z, x, y, c: (z, x ^ c, y ^ (1 - c), c))
        self.cross = self.perm(lambda z, x, y, c: (z, x ^ c, y ^ (1 - c), 1 - c))
        each = [(br, ar) for br in range(2) for ar in range(2)]
        turned = sorted(range(self.z), key=self.turn)
        self.plain = [(br, ar, zr) for br, ar in each for zr in range(self.z)]
        self.order_az = [(br, ar, zr) for br, ar in each for zr in turned]
        self.order_za = [(br, ar, zr) for br in range(2) for zr in turned for ar in range(2)]

    def turn(self, zr):
        return (zr >> 2) * 4 + (zr & 1) * 2 + ((zr >> 1) & 1)

    def perm(self, move):
        return [(self.index[p], self.index[move(*p)]) for p in self.places]

    def zmove(self, mask):
        return self.perm(lambda z, x, y, c: (z ^ mask, x, y, c))

    def send(self, value, perm):
        return lax.ppermute(value, AXES, perm)

    def send_z(self, value, mask):
        return self.send(value, self.zmove(mask))

    def spread(self, block, bits):
        for bit in bits:
            block = join(block, self.send_z(block, bit))
        return block

    def fold(self, total, bits):
        for bit in bits[::-1]:
            half = total.shape[0] // 2
            total = total[:half] + up(self.send_z(total[half:].astype(bf16), bit))
        return total

    def table(self, place, slots):
        pc, br, ar, zr = (jnp.asarray(v, jnp.int32) for v in zip(*slots))
        core = place[3] ^ pc
        x = place[1] ^ jnp.where(core == 0, ar, br)
        yr = jnp.where(core == 0, br, ar)
        dp = (place[0] ^ zr) * self.dims[1] + x
        return (2 * pc + yr) * (self.z * self.dims[1]) + dp

    def slots(self, pc, order, **fixed):
        names = ("br", "ar", "zr")
        return [
            (pc,) + slot
            for slot in order
            if all(slot[names.index(name)] == value for name, value in fixed.items())
        ]


def dot(left, right):
    return lax.dot_general(left, right, (((1,), (0,)), ((), ())), preferred_element_type=f32)


def dot_cols(left, right):
    return lax.dot_general(left, right, (((1,), (1,)), ((), ())), preferred_element_type=f32)


def dot_rows(left, right):
    return lax.dot_general(left, right, (((0,), (0,)), ((), ())), preferred_element_type=f32)


def low_lanes(shape):
    return lax.broadcasted_iota(jnp.int32, shape, len(shape) - 1) < HEAD


def swap(value):
    return pltpu.roll(value, HEAD, axis=1)


def moments(rows):
    center = jnp.mean(rows, axis=1, keepdims=True)
    centered = rows - center
    spread = jnp.mean(centered * centered, axis=1, keepdims=True)
    inverse = lax.rsqrt(spread + norm_eps)
    return centered * inverse, inverse


def norm_back(grad_rows, normed, inverse, gain):
    scaled = grad_rows * gain
    return inverse * (
        scaled
        - jnp.mean(scaled, axis=1, keepdims=True)
        - normed * jnp.mean(scaled * normed, axis=1, keepdims=True)
    )


class Matrix:
    def __init__(self, plan, place, width, rows):
        self.plan = plan
        self.place = place
        self.width = width
        self.rows = rows
        self.direct = rows % 16 == 0
        self.blocks_dp = plan.dims[0] * plan.dims[1]

    def whole(self, pieces):
        order = [slot for _, slots in pieces for slot in slots]
        blocks = join(*[array for array, _ in pieces])
        turn = jnp.argsort(self.plan.table(self.place, order))
        return jnp.take(blocks, turn, axis=0).reshape(4, self.width, blocks.shape[-1])

    def place_blocks(self, place, refs, slots, weight):
        for ref, of_ref in zip(refs, slots):
            for i, (pc, br, ar, zr) in enumerate(of_ref):
                core = place[3] ^ pc
                xr = jnp.where(core == 0, ar, br)
                yr = jnp.where(core == 0, br, ar)
                dp = (place[0] ^ zr) * self.plan.dims[1] + (place[1] ^ xr)
                row = pl.multiple_of(dp * self.rows, 16)
                weight[2 * pc + yr, pl.ds(row, self.rows), :] = ref[i]

    def weight_args(self, pieces):
        if self.direct:
            slots = [of for _, of in pieces]
            return [array for array, _ in pieces], functools.partial(self.fill, slots)
        return [self.whole(pieces)], lambda place, refs, weight: self.copy(refs, weight)

    def fill(self, slots, place, refs, weight):
        self.place_blocks(place, refs, slots, weight)

    def copy(self, refs, weight):
        weight[...] = refs[0][...]

    def grad_shapes(self, cols):
        if self.direct:
            return [jax.ShapeDtypeStruct((4 * self.plan.z, self.rows, cols), bf16)]
        return [jax.ShapeDtypeStruct((2, self.width, cols), bf16)]

    def store(self, place, parts, yr, order, out):
        if not self.direct:
            for at, part in parts:
                out[yr, :, at : at + part.shape[1]] = part.astype(bf16)
            return
        z = self.plan.z
        core = place[3]
        for dp in range(self.blocks_dp):
            zr = place[0] ^ (dp // self.plan.dims[1])
            xr = place[1] ^ (dp % self.plan.dims[1])
            ar = jnp.where(core == 0, xr, yr)
            br = jnp.where(core == 0, yr, xr)
            zi = self.plan.turn(zr)
            if order is self.plan.order_az:
                slot = br * (2 * z) + ar * z + zi
            else:
                slot = br * (2 * z) + zi * 2 + ar
            rows = slice(dp * self.rows, (dp + 1) * self.rows)
            for at, part in parts:
                out[slot, :, at : at + part.shape[1]] = part[rows, :].astype(bf16)

    def grad_result(self, grad, order):
        if self.direct:
            return grad
        whole = grad.reshape(2 * self.blocks_dp, self.rows, grad.shape[-1])
        table = self.plan.table(self.place, [(0,) + slot for slot in order])
        return jnp.take(whole, table, axis=0)


def call(kernel, name, scalars, arrays, outs, scratch=(), mib=16, hbm=(), micros=0):
    scalars, arrays, outs = list(scalars), list(arrays), list(outs)
    hbm = [pltpu.with_memory_space_constraint(part, pltpu.HBM) for part in hbm]
    counts = (len(scalars), len(arrays), len(hbm), len(outs), len(hbm), min(len(hbm), 1))

    def split(*refs):
        parts, at = [], 0
        for n in counts:
            parts.append(list(refs[at : at + n]))
            at += n
        copies = [
            pltpu.make_async_copy(source, target, parts[5][0].at[i])
            for i, (source, target) in enumerate(zip(parts[2], parts[4]))
        ]
        for copy in copies:
            copy.start()
        for copy in copies:
            copy.wait()
        kernel(parts[0], parts[1] + parts[4], parts[3], *refs[at:])

    vmem = pl.BlockSpec(memory_space=pltpu.VMEM)
    specs = [pl.BlockSpec(memory_space=pltpu.SMEM)] * len(scalars) + [vmem] * len(arrays)
    specs += [pl.BlockSpec(memory_space=pltpu.HBM)] * len(hbm)
    own = [pltpu.VMEM(part.shape, part.dtype) for part in hbm]
    if hbm:
        own.append(pltpu.SemaphoreType.DMA((len(hbm),)))
    return pl.pallas_call(
        split,
        name=name,
        out_shape=outs,
        in_specs=specs,
        out_specs=[vmem] * len(outs),
        scratch_shapes=own + list(scratch),
        compiler_params=pltpu.CompilerParams(vmem_limit_bytes=mib * 2**20),
        cost_estimate=pl.CostEstimate(
            flops=1 + int(micros * 1.15e9), bytes_accessed=1, transcendentals=0
        ),
    )(*scalars, *arrays, *hbm)


def shape(dims, kind):
    return jax.ShapeDtypeStruct(tuple(dims), kind)


def rank_of(place):
    return place[2] * 2 + place[3]


def block_of(place, step):
    return rank_of(place) ^ (2 * (step % 2) + step // 2)


def row_blocks(count):
    size = 256 if count % 256 == 0 else count
    return [slice(r, r + size) for r in range(0, count, size)]


def joined(name, matrix, *groups, micros=0):
    if not matrix.direct:
        return [join(*group) for group in groups]

    def kernel(scalars, arrays, outs):
        at = 0
        for group, out in zip(groups, outs):
            row = 0
            for _ in group:
                for i in range(arrays[at].shape[0]):
                    out[row] = arrays[at][i]
                    row += 1
                at += 1

    outs = []
    for group in groups:
        rows = sum(part.shape[0] for part in group)
        outs.append(shape((rows,) + group[0].shape[1:], group[0].dtype))
    arrays = [part for group in groups for part in group]
    return call(kernel, name, [], arrays, outs, mib=8, micros=micros)


def added(name, matrix, *sums, micros=0):
    sums = [each if isinstance(each, list) else [each] for each in sums]
    if not matrix.direct:
        return [
            join(*[
                sum(up(part[at : at + count]) for part, at in terms).astype(kind)
                for count, kind, terms in each
            ])
            for each in sums
        ]
    arrays = []
    for each in sums:
        for _, _, terms in each:
            for part, _ in terms:
                if not any(part is other for other in arrays):
                    arrays.append(part)

    def where(part):
        return next(i for i, other in enumerate(arrays) if part is other)

    def kernel(scalars, refs, outs):
        for each, out in zip(sums, outs):
            row = 0
            for count, kind, terms in each:
                for i in range(count):
                    total = up(refs[where(terms[0][0])][terms[0][1] + i])
                    for part, at in terms[1:]:
                        total = total + up(refs[where(part)][at + i])
                    out[row] = total.astype(kind)
                    row += 1

    outs = [
        shape((sum(one[0] for one in each),) + each[0][2][0][0].shape[1:], each[0][1])
        for each in sums
    ]
    return call(kernel, name, [], arrays, outs, mib=8, micros=micros)


def pack_attention(inputs, output):
    rows = output.shape[0]

    def kernel(scalars, arrays, outs):
        in_ref, out_ref = arrays
        parts = [in_ref[t].astype(bf16) for t in range(3)] + [out_ref[...].astype(bf16)]
        for i, part in enumerate(pack_tiles(parts)):
            outs[0][0, :, i * PAIR : (i + 1) * PAIR] = part

    outs = [shape((1, rows, 6 * PAIR), bf16)]
    return call(kernel, "pack_attention", [], [], outs, mib=8, hbm=[inputs, output])[0]


def pack_mlp(above, down):
    def kernel(scalars, arrays, outs):
        for ref, out in zip(arrays, outs):
            out[0] = ref[...].astype(bf16)

    outs = [shape((1,) + above.shape, bf16)] * 2
    return call(kernel, "pack_mlp", [], [], outs, mib=8, hbm=[above, down])


def prepare(scalars, hbm):
    count, width = hbm[0].shape
    units = hbm[3].shape[0] - 4

    def kernel(scalars, arrays, outs):
        place, lens = scalars
        x_ref, cot_ref, norm_ref, bias_ref = arrays
        n1_ref, glow_ref, head_ref = outs
        size = width // 4
        for t in range(2):
            for mp in range(4):
                line = bias_ref[units + t : units + t + 1, mp * size : (mp + 1) * size]
                head_ref[4 * t + mp : 4 * t + mp + 1, 0:size] = line
        gain1, shift1 = norm_ref[0:1, :], norm_ref[1:2, :]
        for at in row_blocks(count):
            normed, _ = moments(up(x_ref[at, :]))
            n1_ref[at, :] = (normed * gain1 + shift1).astype(bf16)
        captions = lens.shape[0] // 4
        length = count // captions
        for j in range(captions):
            at = slice(j * length, (j + 1) * length)
            limit = lens[rank_of(place) * captions + j]
            keep = lax.broadcasted_iota(jnp.int32, (length, width), 0) < limit
            glow_ref[at, :] = jnp.where(keep, up(cot_ref[at, :]), 0.0).astype(bf16)

    outs = [shape((count, width), bf16)] * 2 + [shape((8, 2 * PAIR), f32)]
    return call(kernel, "prepare", scalars, [], outs, hbm=hbm)


def project(scalars, arrays, pieces, fill):
    count, width = arrays[0].shape

    def kernel(scalars, arrays, outs):
        (place,) = scalars
        n1_ref, head_bias = arrays[:2]
        q_ref, k_ref, v_ref, weight = outs
        fill(place, arrays[2:], weight)
        bias = []
        for step in range(4):
            mp = block_of(place, step)
            bias.append((head_bias[pl.ds(mp, 1), :], head_bias[pl.ds(mp + 4, 1), :]))
        low_line = low_lanes((1, PAIR))
        for yr in range(2):
            pair = 4 + yr
            third = [
                jnp.where(low_line, bias[yr][t][:, PAIR:], swap(bias[2 + yr][t][:, PAIR:]))
                for t in range(2)
            ]
            for at in row_blocks(count):
                joined = []
                for step in (yr, 2 + yr):
                    part = dot(n1_ref[at, :], weight[step, :, 0 : 5 * PAIR])
                    query_bias, value_bias = bias[step]
                    q_ref[step, at, :] = (part[:, 0:PAIR] + query_bias[:, :PAIR]).astype(bf16)
                    k_ref[step, at, :] = part[:, PAIR : 2 * PAIR].astype(bf16)
                    v_ref[step, at, :] = (part[:, 2 * PAIR : 3 * PAIR] + value_bias[:, :PAIR]).astype(bf16)
                    joined.append((part[:, 3 * PAIR : 4 * PAIR], part[:, 4 * PAIR :]))
                (own3, own4), (other3, other4) = joined
                low = low_lanes(own3.shape)
                query = jnp.where(low, own3, swap(other3)) + third[0]
                value = jnp.where(low, own4, swap(other4)) + third[1]
                q_ref[pair, at, :] = query.astype(bf16)
                k_ref[pair, at, :] = jnp.where(low, swap(own3), other3).astype(bf16)
                v_ref[pair, at, :] = value.astype(bf16)

    heads = shape((6, count, PAIR), bf16)
    outs = [heads, heads, heads, shape((4, width, 6 * PAIR), bf16)]
    return call(kernel, "project", scalars, list(arrays) + list(pieces), outs)


def attend(scalars, arrays):
    count, width = arrays[0].shape
    blocks = count // PAIR

    def kernel(scalars, arrays, outs, att):
        place, lens = scalars
        x_ref, norm_ref, bias_ref, q_ref, k_ref, v_ref, weight = arrays
        p_ref, own_ref, other_ref, mid_ref, n2_ref = outs
        first = rank_of(place) * (2 * blocks)
        lane = lax.broadcasted_iota(jnp.int32, (2 * PAIR, PAIR), 1)
        line = lax.broadcasted_iota(jnp.int32, (2 * PAIR, PAIR), 0)
        same = ((line // HEAD) % 2) == (lane // HEAD)
        low = low_lanes((PAIR, PAIR))
        zero = jnp.zeros((PAIR, PAIR), bf16)

        def block(r, _):
            at = pl.ds(pl.multiple_of(r * PAIR, PAIR), PAIR)
            limit = jnp.where(lane < HEAD, lens[first + 2 * r], lens[first + 2 * r + 1] + HEAD)
            keep = same & (lane < limit)
            for pair in range(6):
                query = q_ref[pair, at, :]
                stacked = join(jnp.where(low, query, zero), jnp.where(low, zero, query))
                scores = dot_cols(stacked, k_ref[pair, at, :]) * (HEAD ** (-0.5))
                scores = jnp.where(keep, scores, masked_score)
                expo = jnp.exp(scores - jnp.max(scores, axis=1, keepdims=True))
                probs = (expo / jnp.sum(expo, axis=1, keepdims=True)).astype(bf16)
                p_ref[pair, r] = probs
                out = dot(probs, v_ref[pair, at, :])
                att[pair, at, :] = jnp.where(low, out[0:PAIR], out[PAIR:])
            return 0

        lax.fori_loop(0, blocks, block, 0, unroll=2)
        low_all = low_lanes((count, PAIR))
        for step in range(4):
            pc, yr = step // 2, step % 2
            part_ref = (own_ref, other_ref)[pc]
            third = att[4 + yr] if pc else swap(att[4 + yr])
            part_ref[yr, :, 0:PAIR] = jnp.where(low_all, 0.0, third).astype(bf16)
            part_ref[yr, :, PAIR:] = att[step].astype(bf16)
        out_bias = bias_ref[bias_ref.shape[0] - 2 : bias_ref.shape[0] - 1, :]
        gain2, shift2 = norm_ref[2:3, :], norm_ref[3:4, :]
        for at in row_blocks(count):
            branch = up(x_ref[at, :]) + out_bias
            for step in range(4):
                part_ref = (own_ref, other_ref)[step // 2]
                branch = branch + dot_cols(part_ref[step % 2, at, :], weight[step, :, 4 * PAIR :])
            mid_ref[at, :] = branch
            normed, _ = moments(branch)
            n2_ref[at, :] = (normed * gain2 + shift2).astype(bf16)

    part = shape((2, count, 2 * PAIR), bf16)
    outs = [
        shape((6, blocks, 2 * PAIR, PAIR), bf16),
        part,
        part,
        shape((count, width), f32),
        shape((count, width), bf16),
    ]
    return call(kernel, "attend", scalars, arrays, outs, [pltpu.VMEM((6, count, PAIR), f32)])


def mlp_forward(scalars, arrays, pieces, fill):
    count, width = arrays[0].shape

    def kernel(scalars, arrays, outs):
        (place,) = scalars
        n2_ref, bias_ref = arrays[:2]
        gp_ref, weight = outs[4:]
        fill(place, arrays[2:], weight)
        for step in range(4):
            bias = bias_ref[pl.ds(block_of(place, step), 1), :]
            for at in row_blocks(count):
                value = dot(n2_ref[at, :], weight[step]) + bias
                square = value * value
                t = jnp.tanh((GELU_A * value) * (1.0 + GELU_B * square))
                half = 0.5 * (1.0 + t)
                outs[step][at, :] = (value * half).astype(bf16)
                slope = half + (0.5 * GELU_A) * value * (1.0 - t * t) * (1.0 + (3.0 * GELU_B) * square)
                gp_ref[step, at, :] = slope.astype(bf16)

    outs = [shape((count, width), bf16)] * 4
    outs += [shape((4, count, width), bf16), shape((4, width, width), bf16)]
    return call(kernel, "mlp_forward", scalars, list(arrays) + list(pieces), outs)


def gradient(matrix, order, name, scalars, lefts, rights):
    def kernel(scalars, arrays, outs):
        (place,) = scalars
        lefts, rights = arrays[:2], (arrays[2:4], arrays[4:6])
        for yr in range(2):
            total = dot_rows(lefts[0][...], rights[0][yr][...])
            total = total + dot_rows(lefts[1][...], rights[1][yr][...])
            matrix.store(place, [(0, total)], yr, order, outs[0])

    arrays = list(lefts) + list(rights[0]) + list(rights[1])
    (grad,) = call(kernel, name, scalars, arrays, matrix.grad_shapes(rights[0][0].shape[1]))
    return matrix.grad_result(grad, order)


def expanded_backward(scalars, arrays, pieces, fill):
    count, width = arrays[0].shape

    def kernel(scalars, arrays, outs):
        (place,) = scalars
        glow_ref, gp_ref = arrays[:2]
        ubg_ref, weight = outs[4:]
        fill(place, arrays[2:], weight)
        for step in range(4):
            total = jnp.zeros((1, width), f32)
            for at in row_blocks(count):
                grad = (dot(glow_ref[at, :], weight[step]) * up(gp_ref[step, at, :])).astype(bf16)
                outs[step][at, :] = grad
                total = total + jnp.sum(up(grad), axis=0, keepdims=True)
            ubg_ref[step] = total

    outs = [shape((count, width), bf16)] * 4
    outs += [shape((4, 1, width), f32), shape((4, width, width), bf16)]
    return call(kernel, "expanded_backward", scalars, list(arrays) + list(pieces), outs)


def middle_backward(arrays, parts):
    count, width = arrays[0].shape

    def kernel(scalars, arrays, outs):
        mid_ref, glow_ref, norm_ref, weight = arrays[:4]
        mg_ref, ml_ref, sums_ref = outs
        total = jnp.zeros((4, width), f32)
        for at in row_blocks(count):
            two = sum(dot_cols(part[at, :], weight[step]) for step, part in enumerate(arrays[4:]))
            normed, inverse = moments(mid_ref[at, :])
            out_grad = up(glow_ref[at, :])
            grad = out_grad + norm_back(two, normed, inverse, norm_ref[2:3, :])
            mg_ref[at, :] = grad
            ml_ref[at, :] = grad.astype(bf16)
            lines = [two * normed, two, grad, out_grad]
            total = total + join(*[jnp.sum(line, axis=0, keepdims=True) for line in lines])
        sums_ref[...] = total

    outs = [shape((count, width), f32), shape((count, width), bf16), shape((4, width), f32)]
    return call(kernel, "middle_backward", [], list(arrays) + list(parts), outs)


def block_out(arrays, parts):
    count, width = arrays[0].shape

    def kernel(scalars, arrays, outs):
        mid_ref, bias_ref, weight = arrays[:3]
        bias = bias_ref[bias_ref.shape[0] - 1 :, :]
        for at in row_blocks(count):
            total = sum(dot_cols(part[at, :], weight[step]) for step, part in enumerate(arrays[3:]))
            outs[0][at, :] = (mid_ref[at, :] + total + bias).astype(bf16)

    outs = [shape((count, width), bf16)]
    return call(kernel, "block_out", [], list(arrays) + list(parts), outs)[0]


def attention_backward(scalars, arrays):
    count, width = arrays[0].shape
    blocks = count // PAIR

    def kernel(scalars, arrays, outs, da, dq, dk, dv):
        (place,) = scalars
        ml_ref, q_ref, k_ref, v_ref, p_ref, weight = arrays
        lines_ref = outs[4]
        for yr in range(2):
            for at in row_blocks(count):
                ends = []
                for step in (yr, 2 + yr):
                    grad = dot(ml_ref[at, :], weight[step, :, 4 * PAIR :])
                    da[step, at, :] = grad[:, PAIR:].astype(bf16)
                    ends.append(grad[:, 0:PAIR])
                both = jnp.where(low_lanes(ends[0].shape), swap(ends[0]), ends[1])
                da[4 + yr, at, :] = both.astype(bf16)

        low = low_lanes((PAIR, PAIR))
        zero = jnp.zeros((PAIR, PAIR), bf16)
        scale = HEAD ** (-0.5)

        def stack(value):
            return join(jnp.where(low, value, zero), jnp.where(low, zero, value))

        def block(r, _):
            at = pl.ds(pl.multiple_of(r * PAIR, PAIR), PAIR)
            for pair in range(6):
                grad = stack(da[pair, at, :])
                low_probs = p_ref[pair, r]
                probs = up(low_probs)
                probs_grad = dot_cols(grad, v_ref[pair, at, :])
                shared = jnp.sum(probs * probs_grad, axis=1, keepdims=True)
                scores_grad = (probs * (probs_grad - shared)).astype(bf16)
                dv[pair, at, :] = dot_rows(low_probs, grad)
                both = dot(scores_grad, k_ref[pair, at, :])
                dq[pair, at, :] = jnp.where(low, both[0:PAIR], both[PAIR:]) * scale
                dk[pair, at, :] = dot_rows(scores_grad, stack(q_ref[pair, at, :])) * scale
            return 0

        lax.fori_loop(0, blocks, block, 0, unroll=2)
        low_all = low_lanes((count, PAIR))
        low_line = low_lanes((1, PAIR))

        def column_sum(value):
            return jnp.sum(up(value.astype(bf16)), axis=0, keepdims=True)

        for step in range(4):
            pc, yr = step // 2, step % 2
            pair = 4 + yr
            sums = []
            for value in (dq, dv):
                third = column_sum(value[pair])
                third = swap(third) if pc else third
                sums += [column_sum(value[step]), jnp.where(low_line, third, 0.0)]
            sums.append(jnp.zeros((1, width - 4 * PAIR), f32))
            lines_ref[pl.ds(block_of(place, step), 1), :] = jnp.concatenate(sums, axis=1)
            if pc:
                tail3 = jnp.where(low_all, swap(dq[pair]), dk[pair])
                tail4 = jnp.where(low_all, swap(dv[pair]), 0.0)
            else:
                tail3 = jnp.where(low_all, dq[pair], swap(dk[pair]))
                tail4 = jnp.where(low_all, dv[pair], 0.0)
            for i, part in enumerate((dq[step], dk[step], dv[step], tail3, tail4)):
                outs[step][:, i * PAIR : (i + 1) * PAIR] = part.astype(bf16)

    outs = [shape((count, 5 * PAIR), bf16)] * 4 + [shape((4, width), f32)]
    heads = (6, count, PAIR)
    scratch = [pltpu.VMEM(heads, bf16)] + [pltpu.VMEM(heads, f32)] * 3
    return call(kernel, "attention_backward", scalars, arrays, outs, scratch, micros=0)


def attention_gradient(matrix, order, scalars, lefts, rights, outer_lefts, outer_rights):
    def kernel(scalars, arrays, outs):
        (place,) = scalars
        n1, ml, outer = arrays[0:2], arrays[2:4], arrays[4:6]
        rights = (arrays[6:8], arrays[8:10])
        for yr in range(2):
            first = dot_rows(n1[0][...], rights[0][yr][...])
            first = first + dot_rows(n1[1][...], rights[1][yr][...])
            second = dot_rows(ml[0][...], outer[0][yr]) + dot_rows(ml[1][...], outer[1][yr])
            shared = first[:, 4 * PAIR :] + second[:, 0:PAIR]
            parts = [(0, first[:, 0 : 4 * PAIR]), (4 * PAIR, shared), (5 * PAIR, second[:, PAIR:])]
            matrix.store(place, parts, yr, order, outs[0])

    arrays = list(lefts) + list(outer_lefts) + list(outer_rights) + list(rights[0]) + list(rights[1])
    outs = matrix.grad_shapes(6 * PAIR)
    (grad,) = call(kernel, "attention_gradient", scalars, arrays, outs)
    return matrix.grad_result(grad, order)


def input_backward(scalars, arrays, parts):
    count, width = arrays[0].shape

    def kernel(scalars, arrays, outs):
        (place,) = scalars
        x_ref, mg_ref, norm_ref, weight, sums_ref, ubg_ref, heads_ref = arrays[:7]
        out_ref, lines_ref = outs
        total = jnp.zeros((2, width), f32)
        for at in row_blocks(count):
            one = sum(
                dot_cols(part[at, :], weight[step, :, 0 : 5 * PAIR])
                for step, part in enumerate(arrays[7:])
            )
            normed, inverse = moments(up(x_ref[at, :]))
            out_ref[at, :] = mg_ref[at, :] + norm_back(one, normed, inverse, norm_ref[0:1, :])
            lines = [jnp.sum(one * normed, axis=0, keepdims=True), jnp.sum(one, axis=0, keepdims=True)]
            total = total + join(*lines)
        lines_ref[0:8, :] = join(total, sums_ref[...], jnp.zeros((2, width), f32))
        for step in range(4):
            lines_ref[pl.ds(8 + block_of(place, step), 1), :] = ubg_ref[step]
        lines_ref[12:16, :] = heads_ref[...]

    outs = [shape((count, width), f32), shape((16, width), f32)]
    return call(kernel, "input_backward", scalars, list(arrays) + list(parts), outs)


def adam_step(weight, first, second, grad, rate, decay):
    first_new = beta_first * first + (1.0 - beta_first) * grad
    second_new = beta_second * second + (1.0 - beta_second) * grad * grad
    first_hat = first_new / (1.0 - beta_first**STEP)
    second_hat = second_new / (1.0 - beta_second**STEP)
    weight_new = weight - rate * (first_hat / (jnp.sqrt(second_hat) + adam_eps) + decay * weight)
    return (weight_new, first_new, second_new)


def pack_tiles(parts):
    q, k, v, o = ((part[:, :PAIR], part[:, PAIR:]) for part in parts)
    tail3 = jnp.concatenate([q[1], k[1]], axis=1)
    tail4 = jnp.concatenate([v[1], o[1]], axis=1)
    return q[0], k[0], v[0], tail3, tail4, o[0]


def own_columns(plan, place, value):
    width = value.shape[1]
    columns = width // math.prod(plan.dims)
    group = (place[0] * plan.dims[1] + place[1]) * 4 + rank_of(place)
    turn = lax.rem(width - group * columns, width)
    return pltpu.roll(value, turn, axis=1)[:, 0:columns]


def hold(plan, scalars, params, matrices):
    rows, cols = matrices[2][0].shape
    width = params[0].shape[1]
    columns = width // math.prod(plan.dims)

    def kernel(scalars, state, outs, small_ref):
        for t in range(3):
            parts = [state[t][i] for i in range(3)] + [state[3 + t][...]]
            for i, part in enumerate(pack_tiles(parts)):
                outs[0][t, :, i * PAIR : (i + 1) * PAIR] = part
            outs[0][3 + t] = state[6 + t][...]
            outs[0][6 + t] = state[9 + t][...]
        small_ref[0:8, :] = state[13][...]
        small_ref[8:12, :] = state[12][...]
        small_ref[12:16, :] = state[12][...]
        own = own_columns(plan, scalars[0], small_ref[...])
        outs[1][...] = own[8:12]
        outs[2][...] = own[0:8]

    outs = [shape((9, rows, cols), f32), shape((4, columns), f32), shape((8, columns), f32)]
    state = [value for group in matrices for value in group] + list(params)
    scratch = [pltpu.VMEM((16, width), f32)]
    return call(kernel, "hold", scalars, [], outs, scratch, 12, state, micros=7)


def total_gradients(plan, scalars, parts, lines):
    rows, cols = parts[0][0].shape[1:]
    width = lines[0].shape[2]
    devices = math.prod(plan.dims)
    columns = width // devices
    counts = [len(part) for part in parts]
    held = sum(counts)

    def kernel(scalars, arrays, outs, small_ref):
        at, squares = 0, jnp.zeros((1, 1), f32)

        def square(value):
            return jnp.sum(jnp.sum(value * value, axis=1, keepdims=True), axis=0, keepdims=True)

        for m, n in enumerate(counts):
            total = up(arrays[at][0])
            for i in range(1, n):
                total = total + up(arrays[at + i][0])
            outs[0][m] = total
            squares = squares + square(total)
            at += n
        sums = arrays[held][0]
        for ref in arrays[held + 1 :]:
            sums = sums + ref[0]
        size = width // 4
        small_ref[0:4, :] = sums[0:4]
        small_ref[4:8, :] = sums[8:12]
        for t in range(2):
            for mp in range(4):
                line = sums[12 + mp : 13 + mp, 2 * PAIR * t : 2 * PAIR * t + size]
                small_ref[8 + t : 9 + t, mp * size : (mp + 1) * size] = line
        small_ref[10:12, :] = sums[4:6]
        small_ref[12:16, :] = jnp.zeros((4, width), f32)
        own = own_columns(plan, scalars[0], small_ref[...])
        squares = squares + square(own)
        outs[1][...] = jnp.broadcast_to(squares[None], (devices, 1, 1))
        outs[2][...] = own[0:4]
        outs[3][...] = own[4:12]

    arrays = [part for group in parts for part in group] + list(lines)
    outs = [shape((3, rows, cols), f32), shape((devices, 1, 1), f32)]
    outs += [shape((n, columns), f32) for n in (4, 8)]
    scratch = [pltpu.VMEM((16, width), f32)]
    return call(kernel, "total_gradients", scalars, arrays, outs, scratch, 12)


def update(squares, grads, state, small, smalls, shapes):
    def kernel(scalars, arrays, outs):
        norm = jnp.sqrt(jnp.sum(arrays[0][...], axis=0))
        factor = jnp.minimum(1.0, clip_limit / (norm + 1e-06))
        outs[0][...] = norm
        grad_ref, state_ref = arrays[1:3]

        def step(weight, first, second, grad, rate, decay):
            grad = grad * factor
            new, first, second = adam_step(weight, first, second, grad, rate, decay)
            return [grad, new, first, second, new.astype(bf16)]

        for m in range(3):
            values = [state_ref[3 * m + t] for t in range(3)] + [grad_ref[m]]
            values = step(*values, matrix_rate, matrix_decay)
            for i, value in enumerate(values):
                if m:
                    outs[6 + 5 * m + i][...] = value
                    continue
                tiles = [value[:, t * PAIR : (t + 1) * PAIR] for t in range(6)]
                wide = [tiles[3], tiles[4]] if value.dtype == f32 else [up(t) for t in tiles[3:5]]
                tails = [part for t in wide for part in (t, swap(t))]
                for t in range(4):
                    ref = outs[1 + i] if t < 3 else outs[6 + i]
                    head = tiles[t] if t < 3 else tiles[5]
                    tail = tails[t][:, :HEAD].astype(value.dtype)
                    if t < 3:
                        ref[t, :, :PAIR] = head
                        ref[t, :, PAIR:] = tail
                    else:
                        ref[:, :PAIR] = head
                        ref[:, PAIR:] = tail
        for m in range(2):
            weight, first, second = (ref[...] for ref in arrays[5 + 3 * m : 8 + 3 * m])
            values = step(weight, first, second, arrays[3 + m][...], small_rate, 0.0)
            for i in range(4):
                outs[21 + 4 * m + i][...] = values[i]

    arrays = [squares, grads, state] + list(small)
    outs = [shape((1, 1), f32)]
    for dims in shapes:
        outs += [shape(dims, f32)] * 4 + [shape(dims, bf16)]
    for group in smalls:
        arrays += list(group)
        outs += [shape(group[0].shape, f32)] * 4
    return call(kernel, "update", [], arrays, outs)


def body(
    plan,
    block_input,
    cotangent,
    lengths,
    attn_input,
    attn_input_first,
    attn_input_second,
    attn_output,
    attn_output_first,
    attn_output_second,
    mlp_up,
    mlp_up_first,
    mlp_up_second,
    mlp_down,
    mlp_down_first,
    mlp_down_second,
    norm_params,
    norm_first,
    norm_second,
    bias_params,
    bias_first,
    bias_second,
):
    width = norm_params.shape[1]
    place = jnp.stack([lax.axis_index(axis) for axis in AXES]).astype(jnp.int32)
    matrix = Matrix(plan, place, width, attn_input.shape[0])
    send, send_z = plan.send, plan.send_z
    az, za = plan.order_az, plan.order_za
    low_bits, high_bits = plan.zbits[:2], plan.zbits[2:]
    def turned(value):
        return value.transpose(1, 0, 2)

    attn = pack_attention(turned(attn_input), attn_output)
    attn_z = [send_z(attn, mask) for mask in (1, 2, 3)]
    above, down = pack_mlp(mlp_up, mlp_down)
    above_z = send_z(above, 1)
    down_a = send(down, plan.a)
    n1, grad_low, head_bias = prepare(
        [place, lengths], [block_input, cotangent, norm_params, bias_params]
    )
    attn, *attn_z, above, above_z, down, down_a, n1, grad_low, head_bias = sync(
        attn, *attn_z, above, above_z, down, down_a, n1, grad_low, head_bias
    )

    attn, above, down = joined(
        "join_one", matrix, [attn, *attn_z], [above, above_z], [down, down_a]
    )
    attn = plan.spread(attn, high_bits)
    attn_a, attn_b = send(attn, plan.a), send(attn, plan.b)
    above_z = send_z(above, 2)
    attn_c = [send(attn, plan.core)]
    (above,) = joined("join_two", matrix, [above, above_z], micros=5)
    above = plan.spread(above, high_bits)
    above_a = send(above, plan.a)
    attn, attn_a, attn_b, above, down, *attn_c = sync(
        attn, attn_a, attn_b, above, down, *attn_c
    )

    def blocks(planes, order, *fixed):
        return [
            (array, plan.slots(pc, order, **what))
            for pc, arrays in enumerate(planes)
            for array, what in zip(arrays, fixed)
        ]

    corners = [dict(br=0, ar=0), dict(br=0, ar=1), dict(br=1, ar=0), dict(br=1, ar=1)]
    attn_ab = send(attn_a, plan.b)
    down_z = send_z(down, 2)
    attn_c += [send(attn_a, plan.core), send(attn_b, plan.core)]
    attn_ab, above, above_a, down, down_z, *attn_c[1:] = sync(
        attn_ab, above, above_a, down, down_z, *attn_c[1:]
    )

    (down,) = joined("join_three", matrix, [down, down_z])
    above_b = send(above, plan.b)
    above_ab = send(above_a, plan.b)
    down_z = send_z(down, 1)
    above_c = [send(piece, plan.core) for piece in (above, above_a)]
    attn_c.append(send(attn_ab, plan.core))
    pieces = blocks([[attn, attn_a, attn_b, attn_ab], attn_c], plan.plain, *corners)
    pieces, fill = matrix.weight_args(pieces)
    q, k, v, weight_attn = project([place], [n1, head_bias], pieces, fill)
    probs, att_own, att_other, middle, n2 = attend(
        [place, lengths], [block_input, norm_params, bias_params, q, k, v, weight_attn]
    )
    above, above_a, above_b, above_ab, down, down_z, att_other, n2, *above_c = sync(
        above, above_a, above_b, above_ab, down, down_z, att_other, n2, *above_c
    )

    (down,) = joined("join_four", matrix, [down, down_z])
    down = plan.spread(down, high_bits)
    down_b = send(down, plan.b)
    above_c += [send(piece, plan.core) for piece in (above_b, above_ab)]
    pieces = blocks([[above, above_a, above_b, above_ab], above_c], plan.plain, *corners)
    pieces, fill = matrix.weight_args(pieces)
    *hidden, slope, weight_up = mlp_forward([place], [n2, bias_params], pieces, fill)
    grad_low_c = send(grad_low, plan.core)
    hidden_c = [send(part, plan.core) for part in hidden[2:]]

    down_g = gradient(
        matrix, za, "down_gradient", [place], [grad_low, grad_low_c], [hidden[:2], hidden_c]
    )
    down_b, down_g, n2, att_other = sync(down_b, down_g, n2, att_other)

    n2_c = send(n2, plan.core)
    down_c = [send(down, plan.core), send(down_b, plan.core)]
    pieces = blocks([[down, down_b], down_c], za, dict(br=0), dict(br=1))
    pieces, fill = matrix.weight_args(pieces)
    half = down_g.shape[0] // 2
    down_gb = send(down_g[half:], plan.b)
    *grads, up_bias_grad, weight_down = expanded_backward(
        [place], [grad_low, slope], pieces, fill
    )
    grads_c = [send(part, plan.core) for part in grads[2:]]
    middle_grad, middle_low, sums_two = middle_backward(
        [middle, grad_low, norm_params, weight_up], grads
    )
    up_g = gradient(matrix, az, "up_gradient", [place], [n2, n2_c], [grads[:2], grads_c])
    n1_c, att_c = send(n1, plan.core), send(att_other, plan.core)
    up_g, middle_low, n1_c, att_c = sync(up_g, middle_low, n1_c, att_c)

    up_gb = send(up_g[half:], plan.b)
    terms = [down_g, down_gb]
    if high_bits:
        terms = [plan.fold(up(down_g[:half]) + up(down_gb), high_bits)]
    down_s, down_0 = added(
        "add_one",
        matrix,
        (4, f32, [(part, 0) for part in terms]),
        (4, bf16, [(part, 4) for part in terms]),
    )
    down_s, down_0, middle_low = sync(down_s, down_0, middle_low)

    down_z = send_z(down_0, 1)
    middle_low_c = send(middle_low, plan.core)
    *joint, head_lines = attention_backward(
        [place], [middle_low, q, k, v, probs, weight_attn]
    )
    joint_c = [send(part, plan.core) for part in joint[2:]]
    down_s, down_0, down_1 = added(
        "add_down",
        matrix,
        (2, f32, [(down_s, 0), (down_z, 0)]),
        (1, bf16, [(down_s, 2), (down_z, 2)]),
        (1, bf16, [(down_s, 3), (down_z, 3)]),
        micros=2,
    )
    middle_low_c, up_gb, down_s, down_0, down_1, *rest = sync(
        middle_low_c, up_gb, down_s, down_0, down_1, *joint, *joint_c
    )
    joint, joint_c = rest[:4], rest[4:]

    fourth = half // 2
    (up_0,) = added("add_two", matrix, (fourth, bf16, [(up_g, fourth), (up_gb, fourth)]))
    up_ga = send(up_0, plan.a)
    attn_g = attention_gradient(
        matrix, az, [place], [n1, n1_c], [joint[:2], joint_c],
        [middle_low, middle_low_c], [att_own, att_c],
    )
    attn_gb = send(attn_g[half:], plan.b)
    down_z0, down_z1 = send_z(down_0, 2), send_z(down_1, 2)
    input_grad, lines = input_backward(
        [place],
        [block_input, middle_grad, norm_params, weight_attn, sums_two, up_bias_grad, head_lines],
        joint,
    )
    lines = lines[None]
    up_ga, down_z0, lines = sync(up_ga, down_z0, lines)
    terms = [up_g, up_gb, up_ga]
    if high_bits:
        terms = [plan.fold(sum(up(part[:fourth]) for part in terms), high_bits)]
    up_s, up_0 = added(
        "add_three",
        matrix,
        (2, f32, [(part, 0) for part in terms]),
        (2, bf16, [(part, 2) for part in terms]),
    )
    up_z = send_z(up_0, 1)
    lines_a = send(lines, plan.a)
    (lines,) = added("add_lines", matrix, (1, f32, [(lines, 0), (lines_a, 0)]))
    lines_z = send_z(lines, 1)
    matrices = (
        (turned(attn_input), turned(attn_input_first), turned(attn_input_second)),
        (attn_output, attn_output_first, attn_output_second),
        (mlp_up, mlp_up_first, mlp_up_second),
        (mlp_down, mlp_down_first, mlp_down_second),
    )
    up_z, lines, norms = sync(up_z, lines, norm_params)
    state, own_norm, own_bias = hold(plan, [place], [norms, bias_params], matrices)
    attn_gb, down_z1, up_z, lines_z, state, input_grad = sync(
        attn_gb, down_z1, up_z, lines_z, state, input_grad
    )

    attn_0, down_s, down_0, up_s, up_0, lines = added(
        "add_four",
        matrix,
        (fourth, bf16, [(attn_g, fourth), (attn_gb, fourth)]),
        (1, f32, [(down_s, 0), (down_z0, 0)]),
        (1, bf16, [(down_s, 1), (down_z1, 0)]),
        (1, f32, [(up_s, 0), (up_z, 0)]),
        (1, bf16, [(up_s, 1), (up_z, 1)]),
        (1, f32, [(lines, 0), (lines_z, 0)]),
    )
    attn_ga = send(attn_0, plan.a)
    up_z = send_z(up_0, 2)
    lines_z = send_z(lines, 2)
    for bit in high_bits:
        lines = lines + lines_z
        lines_z = send_z(lines, bit)
    block_output = block_out([middle, bias_params, weight_down], hidden)
    attn_ga, up_z, lines_z, down_0, block_output = sync(
        attn_ga, up_z, lines_z, down_0, block_output
    )

    terms = [attn_g, attn_gb, attn_ga]
    if high_bits:
        terms = [plan.fold(sum(up(part[:fourth]) for part in terms), high_bits)]
    attn_s, *attn_0, lines = added(
        "add_five",
        matrix,
        (1, f32, [(part, 0) for part in terms]),
        (1, bf16, [(part, 1) for part in terms]),
        (1, bf16, [(part, 2) for part in terms]),
        (1, bf16, [(part, 3) for part in terms]),
        (1, f32, [(lines, 0), (lines_z, 0)]),
    )
    attn_z = [send_z(part, mask) for part, mask in zip(attn_0, (2, 1, 3))]
    down_ga = send(down_0, plan.a)
    rest = [send(lines, perm) for perm in (plan.b, plan.core, plan.cross)]
    state, down_ga, *rest = sync(state, down_ga, *rest, *attn_z)
    rest, attn_z = rest[:3], rest[3:]

    sums, squares, norm_sum, bias_sum = total_gradients(
        plan, [place], [[attn_s, *attn_z], [up_s, up_z], [down_s, down_ga]], [lines, *rest]
    )
    squares = lax.all_to_all(squares, AXES, 0, 0, tiled=True)
    grad_norm, *results = update(
        squares,
        sums,
        state,
        [norm_sum, bias_sum],
        ((own_norm, norm_first, norm_second), (own_bias, bias_first, bias_second)),
        [group[0].shape for group in matrices],
    )
    results[:5] = [turned(value) for value in results[:5]]
    return (block_output, input_grad, grad_norm[0, 0], *results)


def solution(mesh):
    dp, mp = mesh.shape["dp"], mesh.shape["mp"]
    dims = (dp // 2, 2, mp // 2, 2)
    fine = Mesh(np.asarray(mesh.devices).reshape(dims), AXES)
    plan = Plan(dims)
    d, m = ("z", "x"), ("y", "c")
    every = d + m
    rows = P(every, None)
    cube = P(d, None, m)
    flat = P(d, m)
    small = P(None, every)
    return jax.shard_map(
        functools.partial(body, plan),
        mesh=fine,
        in_specs=(rows, rows, P(d)) + (cube,) * 3 + (flat,) * 9 + (P(), small, small) * 2,
        out_specs=(rows, rows, P()) + (cube,) * 5 + (flat,) * 15 + (small,) * 8,
        check_vma=False,
    )
```
